32 devices in a mesh: tile: 8 (over z, y), chan: 4 (over x, core).
Axes of the slice: x: 2, y: 2, z: 4, core: 2. Of those that a mesh axis runs over, the one named last changes fastest.
Arguments:
- features: bfloat16 [128, 32768], P('chan', 'tile'), may hold values from -6 to 6
- conv1_weight: bfloat16 [9, 128, 128], P(None, 'chan'), may hold values from -0.1875 to 0.1875
- down_weight: bfloat16 [4, 128, 128], P(None, 'chan'), may hold values from -0.25 to 0.25
- conv2_weight: bfloat16 [9, 128, 128], P(None, 'chan'), may hold values from -0.1875 to 0.1875
- up_weight: bfloat16 [128, 128], P('chan'), may hold values from -0.5 to 0.5
- out_grad: bfloat16 [128, 32768], P('chan', 'tile'), may hold values from -6 to 6
- adjacency: int32 [8, 8, 2], replicated, may hold values from -1 to 7, as said below
Outputs:
- output: bfloat16 [128, 32768], P('chan', 'tile')
- grad_conv1: float32 [9, 128, 128], P(None, 'chan')
- grad_down: float32 [4, 128, 128], P(None, 'chan')
- grad_conv2: float32 [9, 128, 128], P(None, 'chan')
- grad_up: float32 [128, 128], P('chan')
The draws below stay inside these ranges and needn't reach their ends.
Inputs may be any that keep to these rules, and one draw needn't show every extreme that they name: adjacency[t, k, 0] is the tile beside side k of tile t (sides north, east, south, west, then corners north-east, south-east, south-west, north-west); it is -1 only at corners, where no single tile meets; adjacency[t, k, 1] is the number of counterclockwise quarter turns, 0 to 3, of that neighbour as seen from tile t.
All inputs are finite; a program needn't handle non-finite values.
Results may differ from the reference program's by a relative error of at most 0.0073.
Values may be sent and summed in bfloat16 or wider, within the bound.
No kernel may reach another device: no remote copies, remote signals or barrier semaphores. Data moves between devices by JAX's collectives and lax.ppermute only.
A program may use at most 128 MiB of HBM per device.

```python
import jax
import jax.numpy as jnp
import numpy as np
from jax import lax

C = 128
SIDE = 64
TILES = 8
CELLS = 32768


def face_step(face, row, col, side, grid, faces):
    if side == 0:
        if row > 0:
            return (face, row - 1, col, 0)
        return ((face - 1) % faces, grid - 1 - col, grid - 1, 3)
    if side == 1:
        if col < grid - 1:
            return (face, row, col + 1, 0)
        return ((face + 1) % faces, 0, grid - 1 - row, 1)
    if side == 2:
        if row < grid - 1:
            return (face, row + 1, col, 0)
        return ((face + 1) % faces, grid - 1 - col, 0, 3)
    if col > 0:
        return (face, row, col - 1, 0)
    return ((face - 1) % faces, grid - 1, grid - 1 - row, 1)


def corner_walk(face, row, col, first_side, second_side, grid, faces):
    face_one, row_one, col_one, turn_one = face_step(face, row, col, first_side, grid, faces)
    face_two, row_two, col_two, turn_two = face_step(face_one, row_one, col_one, (second_side + turn_one) % 4, grid, faces)
    return (face_two, row_two, col_two, (turn_one + turn_two) % 4)


def base_table(tile_total):
    grid = 1
    while 4 * (2 * grid) * (2 * grid) <= tile_total:
        grid = grid * 2
    faces = tile_total // (grid * grid)
    table = np.zeros((tile_total, 8, 2), np.int32)
    corner_sides = ((0, 1), (2, 1), (2, 3), (0, 3))
    for face in range(faces):
        for row in range(grid):
            for col in range(grid):
                tile_id = face * grid * grid + row * grid + col
                for side in range(4):
                    other_face, other_row, other_col, turn = face_step(face, row, col, side, grid, faces)
                    table[tile_id, side, 0] = other_face * grid * grid + other_row * grid + other_col
                    table[tile_id, side, 1] = turn
                for corner in range(4):
                    first_side, second_side = corner_sides[corner]
                    path_one = corner_walk(face, row, col, first_side, second_side, grid, faces)
                    path_two = corner_walk(face, row, col, second_side, first_side, grid, faces)
                    other_id = path_one[0] * grid * grid + path_one[1] * grid + path_one[2]
                    if path_one == path_two and other_id != tile_id:
                        table[tile_id, 4 + corner, 0] = other_id
                        table[tile_id, 4 + corner, 1] = path_one[3]
                    else:
                        table[tile_id, 4 + corner, 0] = -1
                        table[tile_id, 4 + corner, 1] = 0
    return table


def draw_adjacency(key, part):
    key = jax.random.fold_in(key, 7)
    table = jnp.asarray(base_table(TILES))
    renamed = jax.random.permutation(key, TILES).astype(jnp.int32)
    initial = jnp.argsort(renamed).astype(jnp.int32)
    moved = table[initial]
    partners = moved[:, :, 0]
    partners = jnp.where(partners >= 0, renamed[jnp.clip(partners, 0, TILES - 1)], -1)
    return jnp.stack([partners, moved[:, :, 1]], axis=2).astype(jnp.int32)


def steps_of(stream_key, dims, split, least, top_value):
    gain, own = 1.0, jax.random.fold_in(stream_key, 6)
    for dim, blocks in split:
        heights = jnp.exp(jax.random.uniform(jax.random.fold_in(own, dim), (blocks,), jnp.float32, least / len(split), top_value / len(split)))
        gain = gain * jnp.repeat(heights, dims[dim] // blocks).reshape([-1 if axis == dim else 1 for axis in range(len(dims))])
    return gain


def bell_draw(stream_key, shape, scale, limit, pieces=(), kind=jnp.bfloat16):
    factor_of = steps_of(stream_key, shape, pieces, -0.22, 0.18) if pieces else 1.0
    drawn = jax.random.normal(stream_key, shape, jnp.float32) * scale * factor_of
    return jnp.minimum(jnp.maximum(drawn, -limit), limit).astype(kind)


def setup_inputs(seed: int = 0) -> dict:
    key_of = jax.random.split(jax.random.key(seed), 8)
    return {
        "features": bell_draw(key_of[0], (C, CELLS), 1.0, 6.0, ((0, 4), (1, 8))),
        "conv1_weight": bell_draw(key_of[1], (9, C, C), (9 * C) ** -0.5, 0.1875, ((1, 4),)),
        "down_weight": bell_draw(key_of[2], (4, C, C), (4 * C) ** -0.5, 0.25, ((1, 4),)),
        "conv2_weight": bell_draw(key_of[3], (9, C, C), (9 * C) ** -0.5, 0.1875, ((1, 4),)),
        "up_weight": bell_draw(key_of[4], (C, C), C ** -0.5, 0.5, ((0, 4),)),
        "out_grad": bell_draw(key_of[5], (C, CELLS), 1.0, 6.0, ((0, 4), (1, 8))),
        "adjacency": draw_adjacency(jax.random.fold_in(key_of[7], 71), 0),
    }


side_turns = (0, 1, 2, 3, 0, 2, 2, 0)

def turned(values, quarter):
    return jnp.rot90(values, quarter, axes=(1, 2))

def build_rims(center, width):
    side_len = center.shape[1]
    return jnp.stack([center[:, side_len - width:, :], turned(center[:, :, :width], 1), turned(center[:, :width, :], 2), turned(center[:, :, side_len - width:], 3)])

def pad_block(center, picked, width):
    side_len = center.shape[1]
    north_rows = picked[0]
    east_cols = turned(picked[1], -1)
    south_rows = turned(picked[2], -2)
    west_cols = turned(picked[3], -3)
    north_east = picked[4][:, :, :width]
    south_east = turned(picked[5], -2)[:, :, :width]
    south_west = turned(picked[6], -2)[:, :, side_len - width:]
    north_west = picked[7][:, :, side_len - width:]
    top_band = jnp.concatenate([north_west, north_rows, north_east], axis=2)
    middle = jnp.concatenate([west_cols, center, east_cols], axis=2)
    low_band = jnp.concatenate([south_west, south_rows, south_east], axis=2)
    return jnp.concatenate([top_band, middle, low_band], axis=1)

def choose_rims(partners, rim_slots, current, incoming, first_row):
    row_count = incoming.shape[0]
    relative = partners - first_row
    inside = (relative >= 0) & (relative < row_count)
    clipped = jnp.clip(relative, 0, row_count - 1)
    selected = incoming[clipped, rim_slots]
    return jnp.where(inside[:, None, None, None], selected, current)

def conv_taps(weights, padded, dilation, rows, cols):
    summed = jnp.zeros((weights.shape[1], rows * cols), jnp.float32)
    for row_tap in range(3):
        for col_tap in range(3):
            window = padded[:, row_tap * dilation:row_tap * dilation + rows, col_tap * dilation:col_tap * dilation + cols].reshape(padded.shape[0], rows * cols)
            summed = summed + jnp.dot(weights[3 * row_tap + col_tap], window, preferred_element_type=jnp.float32)
    return summed

def conv_grads(cotangent, padded, dilation, rows, cols):
    result = []
    for row_tap in range(3):
        for col_tap in range(3):
            window = padded[:, row_tap * dilation:row_tap * dilation + rows, col_tap * dilation:col_tap * dilation + cols].reshape(padded.shape[0], rows * cols)
            result.append(lax.dot_general(cotangent, window, (((1,), (1,)), ((), ())), preferred_element_type=jnp.float32))
    return jnp.stack(result)

def conv_back_terms(weight_cols, cotangent, dilation, rows, cols):
    summed = jnp.zeros((weight_cols.shape[2], rows + 2 * dilation, cols + 2 * dilation), jnp.float32)
    for row_tap in range(3):
        for col_tap in range(3):
            term = lax.dot_general(weight_cols[3 * row_tap + col_tap], cotangent, (((0,), (0,)), ((), ())), preferred_element_type=jnp.float32).reshape(weight_cols.shape[2], rows, cols)
            summed = summed + jnp.pad(term, ((0, 0), (row_tap * dilation, 2 * dilation - row_tap * dilation), (col_tap * dilation, 2 * dilation - col_tap * dilation)))
    return summed

def quarter_parts(values, rows, cols):
    blocks = values.reshape(values.shape[0], rows, 2, cols, 2)
    return [blocks[:, :, row_tap, :, col_tap].reshape(values.shape[0], rows * cols) for row_tap in range(2) for col_tap in range(2)]

def down_conv(weights, values, rows, cols):
    parts_list = quarter_parts(values, rows, cols)
    summed = jnp.dot(weights[0], parts_list[0], preferred_element_type=jnp.float32)
    for quarter in range(1, 4):
        summed = summed + jnp.dot(weights[quarter], parts_list[quarter], preferred_element_type=jnp.float32)
    return summed

def down_grads(cotangent, values, rows, cols):
    parts_list = quarter_parts(values, rows, cols)
    return jnp.stack([lax.dot_general(cotangent, piece_part, (((1,), (1,)), ((), ())), preferred_element_type=jnp.float32) for piece_part in parts_list])

def down_back(weight_cols, cotangent, rows, cols):
    stacked = jnp.stack([lax.dot_general(weight_cols[quarter], cotangent, (((0,), (0,)), ((), ())), preferred_element_type=jnp.float32) for quarter in range(4)])
    chans = weight_cols.shape[2]
    return stacked.reshape(2, 2, chans, rows, cols).transpose(2, 3, 0, 4, 1).reshape(chans, 4 * rows * cols)

def up_copy(values, rows, cols):
    chans = values.shape[0]
    grown = jnp.broadcast_to(values.reshape(chans, rows, 1, cols, 1), (chans, rows, 2, cols, 2))
    return grown.reshape(chans, 4 * rows * cols)

def pool_cells(cotangent, rows, cols):
    chans = cotangent.shape[0]
    return cotangent.astype(jnp.float32).reshape(chans, rows, 2, cols, 2).sum(axis=(2, 4)).reshape(chans, rows * cols)

def gelu_back(preact, cotangent):
    return jax.vjp(jax.nn.gelu, preact)[1](cotangent)[0]

def pad_transpose(cotangent, chans, half_len):
    zero_center = jnp.zeros((chans, half_len, half_len), jnp.float32)
    zero_picked = jnp.zeros((8, chans, 1, half_len), jnp.float32)

    def padding(center, picked):
        return pad_block(center, picked, 1)
    _, pullback = jax.vjp(padding, zero_center, zero_picked)
    return pullback(cotangent)

def rims_transpose(returned, chans, half_len):
    zero_center = jnp.zeros((chans, half_len, half_len), jnp.float32)

    def rimming(center):
        return build_rims(center, 1)
    _, pullback = jax.vjp(rimming, zero_center)
    return pullback(returned)[0]

def reference(features, conv1_weight, down_weight, conv2_weight, up_weight, out_grad, adjacency):
    side_len = SIDE
    half_len = side_len // 2
    tiles_x = features.reshape(C, TILES, side_len, side_len).transpose(1, 0, 2, 3)
    tiles_g = out_grad.reshape(C, TILES, side_len * side_len).transpose(1, 0, 2)
    partners = adjacency[:, :, 0]
    rim_slots = (adjacency[:, :, 1] + jnp.array(side_turns, jnp.int32)) % 4

    def fine_rims_of(center):
        return build_rims(center, 2)
    fine_rims = jax.vmap(fine_rims_of)(tiles_x)

    def padded_fine(tile_index):
        empty = jnp.zeros((8,) + fine_rims.shape[2:], fine_rims.dtype)
        picked = choose_rims(partners[tile_index], rim_slots[tile_index], empty, fine_rims, 0)
        return pad_block(tiles_x[tile_index], picked, 2)

    def forward_fine(tile_index):
        fine_all = padded_fine(tile_index)
        pre_one = conv_taps(conv1_weight, fine_all, 2, side_len, side_len)
        act_one = jax.nn.gelu(pre_one).astype(jnp.bfloat16)
        pre_two = down_conv(down_weight, act_one, half_len, half_len)
        act_two = jax.nn.gelu(pre_two).astype(jnp.bfloat16)
        return (pre_one, act_one, pre_two, act_two)
    tile_ids = jnp.arange(TILES, dtype=jnp.int32)
    pre_one, act_one, pre_two, act_two = lax.map(forward_fine, tile_ids)

    def coarse_rims_of(center):
        return build_rims(center, 1)
    coarse_rims = jax.vmap(coarse_rims_of)(act_two.reshape(TILES, C, half_len, half_len))

    def coarse_step(carry, tile_index):
        grad_conv2, grad_up = carry
        center = act_two[tile_index].reshape(C, half_len, half_len)
        empty = jnp.zeros((8,) + coarse_rims.shape[2:], coarse_rims.dtype)
        picked = choose_rims(partners[tile_index], rim_slots[tile_index], empty, coarse_rims, 0)
        coarse_all = pad_block(center, picked, 1)
        pre_three = conv_taps(conv2_weight, coarse_all, 1, half_len, half_len)
        coarse = jax.nn.gelu(pre_three).astype(jnp.bfloat16)
        lifted = jnp.dot(up_weight, coarse, preferred_element_type=jnp.float32)
        output = (act_one[tile_index].astype(jnp.float32) + up_copy(lifted, half_len, half_len)).astype(jnp.bfloat16)
        pooled = pool_cells(tiles_g[tile_index], half_len, half_len).astype(jnp.bfloat16)
        grad_up = grad_up + lax.dot_general(pooled, coarse, (((1,), (1,)), ((), ())), preferred_element_type=jnp.float32)
        back_up = lax.dot_general(up_weight, pooled, (((0,), (0,)), ((), ())), preferred_element_type=jnp.float32)
        grad_three = gelu_back(pre_three, back_up).astype(jnp.bfloat16)
        grad_conv2 = grad_conv2 + conv_grads(grad_three, coarse_all, 1, half_len, half_len)
        coarse_back = conv_back_terms(conv2_weight, grad_three, 1, half_len, half_len)
        grad_center, grad_picked = pad_transpose(coarse_back, C, half_len)
        return ((grad_conv2, grad_up), (output, grad_center, grad_picked))
    start_coarse = (jnp.zeros((9, C, C), jnp.float32), jnp.zeros((C, C), jnp.float32))
    (grad_conv2, grad_up), (outputs, grad_center, grad_picked) = lax.scan(coarse_step, start_coarse, tile_ids)
    has_partner = (partners >= 0).astype(jnp.float32)
    masked = (grad_picked * has_partner[:, :, None, None, None]).reshape(TILES * 8, C, 1, half_len)
    buffer = jnp.zeros((TILES, 4, C, 1, half_len), jnp.float32).at[jnp.clip(partners, 0, TILES - 1).reshape(-1), rim_slots.reshape(-1)].add(masked)

    def fine_step(carry, tile_index):
        grad_conv1, grad_down = carry
        grad_more = rims_transpose(buffer[tile_index], C, half_len)
        grad_act_two = (grad_center[tile_index] + grad_more).reshape(C, half_len * half_len)
        grad_two = gelu_back(pre_two[tile_index], grad_act_two).astype(jnp.bfloat16)
        grad_down = grad_down + down_grads(grad_two, act_one[tile_index], half_len, half_len)
        grad_act_one = tiles_g[tile_index].astype(jnp.float32) + down_back(down_weight, grad_two, half_len, half_len)
        grad_one = gelu_back(pre_one[tile_index], grad_act_one).astype(jnp.bfloat16)
        grad_conv1 = grad_conv1 + conv_grads(grad_one, padded_fine(tile_index), 2, side_len, side_len)
        return ((grad_conv1, grad_down), 0)
    start_fine = (jnp.zeros((9, C, C), jnp.float32), jnp.zeros((4, C, C), jnp.float32))
    (grad_conv1, grad_down), _ = lax.scan(fine_step, start_fine, tile_ids)
    grad_scale = CELLS ** (-0.5)
    output = outputs.transpose(1, 0, 2).reshape(C, CELLS)
    return (output, grad_conv1 * grad_scale, grad_down * grad_scale, grad_conv2 * grad_scale, grad_up * grad_scale)
```

```python
from functools import partial

import jax
import jax.numpy as jnp
import numpy as np
from jax import lax
from jax.experimental import pallas as pl
from jax.experimental.pallas import tpu as pltpu
from jax.sharding import PartitionSpec as P

SIDE = 64
HALF = 32
CELLS = HALF * HALF
PADDED = 36 * HALF
BLOCK = 8 * SIDE
BF16 = jnp.bfloat16
F32 = jnp.float32
NT = (((1,), (1,)), ((), ()))
ROOT = float(np.sqrt(2.0 / np.pi))
CUBE = 0.044715
side_turns = (0, 1, 2, 3, 0, 2, 2, 0)


def mm(left, right):
    return jnp.dot(left, right, preferred_element_type=F32)


def mm_nt(left, right):
    return lax.dot_general(left, right, NT, preferred_element_type=F32)


def gelu(v):
    return 0.5 * v * (1.0 + jnp.tanh(ROOT * (v + CUBE * (v * v * v))))


def gelu_slope(v):
    square = v * v
    t = jnp.tanh(ROOT * (v + CUBE * (square * v)))
    return 0.5 * (1.0 + t) + (0.5 * ROOT) * v * (1.0 - t * t) * (1.0 + 3.0 * CUBE * square)


def gelu_and_slope(v):
    square = v * v
    t = jnp.tanh(ROOT * (v + CUBE * (square * v)))
    both = 0.5 * (1.0 + t)
    return v * both, both + (0.5 * ROOT) * v * (1.0 - t * t) * (1.0 + 3.0 * CUBE * square)


def iota(shape, dim):
    return lax.broadcasted_iota(jnp.int32, shape, dim)


def one_hot(mask):
    return jnp.where(mask, 1.0, 0.0).astype(BF16)


def flip32(rows):
    anti = one_hot(iota((HALF, HALF), 0) + iota((HALF, HALF), 1) == HALF - 1)
    return mm(anti, rows)


def own_rows(me, own, chans):
    return one_hot(iota((own, chans), 0) + me * own == iota((own, chans), 1))


def side_of(codes_ref, tile, side):
    code = codes_ref[tile, side]
    return jnp.maximum(code, 0) // 4, code & 3, code >= 0


def is_beside(codes_ref, tile, side, partner):
    code = codes_ref[tile, side]
    return (code >= partner * 4) & (code < partner * 4 + 4)


def rows_of(slot, base, own):
    return pl.multiple_of((slot ^ base) * own, own)


def place_conv(packs, base, start, dst_ref):
    own = packs[0].shape[1]
    for slot, pack in enumerate(packs):
        row = rows_of(slot, base, own)
        for a in range(3):
            for b in range(3):
                dst_ref[pl.ds(a * 128 + row, own), b * 128 : (b + 1) * 128] = pack[start + 3 * a + b]


def spread_columns(dst, left, right, center, north, south, west, east, corners):
    rows = 34 * HALF
    middle = jnp.concatenate([north, center, south], axis=0)
    north_east, south_east, south_west, north_west = corners
    left[...] = pltpu.roll(middle, 1, 0)
    right[...] = pltpu.roll(middle, rows - 1, 0)
    left[pl.ds(HALF, HALF, stride=HALF), :] = west
    left[0:1, :] = north_west
    left[33 * HALF : 33 * HALF + 1, :] = south_west
    right[pl.ds(2 * HALF - 1, HALF, stride=HALF), :] = east
    right[HALF - 1 : HALF, :] = north_east
    right[rows - 1 : rows, :] = south_east
    dst[0:rows, 0:128] = left[...].astype(BF16)
    dst[0:rows, 128:256] = middle.astype(BF16)
    dst[0:rows, 256:384] = right[...].astype(BF16)
    dst[rows:PADDED, :] = jnp.zeros((PADDED - rows, 384), BF16)


def fetch(pairs, sems):
    started = [
        pltpu.make_async_copy(source, target, sems.at[index])
        for index, (source, target) in enumerate(pairs)
    ]
    for copy in started:
        copy.start()
    return started


def stacked(ref):
    return jnp.concatenate([ref[:, jb * BLOCK : (jb + 1) * BLOCK] for jb in range(8)], axis=0)


def sort_kernel(
    f_hbm, g_hbm, w1_hbm, wd_hbm, w2_hbm, up_hbm, m_hbm, pack_ref, rims_ref, sorted_ref, pack2_ref, f_ref, g_ref, m_ref, sems
):
    count = f_ref.shape[0]
    started = fetch(
        [
            (f_hbm, f_ref),
            (m_hbm, m_ref),
            (g_hbm, g_ref),
            (w1_hbm, pack_ref.at[32:41]),
            (wd_hbm, pack_ref.at[41:45]),
            (w2_hbm, pack2_ref.at[8:17]),
            (up_hbm, pack2_ref.at[17]),
        ],
        sems,
    )
    lane = iota((count, BLOCK), 1)
    turn, slot = lane // 128, lane % HALF
    wanted = jnp.where(
        turn == 0, 7, jnp.where(turn == 1, slot // 4, jnp.where(turn == 2, 0, (HALF - 1 - slot) // 4))
    )
    spot, cell = iota((BLOCK, 128), 0), iota((BLOCK, 128), 1)
    pooling = one_hot((spot // 128 == cell // HALF) & (spot % HALF == cell % HALF))

    def moved(ref):
        stack = jnp.concatenate([ref[:, jb * BLOCK : (jb + 1) * BLOCK] for jb in range(8)], axis=0)
        both = mm(stack, m_ref[...])
        parts = [both[jb * count : (jb + 1) * count] for jb in range(8)]
        rims = jnp.zeros((count, BLOCK), F32)
        for jb in range(8):
            rims = rims + jnp.where(wanted == jb, parts[jb][:, BLOCK:], 0.0)
        return [[part[:, ph * 128 : (ph + 1) * 128] for ph in range(4)] for part in parts], rims.astype(BF16)

    started[0].wait()
    started[1].wait()
    pieces, rims = moved(f_ref)
    for turn_index in range(4):
        rims_ref[0, turn_index] = rims[:, turn_index * 128 : (turn_index + 1) * 128]
    for jb in range(8):
        for ph in range(4):
            pack_ref[ph * 8 + jb] = pieces[jb][ph].astype(BF16)
    started[2].wait()
    pieces, rims = moved(g_ref)
    rims_ref[0, 4] = mm(rims, pooling).astype(BF16)
    for jb in range(8):
        for ph in range(4):
            sorted_ref[:, ph * CELLS + jb * 128 : ph * CELLS + (jb + 1) * 128] = pieces[jb][ph].astype(BF16)
        pack2_ref[jb] = ((pieces[jb][0] + pieces[jb][1]) + (pieces[jb][2] + pieces[jb][3])).astype(BF16)
    for copy in started[3:]:
        copy.wait()


def hold(refs, spots, core, put):
    for ref, slots in zip(refs, spots):
        for index, (even, odd) in enumerate(slots):
            slot = even if even == odd else jnp.where(core == 0, even, odd)
            put(slot, ref, index)


def pick_kernel(spots, codes_ref, where_ref, *refs):
    *rims, out_ref, held = refs
    tile, base, core = where_ref[0], where_ref[2], where_ref[1] & 1

    def put(slot, ref, index):
        held[slot] = ref[index]

    hold(rims, spots, core, put)
    lane = iota(out_ref.shape[1:], 1) % HALF
    corners = jnp.zeros(lane.shape, F32)
    for side in range(8):
        partner, turn, there = side_of(codes_ref, tile, side)
        picked = jnp.where(there, held[partner ^ base, turn].astype(F32), 0.0)
        if side < 4:
            out_ref[side] = picked.astype(BF16)
        else:
            shift, spot = ((0, 0), (0, HALF - 1), (1, 1), (127, HALF - 2))[side - 4]
            moved = pltpu.roll(picked, shift, 1) if shift else picked
            corners = corners + jnp.where(lane == spot, moved, 0.0)
    out_ref[4] = corners.astype(BF16)
    for other in range(out_ref.shape[0] - 5):
        out_ref[5 + other] = held[other ^ base, 4]


def stage_kernel(pack_ref, rims_ref, far_ref, near_ref, pair_ref):
    near_ref[...] = pack_ref[...]
    pair_ref[0:1] = rims_ref[...]
    pair_ref[1:2] = far_ref[...]


def fine_center_kernel(nc, where_ref, *refs):
    packs, refs = refs[:nc], refs[nc:]
    x3_ref, z1_ref, w1t, wdt, w1s, wds, f_all = refs
    base = where_ref[3]
    own = packs[0].shape[1]
    for slot, pack in enumerate(packs):
        row = rows_of(slot, base, own)
        for block in range(32):
            f_all[pl.ds(row, own), block * 128 : (block + 1) * 128] = pack[block]
        for a in range(3):
            for b in range(3):
                w1s[pl.ds(a * 128 + row, own), b * 128 : (b + 1) * 128] = pack[32 + 3 * a + b]
        for ph in range(4):
            wds[pl.ds(row, own), ph * 128 : (ph + 1) * 128] = pack[41 + ph]
    for a in range(3):
        w1t[a * 384 : (a + 1) * 384, :] = jnp.transpose(w1s[a * 128 : (a + 1) * 128, :])
    wdt[...] = jnp.transpose(wds[...])
    column = iota((CELLS, 128), 0) % HALF
    for ph in range(4):
        center = jnp.transpose(f_all[:, ph * CELLS : (ph + 1) * CELLS]).astype(F32)
        left = jnp.where(column == 0, 0.0, pltpu.roll(center, 1, 0))
        right = jnp.where(column == HALF - 1, 0.0, pltpu.roll(center, CELLS - 1, 0))
        x3_ref[ph, 0:HALF, :] = jnp.zeros((HALF, 384), BF16)
        x3_ref[ph, HALF : HALF + CELLS, 0:128] = left.astype(BF16)
        x3_ref[ph, HALF : HALF + CELLS, 128:256] = center.astype(BF16)
        x3_ref[ph, HALF : HALF + CELLS, 256:384] = right.astype(BF16)
        x3_ref[ph, HALF + CELLS : PADDED, :] = jnp.zeros((PADDED - HALF - CELLS, 384), BF16)
        for start in range(0, CELLS, 256):
            window = jnp.concatenate(
                [x3_ref[ph, start + a * HALF : start + a * HALF + 256, :] for a in range(3)], axis=1
            )
            z1_ref[ph, start : start + 256, :] = mm(window, w1t[...])


def ring_pieces(ring, ph):
    a, b = ph // 2, ph % 2
    near, far = ph * HALF, ((1 - a) * 2 + (1 - b)) * HALF
    east, west = ((1 - b) * 2 + a) * HALF, (b * 2 + (1 - a)) * HALF
    return (
        ring[0, near : near + HALF],
        ring[1, east : east + HALF],
        ring[2, far : far + HALF],
        ring[3, west : west + HALF],
        (
            ring[4, near : near + 1],
            ring[4, far + HALF - 1 : far + HALF],
            ring[4, far + 1 : far + 2],
            ring[4, near + HALF - 2 : near + HALF - 1],
        ),
    )


def windows_of(row, first, final):
    place = iota((HALF, 128), 0)
    return jnp.concatenate(
        [
            jnp.where(place == 0, first, pltpu.roll(row, 1, 0)),
            row,
            jnp.where(place == HALF - 1, final, pltpu.roll(row, HALF - 1, 0)),
        ],
        axis=1,
    ).astype(BF16)


def fine_ring_kernel(nc, where_ref, z1_in, w1t, wdt, *refs):
    rings, refs = refs[:nc], refs[nc:]
    act_ref, slope2_ref, act2_ref, rims_ref, half_ref, ring, ring_all, z1, wide = refs
    base = where_ref[3]
    own = rings[0].shape[1]
    for slot in range(nc):
        row = rows_of(slot, base, own)
        for side in range(5):
            ring_all[side, pl.ds(row, own), :] = rings[slot][side]
    row, col = iota((128, 128), 0), iota((128, 128), 1)
    same = one_hot(row == col)
    turned = one_hot((row // HALF == col // HALF) & (row % HALF + col % HALF == HALF - 1))
    for side in range(5):
        ring[side] = mm_nt(turned if side in (2, 3) else same, ring_all[side])
    z1[...] = z1_in[...]
    pieces = [ring_pieces(ring, ph) for ph in range(4)]

    def owed(rows, weights):
        return mm(jnp.concatenate(rows, axis=0), weights)

    def column(tap):
        return jnp.concatenate(
            [w1t[a * 384 + tap * 128 : a * 384 + (tap + 1) * 128, :] for a in range(3)], axis=0
        )

    north = owed([windows_of(p[0], p[4][3], p[4][0]) for p in pieces], w1t[0:384, :])
    south = owed([windows_of(p[2], p[4][2], p[4][1]) for p in pieces], w1t[768:1152, :])
    west = owed([windows_of(p[3], 0.0, 0.0) for p in pieces], column(0))
    east = owed([windows_of(p[1], 0.0, 0.0) for p in pieces], column(2))
    first = pl.ds(0, HALF, stride=HALF)
    last = pl.ds(HALF - 1, HALF, stride=HALF)
    for ph in range(4):
        rows = slice(ph * HALF, (ph + 1) * HALF)
        z1[ph, 0:HALF, :] += north[rows]
        z1[ph, CELLS - HALF : CELLS, :] += south[rows]
        z1[ph, first, :] = z1[ph, first, :] + west[rows]
        z1[ph, last, :] = z1[ph, last, :] + east[rows]

    def chunk(index, carry):
        start = index * 256
        acts = []
        for ph in range(4):
            act = gelu(z1[ph, pl.ds(start, 256), :]).astype(BF16)
            act_ref[ph, pl.ds(start, 256), :] = act
            acts.append(act)
        z2 = mm(jnp.concatenate(acts, axis=1), wdt[...])
        value, slope = gelu_and_slope(z2)
        slope2_ref[pl.ds(start, 256), :] = slope
        act2 = value.astype(BF16)
        act2_ref[pl.ds(start, 256), :] = act2
        wide[pl.ds(start, 256), :] = act2.astype(F32)
        return carry

    lax.fori_loop(0, 4, chunk, 0)
    for deep in range(2):
        start = CELLS - (deep + 1) * HALF
        rims_ref[0, deep * 128 : deep * 128 + 32, :] = act2_ref[start : start + HALF, :]
        rims_ref[0, deep * 128 + 32 : deep * 128 + 64, :] = wide[
            pl.ds(deep, HALF, stride=HALF), :
        ].astype(BF16)
        rims_ref[0, deep * 128 + 64 : deep * 128 + 96, :] = flip32(
            act2_ref[deep * HALF : (deep + 1) * HALF, :]
        ).astype(BF16)
        rims_ref[0, deep * 128 + 96 : deep * 128 + 128, :] = flip32(
            wide[pl.ds(HALF - 1 - deep, HALF, stride=HALF), :].astype(BF16)
        ).astype(BF16)
    half_ref[0] = rims_ref[0, pl.ds(pl.multiple_of((where_ref[1] & 1) * 128, 128), 128), :]


def own_fine_kernel(w1_ref, ring, x3_in, act_ref, slope_ref, x3_ref):
    own = w1_ref.shape[1]
    row, col = iota((CELLS, HALF), 0), iota((CELLS, HALF), 1)
    at_first, at_last = one_hot(row == col * HALF), one_hot(row == col * HALF + HALF - 1)
    inner = slice(HALF, HALF + CELLS)
    stack = jnp.concatenate(
        [
            jnp.concatenate([w1_ref[3 * a + b] for b in range(3)], axis=1)
            for a in range(3)
        ],
        axis=0,
    )
    for ph in range(4):
        north, east, south, west, corners = ring_pieces(ring, ph)
        x3_ref[ph, inner, 128:256] = x3_in[ph, inner, 128:256]
        x3_ref[ph, 2 * HALF + CELLS : PADDED, :] = jnp.zeros((PADDED - 2 * HALF - CELLS, 384), BF16)
        x3_ref[ph, 0:HALF, :] = windows_of(north, corners[3], corners[0])
        x3_ref[ph, HALF + CELLS : 2 * HALF + CELLS, :] = windows_of(south, corners[2], corners[1])
        x3_ref[ph, inner, 0:128] = x3_in[ph, inner, 0:128] + mm(at_first, west.astype(BF16)).astype(BF16)
        x3_ref[ph, inner, 256:384] = x3_in[ph, inner, 256:384] + mm(at_last, east.astype(BF16)).astype(
            BF16
        )
        terms = mm_nt(stack, x3_ref[ph])
        total = terms[0:own, 0:CELLS]
        for a in range(1, 3):
            moved = pltpu.roll(terms[a * own : (a + 1) * own], PADDED - a * HALF, 1)
            total = total + moved[:, 0:CELLS]
        value, slope = gelu_and_slope(total)
        act_ref[:, ph * CELLS : (ph + 1) * CELLS] = value.astype(BF16)
        slope_ref[:, ph * CELLS : (ph + 1) * CELLS] = slope


def turned_tap(turn, a, b):
    return ((a, b), (b, 2 - a), (2 - a, 2 - b), (2 - b, a))[turn]


CORNER_ENDS = {4: 0, 5: HALF - 1, 6: 0, 7: HALF - 1}
LOW_LEFT = (4, 5, 6, 7)
LOW_RIGHT = (7, 4, 5, 6)


def is_owing(codes_ref, other, side, tile):
    owing = is_beside(codes_ref, other, side, tile)
    if side in (0, 2):
        owing = owing | is_beside(codes_ref, other, LOW_LEFT[side], tile)
        owing = owing | is_beside(codes_ref, other, LOW_RIGHT[side], tile)
    return owing


def strip_of(side, other, codes_ref, base, rims_all):
    turn = (side + 2) % 4

    def rim(partner, slot):
        return rims_all[partner ^ base, pl.ds(pl.multiple_of(slot * HALF, HALF), HALF), :]

    partner, slot, _ = side_of(codes_ref, other, side)
    left_partner, left_slot, _ = side_of(codes_ref, other, (side + 1) % 4)
    right_partner, right_slot, _ = side_of(codes_ref, other, (side + 3) % 4)
    ends = []
    for corner in (LOW_LEFT[side], LOW_RIGHT[side]):
        corner_partner, corner_slot, there = side_of(codes_ref, other, corner)
        spot = CORNER_ENDS[corner]
        row = rim(corner_partner, corner_slot).astype(F32)[spot : spot + 1]
        ends.append(jnp.where(there, row, 0.0))
    left, right = rim(left_partner, left_slot).astype(F32), rim(right_partner, right_slot).astype(F32)
    last = HALF - 1
    here = rims_all[other ^ base, turn * HALF : (turn + 1) * HALF, :].astype(F32)
    above = rims_all[other ^ base, 128 + turn * HALF : 128 + (turn + 1) * HALF, :].astype(F32)
    below = flip32(rim(partner, slot))
    place = iota((HALF, 128), 0)
    by_tap = {}
    for a, (row, first, final) in enumerate(
        (
            (above, left[1:2], right[last - 1 : last]),
            (here, left[0:1], right[last : last + 1]),
            (below, ends[0], ends[1]),
        )
    ):
        by_tap[turned_tap(turn, a, 0)] = jnp.where(place == 0, first, pltpu.roll(row, 1, 0))
        by_tap[turned_tap(turn, a, 1)] = row
        by_tap[turned_tap(turn, a, 2)] = jnp.where(place == last, final, pltpu.roll(row, last, 0))
    return jnp.concatenate([by_tap[a, b] for a in range(3) for b in range(3)], axis=1).astype(BF16)


def back_from(others, codes_ref, tile, base, rims_all, prims, w2s, w2t, ups, back):
    last = HALF - 1
    place = iota((HALF, 128), 0)
    z3 = mm(
        jnp.concatenate([strip_of(side, others[side], codes_ref, base, rims_all) for side in range(4)], axis=0),
        w2t[...],
    )
    pooled = []
    for side in range(4):
        turn = (side + 2) % 4
        select = one_hot(iota((HALF, 128), 0) + turn * HALF == iota((HALF, 128), 1))
        cells = prims[:, pl.ds(pl.multiple_of(others[side] * 128, 128), 128)]
        pooled.append(mm_nt(select, cells))
    g3 = gelu_slope(z3) * mm(jnp.concatenate(pooled, axis=0).astype(BF16), ups[...])
    row, col = iota((128, 128), 0), iota((128, 128), 1)
    turned = one_hot((row // HALF == col // HALF) & (row % HALF + col % HALF == HALF - 1))
    g3 = mm(turned, g3.astype(BF16)).astype(BF16)
    for side in range(4):
        other = others[side]
        owed = []
        for b in range(3):
            r, c = turned_tap((side + 2) % 4, 2, b)
            owed.append(
                mm(
                    g3[side * HALF : (side + 1) * HALF],
                    w2s[r * 128 : (r + 1) * 128, c * 128 : (c + 1) * 128],
                )
            )
        total = (
            jnp.where(place == 0, 0.0, pltpu.roll(owed[0], 1, 0))
            + owed[1]
            + jnp.where(place == last, 0.0, pltpu.roll(owed[2], last, 0))
        )
        _, slot, _ = side_of(codes_ref, other, side)
        counts = is_beside(codes_ref, other, side, tile) & (others[side + 4] == 1)
        back[pl.ds(pl.multiple_of(slot * HALF, HALF), HALF), :] += jnp.where(counts, total, 0.0)
        if side in (0, 2):
            for corner, line in (
                (LOW_LEFT[side], owed[0][last : last + 1]),
                (LOW_RIGHT[side], owed[2][0:1]),
            ):
                _, corner_slot, _ = side_of(codes_ref, other, corner)
                counts = is_beside(codes_ref, other, corner, tile) & (others[side + 4] == 1)

                @pl.when(counts)
                def _():
                    back[pl.ds(pl.multiple_of(corner_slot * HALF, HALF), HALF), :] += jnp.where(
                        place == CORNER_ENDS[corner], line, 0.0
                    )


def own_taps(grad_ref, start, grads, own):
    for a in range(3):
        for b in range(3):
            row = (start + 3 * a + b) * own
            grad_ref[row : row + own, :] = grads[
                a * own : (a + 1) * own, b * 128 : (b + 1) * 128
            ].astype(BF16)


def shifted_stack(values):
    wide = jnp.concatenate([values, jnp.zeros((values.shape[0], PADDED - CELLS), F32)], axis=1)
    return jnp.concatenate(
        [(pltpu.roll(wide, a * HALF, 1) if a else wide).astype(BF16) for a in range(3)], axis=0
    )


def level_kernel(
    nc,
    spots,
    codes_ref,
    where_ref,
    act2_ref,
    slope2_ref,
    act_ref,
    wdt_ref,
    own_ref,
    slope1_ref,
    og_ref,
    x3_ref,
    m_ref,
    *refs,
):
    packs, mores, refs = refs[:nc], refs[nc : 2 * nc], refs[2 * nc :]
    *rims, out_ref, grad_ref, w2s, w2t, ups, pooled_all, prims, rims_all, left, right, g3pad, sums, a3, coarse, field, back = refs
    tile, me, tile_base, base = where_ref[0], where_ref[1], where_ref[2], where_ref[3]
    own = packs[0].shape[1]
    place_conv(packs, base, 8, w2s)
    for slot in range(nc):
        row = rows_of(slot, base, own)
        ups[pl.ds(row, own), :] = packs[slot][17]
        for jb in range(8):
            pooled_all[pl.ds(row, own), jb * 128 : (jb + 1) * 128] = packs[slot][jb]
        for other in range(mores[slot].shape[0] - 5):
            prims[pl.ds(row, own), other * 128 : (other + 1) * 128] = mores[slot][5 + other]

    def put(slot, ref, index):
        rims_all[slot] = ref[index]

    if len(rims) == 9:
        core = me & 1
        rims_all[1, pl.ds(pl.multiple_of(core * 128, 128), 128), :] = rims[4][0]
        rims_all[1, pl.ds(pl.multiple_of(128 - core * 128, 128), 128), :] = rims[8][0]
        rims = rims[:4] + rims[5:8]
    hold(rims, spots, me & 1, put)
    got = []
    for side in range(8):
        partner, turn, there = side_of(codes_ref, tile, side)
        piece = rims_all[
            partner ^ tile_base, pl.ds(pl.multiple_of(turn * HALF, HALF), HALF), :
        ].astype(F32)
        got.append(jnp.where(there, piece, 0.0))
    spread_columns(
        a3,
        left,
        right,
        act2_ref[...].astype(F32),
        got[0],
        flip32(got[2].astype(BF16)),
        flip32(got[3].astype(BF16)),
        got[1],
        (got[4][0:1], got[5][HALF - 1 : HALF], got[6][0:1], got[7][HALF - 1 : HALF]),
    )
    for a in range(3):
        w2t[a * 384 : (a + 1) * 384, :] = jnp.transpose(w2s[a * 128 : (a + 1) * 128, :])
    pooled = jnp.transpose(pooled_all[...])
    g3pad[0 : 2 * HALF, :] = jnp.zeros((2 * HALF, 128), BF16)
    g3pad[CELLS + 2 * HALF : CELLS + 4 * HALF, :] = jnp.zeros((2 * HALF, 128), BF16)
    for index in range(4):
        start = index * 256
        z3 = mm(
            jnp.concatenate(
                [a3[start + a * HALF : start + a * HALF + 256, :] for a in range(3)], axis=1
            ),
            w2t[...],
        )
        value, slope = gelu_and_slope(z3)
        coarse[start : start + 256, :] = value.astype(BF16)
        back_up = mm(pooled[start : start + 256, :], ups[...])
        g3pad[2 * HALF + start : 2 * HALF + start + 256, :] = (slope * back_up).astype(BF16)
    step = 34 * HALF // 4
    for index in range(4):
        start = index * step
        lhs = jnp.concatenate(
            [g3pad[start + (2 - a) * HALF : start + (2 - a) * HALF + step, :] for a in range(3)], axis=1
        )
        sums[start : start + step, :] = mm(lhs, w2s[...])
    rows = 34 * HALF
    column = iota((rows, 128), 0) % HALF
    middle = (
        sums[:, 128:256]
        + jnp.where(column == HALF - 1, 0.0, pltpu.roll(sums[:, 0:128], rows - 1, 0))
        + jnp.where(column == 0, 0.0, pltpu.roll(sums[:, 256:384], 1, 0))
    )
    field[...] = middle[HALF : HALF + CELLS, :]

    back[...] = jnp.zeros_like(back)
    tiles = codes_ref.shape[0]

    def following(before):
        found = []
        for side in range(4):
            spot = jnp.int32(tiles)
            for other in reversed(range(tiles)):
                take = is_owing(codes_ref, other, side, tile) & (other > before[side])
                spot = jnp.where(take, other, spot)
            found.append(spot)
        return tuple(found)

    def left_over(found):
        return (
            (found[0] < tiles) | (found[1] < tiles) | (found[2] < tiles) | (found[3] < tiles)
        )

    def visit(found):
        others = [jnp.minimum(spot, tiles - 1) for spot in found]
        others = others + [jnp.where(spot < tiles, 1, 0) for spot in found]
        back_from(others, codes_ref, tile, tile_base, rims_all, prims, w2s, w2t, ups, back)
        return following(found)

    lax.while_loop(left_over, visit, following((jnp.int32(-1),) * 4))
    anti = jnp.where(iota((HALF, HALF), 0) + iota((HALF, HALF), 1) == HALF - 1, 1.0, 0.0)

    def flip(values):
        return lax.dot_general(
            anti,
            values,
            (((1,), (0,)), ((), ())),
            preferred_element_type=F32,
            precision=lax.Precision.HIGHEST,
        )

    field[CELLS - HALF : CELLS, :] += back[0:32, :]
    field[0:HALF, :] += flip(back[64:96, :])
    first = pl.ds(0, HALF, stride=HALF)
    last = pl.ds(HALF - 1, HALF, stride=HALF)
    field[first, :] = field[first, :] + back[32:64, :]
    field[last, :] = field[last, :] + flip(back[96:128, :])

    g2 = (slope2_ref[...] * field[...]).astype(BF16)
    pick = own_rows(me, own, 128)
    g2_turned = mm_nt(one_hot(iota((128, 128), 0) == iota((128, 128), 1)), g2).astype(BF16)
    g2_own = mm_nt(pick, g2).astype(BF16)
    grads = jnp.zeros((3 * own, 384), F32)
    for ph in range(4):
        grad_ref[(9 + ph) * own : (10 + ph) * own, :] = mm(g2_own, act_ref[ph]).astype(BF16)
        turned = wdt_ref[pl.ds(pl.multiple_of(ph * 128 + me * own, own), own), :]
        cells = slice(ph * CELLS, (ph + 1) * CELLS)
        g1 = slope1_ref[:, cells] * (og_ref[:, cells].astype(F32) + mm(turned, g2_turned))
        grads = grads + mm(shifted_stack(g1), x3_ref[ph])
    own_taps(grad_ref, 0, grads, own)
    g3 = mm_nt(pick, g3pad[2 * HALF : 2 * HALF + CELLS, :])
    own_taps(grad_ref, 13, mm(shifted_stack(g3), a3[...]), own)
    own_spot = pl.ds(pl.multiple_of(me * own, own), own)
    grad_ref[22 * own : 23 * own, :] = mm(pooled_all[own_spot, :], coarse[...]).astype(BF16)
    if grad_ref.shape[0] > 23 * own:
        grad_ref[23 * own :, :] = jnp.zeros((grad_ref.shape[0] - 23 * own, 128), BF16)

    lifted = mm_nt(ups[own_spot, :], coarse[...])
    total = [
        own_ref[:, ph * CELLS : (ph + 1) * CELLS].astype(F32) + lifted for ph in range(4)
    ]
    stack = jnp.concatenate(
        [
            jnp.concatenate([total[ph][:, jb * 128 : (jb + 1) * 128] for ph in range(4)], axis=1)
            for jb in range(8)
        ],
        axis=0,
    ).astype(BF16)
    natural = mm_nt(stack, m_ref[:, 0:BLOCK]).astype(BF16)
    for jb in range(8):
        out_ref[:, jb * BLOCK : (jb + 1) * BLOCK] = natural[jb * own : (jb + 1) * own]


def sum_kernel(scale, in_ref, out_ref):
    total = in_ref[0].astype(F32)
    for slot in range(1, in_ref.shape[0]):
        total = total + in_ref[slot].astype(F32)
    out_ref[...] = (total * scale).astype(BF16)


def unpack_kernel(flat, one_ref, down_ref, two_ref, up_ref):
    own = up_ref.shape[0]
    for tap in range(9):
        one_ref[tap] = flat[tap * own : (tap + 1) * own, :].astype(F32)
        two_ref[tap] = flat[(13 + tap) * own : (14 + tap) * own, :].astype(F32)
    for ph in range(4):
        down_ref[ph] = flat[(9 + ph) * own : (10 + ph) * own, :].astype(F32)
    up_ref[...] = flat[22 * own : 23 * own, :].astype(F32)


def call(kernel, outs, *args, scratch=(), far=(), room=24, alias={}):
    specs = [
        pl.BlockSpec(
            memory_space=pltpu.SMEM if a.dtype == jnp.int32 else pltpu.HBM if i in far else pltpu.VMEM
        )
        for i, a in enumerate(args)
    ]
    many = isinstance(outs, list)
    vmem = pl.BlockSpec(memory_space=pltpu.VMEM)
    return pl.pallas_call(
        kernel,
        out_shape=outs,
        in_specs=specs,
        out_specs=[vmem] * len(outs) if many else vmem,
        scratch_shapes=list(scratch),
        input_output_aliases=alias,
        compiler_params=pltpu.CompilerParams(vmem_limit_bytes=room * 1024 * 1024),
    )(*args)


def shape(dims, kind=BF16):
    return jax.ShapeDtypeStruct(dims, kind)


def sort_matrix():
    table = np.zeros((BLOCK, 2 * BLOCK), np.float32)

    def lane(a, b, q, k):
        return q * 128 + a * 64 + 2 * k + b

    for a in range(2):
        for b in range(2):
            for q in range(4):
                for k in range(HALF):
                    table[lane(a, b, q, k), (2 * a + b) * 128 + q * HALF + k] = 1
    for x in range(2):
        for y in range(2):
            for j in range(HALF):
                spot = BLOCK + (2 * x + y) * HALF + j
                back = HALF - 1 - j
                table[lane(x, y, 3, j), spot] = 1
                table[lane(y, 1 - x, j % 4, 0), spot + 128] = 1
                table[lane(1 - x, 1 - y, 0, back), spot + 256] = 1
                table[lane(1 - y, x, back % 4, HALF - 1), spot + 384] = 1
    return jnp.asarray(table, BF16)


def paired(values, axis, bit):
    count = lax.axis_size(axis)
    return lax.ppermute(values, axis, [(i, i ^ bit) for i in range(count)])


FIRST, SECOND = (7, 4, 2), (6, 5, 3)


def is_split():
    return lax.axis_size("tile") == 8 and lax.axis_size("chan") % 2 == 0


def spots_of():
    tiles = lax.axis_size("tile")
    if not is_split():
        return [[(slot, slot) for slot in range(tiles)]]
    pairs = list(zip(FIRST, SECOND))
    return [[(0, 0)]] + [[pair] for pair in pairs] + [[pair[::-1]] for pair in pairs]


def copies(block, half=None, beside=()):
    tiles, nc = lax.axis_size("tile"), lax.axis_size("chan")
    if not is_split():
        return [swap(jnp.broadcast_to(block, (tiles,) + block.shape[1:]))], beside
    got = []
    for slots in zip(FIRST, SECOND):
        perm = [
            (tile * nc + chan, (tile ^ slots[chan & 1]) * nc + chan)
            for tile in range(tiles)
            for chan in range(nc)
        ]
        got.append(lax.ppermute(block, ("tile", "chan"), perm))
    got.append(paired(half, "tile", 1))
    got, beside = lax.optimization_barrier((got, beside))
    return [block] + got + [paired(part, "chan", 1) for part in got], beside


def swap(values):
    return lax.all_to_all(values, "tile", split_axis=0, concat_axis=0)


def gathered(values, axis):
    slots = {0: values}
    bit = lax.axis_size(axis) // 2
    while bit:
        slots.update({slot ^ bit: paired(held, axis, bit) for slot, held in list(slots.items())})
        bit //= 2
    return [slots[slot] for slot in range(len(slots))]


def per_device(features, conv1_weight, down_weight, conv2_weight, up_weight, out_grad, adjacency):
    own = features.shape[0]
    tiles, nc = lax.axis_size("tile"), lax.axis_size("chan")
    scale = float((tiles * SIDE * SIDE) ** (-0.5))
    tile, chan = lax.axis_index("tile"), lax.axis_index("chan")
    where = jnp.stack([tile, chan, tile if is_split() else tile * 0, chan]).astype(jnp.int32)
    matrix = sort_matrix()
    half = nc // 2

    pack, rims, sorted_g, pack2 = call(
        sort_kernel,
        [
            shape((45, own, 128)),
            shape((1, 5, own, 128)),
            shape((own, 4 * CELLS)),
            shape((18, own, 128)),
        ],
        features,
        out_grad,
        conv1_weight,
        down_weight,
        conv2_weight,
        up_weight,
        matrix,
        far=range(7),
        room=60,
        scratch=[
            pltpu.VMEM((own, 4 * CELLS), BF16),
            pltpu.VMEM((own, 4 * CELLS), BF16),
            pltpu.VMEM((BLOCK, 2 * BLOCK), BF16),
            pltpu.SemaphoreType.DMA((7,)),
        ],
    )
    pack_far = paired(pack, "chan", half)
    if is_split():
        far, near = paired(rims, "tile", 4), paired(rims, "tile", 2)
        cross = paired(far, "tile", 2)
        pack_near, pair = call(
            stage_kernel, [shape(pack.shape), shape((2,) + rims.shape[1:])], pack, rims, far
        )
        beside = paired(pair, "tile", 1)
        cross, near, pack_near, pack2, adjacency = lax.optimization_barrier(
            (cross, near, pack_near, pack2, adjacency)
        )
        last = [paired(near, "tile", 1), paired(cross, "tile", 1)]
        all_rims = [pair, near, cross, beside] + last
        rim_spots = [[(slot, slot) for slot in group] for group in ((0, 4), (2,), (6,), (1, 5), (3,), (7,))]
    else:
        all_rims, rim_spots = copies(rims)[0], spots_of()
        pack_near = pack
    turns = (adjacency[:, :, 1] + jnp.array(side_turns, jnp.int32)) & 3
    codes = jnp.where(adjacency[:, :, 0] < 0, -1, adjacency[:, :, 0] * 4 + turns)
    ring = call(
        partial(pick_kernel, rim_spots),
        shape((5 + tiles, own, 128)),
        codes,
        where,
        *all_rims,
        scratch=[pltpu.VMEM((tiles + 1, 5, own, 128), BF16)],
    )
    pack_far, ring = lax.optimization_barrier((pack_far, ring))
    ring_far = paired(ring, "chan", half)

    def whole(near, far, held=None):
        return [near if held is None else held, paired(near, "chan", 1), far, paired(far, "chan", 1)]

    packs = whole(pack, pack_far, pack_near)
    x3, z1c, w1t, wdt = call(
        partial(fine_center_kernel, nc),
        [
            shape((4, PADDED, 384)),
            shape((4, CELLS, 128), F32),
            shape((1152, 128)),
            shape((512, 128)),
        ],
        where,
        *packs,
        scratch=[
            pltpu.VMEM((384, 384), BF16),
            pltpu.VMEM((128, 512), BF16),
            pltpu.VMEM((128, 4 * CELLS), BF16),
        ],
    )
    x3, ring_far, pack2 = lax.optimization_barrier((x3, ring_far, pack2))
    pack2_far, pack2_side = paired(pack2, "chan", half), paired(pack2, "chan", 1)
    rings = whole(ring, ring_far)
    act, slope2, act2, rims2, half2, ring_sorted = call(
        partial(fine_ring_kernel, nc),
        [
            shape((4, CELLS, 128)),
            shape((CELLS, 128), F32),
            shape((CELLS, 128)),
            shape((1, 256, 128)),
            shape((1, 128, 128)),
            shape((5, 128, 128), F32),
        ],
        where,
        z1c,
        w1t,
        wdt,
        *rings,
        scratch=[
            pltpu.VMEM((5, 128, 128), BF16),
            pltpu.VMEM((4, CELLS, 128), F32),
            pltpu.VMEM((CELLS, 128), F32),
        ],
    )
    rims2, half2, pack2_side = lax.optimization_barrier((rims2, half2, pack2_side))
    act1, slope1, x3 = call(
        own_fine_kernel,
        [shape((own, 4 * CELLS)), shape((own, 4 * CELLS), F32), shape((4, PADDED, 384))],
        conv1_weight,
        ring_sorted,
        x3,
        alias={2: 2},
    )
    all_rims2, (act1, slope1, x3, pack2_far) = copies(rims2, half2, (act1, slope1, x3, pack2_far))
    packs2 = [pack2, pack2_side, pack2_far, paired(pack2_far, "chan", 1)]
    rows = -(-23 * own // (16 * tiles)) * 16
    output, late = call(
        partial(level_kernel, nc, spots_of()),
        [shape((own, 4 * CELLS)), shape((rows * tiles, 128))],
        codes,
        where,
        act2,
        slope2,
        act,
        wdt,
        act1,
        slope1,
        sorted_g,
        x3,
        matrix,
        *packs2,
        *rings,
        *all_rims2,
        scratch=[
            pltpu.VMEM((384, 384), BF16),
            pltpu.VMEM((1152, 128), BF16),
            pltpu.VMEM((128, 128), BF16),
            pltpu.VMEM((128, CELLS), BF16),
            pltpu.VMEM((128, tiles * 128), BF16),
            pltpu.VMEM((tiles, 256, 128), BF16),
            pltpu.VMEM((34 * HALF, 128), F32),
            pltpu.VMEM((34 * HALF, 128), F32),
            pltpu.VMEM((CELLS + 4 * HALF, 128), BF16),
            pltpu.VMEM((34 * HALF, 384), F32),
            pltpu.VMEM((PADDED, 384), BF16),
            pltpu.VMEM((CELLS, 128), BF16),
            pltpu.VMEM((CELLS, 128), F32),
            pltpu.VMEM((128, 128), F32),
        ],
    )
    pieces = swap(late.reshape(tiles, rows, 128))
    total = call(partial(sum_kernel, scale), shape((rows, 128)), pieces)
    total = swap(jnp.broadcast_to(total[None], (tiles, rows, 128)))
    grads = call(
        unpack_kernel,
        [
            shape((9, own, 128), F32),
            shape((4, own, 128), F32),
            shape((9, own, 128), F32),
            shape((own, 128), F32),
        ],
        total.reshape(tiles * rows, 128),
    )
    return (output, *grads)


def solution(mesh):
    placed = (
        P("chan", "tile"),
        P(None, "chan", None),
        P(None, "chan", None),
        P(None, "chan", None),
        P("chan", None),
        P("chan", "tile"),
        P(),
    )
    return jax.shard_map(
        per_device,
        mesh=mesh,
        in_specs=placed,
        out_specs=(
            P("chan", "tile"),
            P(None, "chan", None),
            P(None, "chan", None),
            P(None, "chan", None),
            P("chan", None),
        ),
        check_vma=False,
    )
```

```python
from functools import partial

import jax
import jax.numpy as jnp
import numpy as np
from jax import lax
from jax.experimental import pallas as pl
from jax.experimental.pallas import tpu as pltpu
from jax.sharding import PartitionSpec as P

SIDE = 64
HALF = 32
CELLS = HALF * HALF
PADDED = 36 * HALF
BLOCK = 8 * SIDE
BF16 = jnp.bfloat16
F32 = jnp.float32
NT = (((1,), (1,)), ((), ()))
ROOT = float(np.sqrt(2.0 / np.pi))
CUBE = 0.044715
side_turns = (0, 1, 2, 3, 0, 2, 2, 0)


def mm(left, right):
    return jnp.dot(left, right, preferred_element_type=F32)


def mm_nt(left, right):
    return lax.dot_general(left, right, NT, preferred_element_type=F32)


def gelu(v):
    return 0.5 * v * (1.0 + jnp.tanh(ROOT * (v + CUBE * (v * v * v))))


def gelu_slope(v):
    square = v * v
    t = jnp.tanh(ROOT * (v + CUBE * (square * v)))
    return 0.5 * (1.0 + t) + (0.5 * ROOT) * v * (1.0 - t * t) * (1.0 + 3.0 * CUBE * square)


def gelu_and_slope(v):
    square = v * v
    t = jnp.tanh(ROOT * (v + CUBE * (square * v)))
    both = 0.5 * (1.0 + t)
    return v * both, both + (0.5 * ROOT) * v * (1.0 - t * t) * (1.0 + 3.0 * CUBE * square)


def iota(shape, dim):
    return lax.broadcasted_iota(jnp.int32, shape, dim)


def one_hot(mask):
    return jnp.where(mask, 1.0, 0.0).astype(BF16)


def flip32(rows):
    anti = one_hot(iota((HALF, HALF), 0) + iota((HALF, HALF), 1) == HALF - 1)
    return mm(anti, rows)


def own_rows(me, own, chans):
    return one_hot(iota((own, chans), 0) + me * own == iota((own, chans), 1))


def side_of(codes_ref, tile, side):
    code = codes_ref[tile, side]
    return jnp.maximum(code, 0) // 4, code & 3, code >= 0


def is_beside(codes_ref, tile, side, partner):
    code = codes_ref[tile, side]
    return (code >= partner * 4) & (code < partner * 4 + 4)


def rows_of(slot, base, own):
    return pl.multiple_of((slot ^ base) * own, own)


def place_conv(packs, base, start, dst_ref):
    own = packs[0].shape[1]
    for slot, pack in enumerate(packs):
        row = rows_of(slot, base, own)
        for a in range(3):
            for b in range(3):
                dst_ref[pl.ds(a * 128 + row, own), b * 128 : (b + 1) * 128] = pack[start + 3 * a + b]


def spread_columns(dst, left, right, center, north, south, west, east, corners):
    rows = 34 * HALF
    middle = jnp.concatenate([north, center, south], axis=0)
    north_east, south_east, south_west, north_west = corners
    left[...] = pltpu.roll(middle, 1, 0)
    right[...] = pltpu.roll(middle, rows - 1, 0)
    left[pl.ds(HALF, HALF, stride=HALF), :] = west
    left[0:1, :] = north_west
    left[33 * HALF : 33 * HALF + 1, :] = south_west
    right[pl.ds(2 * HALF - 1, HALF, stride=HALF), :] = east
    right[HALF - 1 : HALF, :] = north_east
    right[rows - 1 : rows, :] = south_east
    dst[0:rows, 0:128] = left[...].astype(BF16)
    dst[0:rows, 128:256] = middle.astype(BF16)
    dst[0:rows, 256:384] = right[...].astype(BF16)
    dst[rows:PADDED, :] = jnp.zeros((PADDED - rows, 384), BF16)


def fetch(pairs, sems):
    started = [
        pltpu.make_async_copy(source, target, sems.at[index])
        for index, (source, target) in enumerate(pairs)
    ]
    for copy in started:
        copy.start()
    return started


def stacked(ref):
    return jnp.concatenate([ref[:, jb * BLOCK : (jb + 1) * BLOCK] for jb in range(8)], axis=0)


def sort_kernel(
    f_hbm, g_hbm, w1_hbm, wd_hbm, w2_hbm, up_hbm, m_hbm, pack_ref, rims_ref, sorted_ref, f_ref, g_ref, m_ref, sems
):
    count = f_ref.shape[0]
    started = fetch(
        [
            (f_hbm, f_ref),
            (m_hbm, m_ref),
            (g_hbm, g_ref),
            (w1_hbm, pack_ref.at[32:41]),
            (wd_hbm, pack_ref.at[41:45]),
            (w2_hbm, pack_ref.at[53:62]),
            (up_hbm, pack_ref.at[62]),
        ],
        sems,
    )
    lane = iota((count, BLOCK), 1)
    turn, slot = lane // 128, lane % HALF
    wanted = jnp.where(
        turn == 0, 7, jnp.where(turn == 1, slot // 4, jnp.where(turn == 2, 0, (HALF - 1 - slot) // 4))
    )
    spot, cell = iota((BLOCK, 128), 0), iota((BLOCK, 128), 1)
    pooling = one_hot((spot // 128 == cell // HALF) & (spot % HALF == cell % HALF))

    def moved(ref):
        stack = jnp.concatenate([ref[:, jb * BLOCK : (jb + 1) * BLOCK] for jb in range(8)], axis=0)
        both = mm(stack, m_ref[...])
        parts = [both[jb * count : (jb + 1) * count] for jb in range(8)]
        rims = jnp.zeros((count, BLOCK), F32)
        for jb in range(8):
            rims = rims + jnp.where(wanted == jb, parts[jb][:, BLOCK:], 0.0)
        return [[part[:, ph * 128 : (ph + 1) * 128] for ph in range(4)] for part in parts], rims.astype(BF16)

    started[0].wait()
    started[1].wait()
    pieces, rims = moved(f_ref)
    for turn_index in range(4):
        rims_ref[0, turn_index] = rims[:, turn_index * 128 : (turn_index + 1) * 128]
    for jb in range(8):
        for ph in range(4):
            pack_ref[ph * 8 + jb] = pieces[jb][ph].astype(BF16)
    started[2].wait()
    pieces, rims = moved(g_ref)
    rims_ref[0, 4] = mm(rims, pooling).astype(BF16)
    for jb in range(8):
        for ph in range(4):
            sorted_ref[:, ph * CELLS + jb * 128 : ph * CELLS + (jb + 1) * 128] = pieces[jb][ph].astype(BF16)
        pack_ref[45 + jb] = ((pieces[jb][0] + pieces[jb][1]) + (pieces[jb][2] + pieces[jb][3])).astype(BF16)
    for copy in started[3:]:
        copy.wait()


def hold(refs, spots, core, put):
    for ref, slots in zip(refs, spots):
        for index, (even, odd) in enumerate(slots):
            slot = even if even == odd else jnp.where(core == 0, even, odd)
            put(slot, ref, index)


def pick_kernel(spots, codes_ref, where_ref, *refs):
    *rims, out_ref, held = refs
    tile, base, core = where_ref[0], where_ref[2], where_ref[1] & 1

    def put(slot, ref, index):
        held[slot] = ref[index]

    hold(rims, spots, core, put)
    lane = iota(out_ref.shape[1:], 1) % HALF
    corners = jnp.zeros(lane.shape, F32)
    for side in range(8):
        partner, turn, there = side_of(codes_ref, tile, side)
        picked = jnp.where(there, held[partner ^ base, turn].astype(F32), 0.0)
        if side < 4:
            out_ref[side] = picked.astype(BF16)
        else:
            shift, spot = ((0, 0), (0, HALF - 1), (1, 1), (127, HALF - 2))[side - 4]
            moved = pltpu.roll(picked, shift, 1) if shift else picked
            corners = corners + jnp.where(lane == spot, moved, 0.0)
    out_ref[4] = corners.astype(BF16)
    for other in range(out_ref.shape[0] - 5):
        out_ref[5 + other] = held[other ^ base, 4]


def stage_kernel(pack_ref, rims_ref, far_ref, near_ref, pair_ref):
    near_ref[...] = pack_ref[...]
    pair_ref[0:1] = rims_ref[...]
    pair_ref[1:2] = far_ref[...]


def fine_center_kernel(nc, where_ref, *refs):
    packs, refs = refs[:nc], refs[nc:]
    x3_ref, z1_ref, w1t, wdt, w1s, wds, f_all = refs
    base = where_ref[3]
    own = packs[0].shape[1]
    for slot, pack in enumerate(packs):
        row = rows_of(slot, base, own)
        for block in range(32):
            f_all[pl.ds(row, own), block * 128 : (block + 1) * 128] = pack[block]
        for a in range(3):
            for b in range(3):
                w1s[pl.ds(a * 128 + row, own), b * 128 : (b + 1) * 128] = pack[32 + 3 * a + b]
        for ph in range(4):
            wds[pl.ds(row, own), ph * 128 : (ph + 1) * 128] = pack[41 + ph]
    for a in range(3):
        w1t[a * 384 : (a + 1) * 384, :] = jnp.transpose(w1s[a * 128 : (a + 1) * 128, :])
    wdt[...] = jnp.transpose(wds[...])
    column = iota((CELLS, 128), 0) % HALF
    for ph in range(4):
        center = jnp.transpose(f_all[:, ph * CELLS : (ph + 1) * CELLS]).astype(F32)
        left = jnp.where(column == 0, 0.0, pltpu.roll(center, 1, 0))
        right = jnp.where(column == HALF - 1, 0.0, pltpu.roll(center, CELLS - 1, 0))
        x3_ref[ph, 0:HALF, :] = jnp.zeros((HALF, 384), BF16)
        x3_ref[ph, HALF : HALF + CELLS, 0:128] = left.astype(BF16)
        x3_ref[ph, HALF : HALF + CELLS, 128:256] = center.astype(BF16)
        x3_ref[ph, HALF : HALF + CELLS, 256:384] = right.astype(BF16)
        x3_ref[ph, HALF + CELLS : PADDED, :] = jnp.zeros((PADDED - HALF - CELLS, 384), BF16)
        for start in range(0, CELLS, 256):
            window = jnp.concatenate(
                [x3_ref[ph, start + a * HALF : start + a * HALF + 256, :] for a in range(3)], axis=1
            )
            z1_ref[ph, start : start + 256, :] = mm(window, w1t[...])


def ring_pieces(ring, ph):
    a, b = ph // 2, ph % 2
    near, far = ph * HALF, ((1 - a) * 2 + (1 - b)) * HALF
    east, west = ((1 - b) * 2 + a) * HALF, (b * 2 + (1 - a)) * HALF
    return (
        ring[0, near : near + HALF],
        ring[1, east : east + HALF],
        ring[2, far : far + HALF],
        ring[3, west : west + HALF],
        (
            ring[4, near : near + 1],
            ring[4, far + HALF - 1 : far + HALF],
            ring[4, far + 1 : far + 2],
            ring[4, near + HALF - 2 : near + HALF - 1],
        ),
    )


def windows_of(row, first, final):
    place = iota((HALF, 128), 0)
    return jnp.concatenate(
        [
            jnp.where(place == 0, first, pltpu.roll(row, 1, 0)),
            row,
            jnp.where(place == HALF - 1, final, pltpu.roll(row, HALF - 1, 0)),
        ],
        axis=1,
    ).astype(BF16)


def fine_ring_kernel(nc, where_ref, z1_in, w1t, wdt, *refs):
    rings, refs = refs[:nc], refs[nc:]
    act_ref, slope2_ref, act2_ref, rims_ref, half_ref, ring, ring_all, z1, wide = refs
    base = where_ref[3]
    own = rings[0].shape[1]
    for slot in range(nc):
        row = rows_of(slot, base, own)
        for side in range(5):
            ring_all[side, pl.ds(row, own), :] = rings[slot][side]
    row, col = iota((128, 128), 0), iota((128, 128), 1)
    same = one_hot(row == col)
    turned = one_hot((row // HALF == col // HALF) & (row % HALF + col % HALF == HALF - 1))
    for side in range(5):
        ring[side] = mm_nt(turned if side in (2, 3) else same, ring_all[side])
    z1[...] = z1_in[...]
    pieces = [ring_pieces(ring, ph) for ph in range(4)]

    def owed(rows, weights):
        return mm(jnp.concatenate(rows, axis=0), weights)

    def column(tap):
        return jnp.concatenate(
            [w1t[a * 384 + tap * 128 : a * 384 + (tap + 1) * 128, :] for a in range(3)], axis=0
        )

    north = owed([windows_of(p[0], p[4][3], p[4][0]) for p in pieces], w1t[0:384, :])
    south = owed([windows_of(p[2], p[4][2], p[4][1]) for p in pieces], w1t[768:1152, :])
    west = owed([windows_of(p[3], 0.0, 0.0) for p in pieces], column(0))
    east = owed([windows_of(p[1], 0.0, 0.0) for p in pieces], column(2))
    first = pl.ds(0, HALF, stride=HALF)
    last = pl.ds(HALF - 1, HALF, stride=HALF)
    for ph in range(4):
        rows = slice(ph * HALF, (ph + 1) * HALF)
        z1[ph, 0:HALF, :] += north[rows]
        z1[ph, CELLS - HALF : CELLS, :] += south[rows]
        z1[ph, first, :] = z1[ph, first, :] + west[rows]
        z1[ph, last, :] = z1[ph, last, :] + east[rows]

    def chunk(index, carry):
        start = index * 256
        acts = []
        for ph in range(4):
            act = gelu(z1[ph, pl.ds(start, 256), :]).astype(BF16)
            act_ref[ph, pl.ds(start, 256), :] = act
            acts.append(act)
        z2 = mm(jnp.concatenate(acts, axis=1), wdt[...])
        value, slope = gelu_and_slope(z2)
        slope2_ref[pl.ds(start, 256), :] = slope
        act2 = value.astype(BF16)
        act2_ref[pl.ds(start, 256), :] = act2
        wide[pl.ds(start, 256), :] = act2.astype(F32)
        return carry

    lax.fori_loop(0, 4, chunk, 0)
    for deep in range(2):
        start = CELLS - (deep + 1) * HALF
        rims_ref[0, deep * 128 : deep * 128 + 32, :] = act2_ref[start : start + HALF, :]
        rims_ref[0, deep * 128 + 32 : deep * 128 + 64, :] = wide[
            pl.ds(deep, HALF, stride=HALF), :
        ].astype(BF16)
        rims_ref[0, deep * 128 + 64 : deep * 128 + 96, :] = flip32(
            act2_ref[deep * HALF : (deep + 1) * HALF, :]
        ).astype(BF16)
        rims_ref[0, deep * 128 + 96 : deep * 128 + 128, :] = flip32(
            wide[pl.ds(HALF - 1 - deep, HALF, stride=HALF), :].astype(BF16)
        ).astype(BF16)
    half_ref[0] = rims_ref[0, pl.ds(pl.multiple_of((where_ref[1] & 1) * 128, 128), 128), :]


def own_fine_kernel(w1_ref, ring, x3_in, act_ref, slope_ref, x3_ref):
    own = w1_ref.shape[1]
    row, col = iota((CELLS, HALF), 0), iota((CELLS, HALF), 1)
    at_first, at_last = one_hot(row == col * HALF), one_hot(row == col * HALF + HALF - 1)
    inner = slice(HALF, HALF + CELLS)
    stack = jnp.concatenate(
        [
            jnp.concatenate([w1_ref[3 * a + b] for b in range(3)], axis=1)
            for a in range(3)
        ],
        axis=0,
    )
    for ph in range(4):
        north, east, south, west, corners = ring_pieces(ring, ph)
        x3_ref[ph, inner, 128:256] = x3_in[ph, inner, 128:256]
        x3_ref[ph, 2 * HALF + CELLS : PADDED, :] = jnp.zeros((PADDED - 2 * HALF - CELLS, 384), BF16)
        x3_ref[ph, 0:HALF, :] = windows_of(north, corners[3], corners[0])
        x3_ref[ph, HALF + CELLS : 2 * HALF + CELLS, :] = windows_of(south, corners[2], corners[1])
        x3_ref[ph, inner, 0:128] = x3_in[ph, inner, 0:128] + mm(at_first, west.astype(BF16)).astype(BF16)
        x3_ref[ph, inner, 256:384] = x3_in[ph, inner, 256:384] + mm(at_last, east.astype(BF16)).astype(
            BF16
        )
        terms = mm_nt(stack, x3_ref[ph])
        total = terms[0:own, 0:CELLS]
        for a in range(1, 3):
            moved = pltpu.roll(terms[a * own : (a + 1) * own], PADDED - a * HALF, 1)
            total = total + moved[:, 0:CELLS]
        value, slope = gelu_and_slope(total)
        act_ref[:, ph * CELLS : (ph + 1) * CELLS] = value.astype(BF16)
        slope_ref[:, ph * CELLS : (ph + 1) * CELLS] = slope


def turned_tap(turn, a, b):
    return ((a, b), (b, 2 - a), (2 - a, 2 - b), (2 - b, a))[turn]


CORNER_ENDS = {4: 0, 5: HALF - 1, 6: 0, 7: HALF - 1}
LOW_LEFT = (4, 5, 6, 7)
LOW_RIGHT = (7, 4, 5, 6)


def is_owing(codes_ref, other, side, tile):
    owing = is_beside(codes_ref, other, side, tile)
    if side in (0, 2):
        owing = owing | is_beside(codes_ref, other, LOW_LEFT[side], tile)
        owing = owing | is_beside(codes_ref, other, LOW_RIGHT[side], tile)
    return owing


def strip_of(side, other, codes_ref, base, rims_all):
    turn = (side + 2) % 4

    def rim(partner, slot):
        return rims_all[partner ^ base, pl.ds(pl.multiple_of(slot * HALF, HALF), HALF), :]

    partner, slot, _ = side_of(codes_ref, other, side)
    left_partner, left_slot, _ = side_of(codes_ref, other, (side + 1) % 4)
    right_partner, right_slot, _ = side_of(codes_ref, other, (side + 3) % 4)
    ends = []
    for corner in (LOW_LEFT[side], LOW_RIGHT[side]):
        corner_partner, corner_slot, there = side_of(codes_ref, other, corner)
        spot = CORNER_ENDS[corner]
        row = rim(corner_partner, corner_slot).astype(F32)[spot : spot + 1]
        ends.append(jnp.where(there, row, 0.0))
    left, right = rim(left_partner, left_slot).astype(F32), rim(right_partner, right_slot).astype(F32)
    last = HALF - 1
    here = rims_all[other ^ base, turn * HALF : (turn + 1) * HALF, :].astype(F32)
    above = rims_all[other ^ base, 128 + turn * HALF : 128 + (turn + 1) * HALF, :].astype(F32)
    below = flip32(rim(partner, slot))
    place = iota((HALF, 128), 0)
    by_tap = {}
    for a, (row, first, final) in enumerate(
        (
            (above, left[1:2], right[last - 1 : last]),
            (here, left[0:1], right[last : last + 1]),
            (below, ends[0], ends[1]),
        )
    ):
        by_tap[turned_tap(turn, a, 0)] = jnp.where(place == 0, first, pltpu.roll(row, 1, 0))
        by_tap[turned_tap(turn, a, 1)] = row
        by_tap[turned_tap(turn, a, 2)] = jnp.where(place == last, final, pltpu.roll(row, last, 0))
    return jnp.concatenate([by_tap[a, b] for a in range(3) for b in range(3)], axis=1).astype(BF16)


def back_from(others, codes_ref, tile, base, rims_all, prims, w2s, w2t, ups, back):
    last = HALF - 1
    place = iota((HALF, 128), 0)
    z3 = mm(
        jnp.concatenate([strip_of(side, others[side], codes_ref, base, rims_all) for side in range(4)], axis=0),
        w2t[...],
    )
    pooled = []
    for side in range(4):
        turn = (side + 2) % 4
        select = one_hot(iota((HALF, 128), 0) + turn * HALF == iota((HALF, 128), 1))
        cells = prims[:, pl.ds(pl.multiple_of(others[side] * 128, 128), 128)]
        pooled.append(mm_nt(select, cells))
    g3 = gelu_slope(z3) * mm(jnp.concatenate(pooled, axis=0).astype(BF16), ups[...])
    row, col = iota((128, 128), 0), iota((128, 128), 1)
    turned = one_hot((row // HALF == col // HALF) & (row % HALF + col % HALF == HALF - 1))
    g3 = mm(turned, g3.astype(BF16)).astype(BF16)
    for side in range(4):
        other = others[side]
        owed = []
        for b in range(3):
            r, c = turned_tap((side + 2) % 4, 2, b)
            owed.append(
                mm(
                    g3[side * HALF : (side + 1) * HALF],
                    w2s[r * 128 : (r + 1) * 128, c * 128 : (c + 1) * 128],
                )
            )
        total = (
            jnp.where(place == 0, 0.0, pltpu.roll(owed[0], 1, 0))
            + owed[1]
            + jnp.where(place == last, 0.0, pltpu.roll(owed[2], last, 0))
        )
        _, slot, _ = side_of(codes_ref, other, side)
        counts = is_beside(codes_ref, other, side, tile) & (others[side + 4] == 1)
        back[pl.ds(pl.multiple_of(slot * HALF, HALF), HALF), :] += jnp.where(counts, total, 0.0)
        if side in (0, 2):
            for corner, line in (
                (LOW_LEFT[side], owed[0][last : last + 1]),
                (LOW_RIGHT[side], owed[2][0:1]),
            ):
                _, corner_slot, _ = side_of(codes_ref, other, corner)
                counts = is_beside(codes_ref, other, corner, tile) & (others[side + 4] == 1)

                @pl.when(counts)
                def _():
                    back[pl.ds(pl.multiple_of(corner_slot * HALF, HALF), HALF), :] += jnp.where(
                        place == CORNER_ENDS[corner], line, 0.0
                    )


def own_taps(grad_ref, start, grads, own):
    for a in range(3):
        for b in range(3):
            row = (start + 3 * a + b) * own
            grad_ref[row : row + own, :] = grads[
                a * own : (a + 1) * own, b * 128 : (b + 1) * 128
            ].astype(BF16)


def shifted_stack(values):
    wide = jnp.concatenate([values, jnp.zeros((values.shape[0], PADDED - CELLS), F32)], axis=1)
    return jnp.concatenate(
        [(pltpu.roll(wide, a * HALF, 1) if a else wide).astype(BF16) for a in range(3)], axis=0
    )


def level_kernel(
    nc,
    spots,
    codes_ref,
    where_ref,
    act2_ref,
    slope2_ref,
    act_ref,
    wdt_ref,
    own_ref,
    slope1_ref,
    og_ref,
    x3_ref,
    m_ref,
    *refs,
):
    packs, mores, refs = refs[:nc], refs[nc : 2 * nc], refs[2 * nc :]
    *rims, out_ref, grad_ref, w2s, w2t, ups, pooled_all, prims, rims_all, left, right, g3pad, sums, a3, coarse, field, back = refs
    tile, me, tile_base, base = where_ref[0], where_ref[1], where_ref[2], where_ref[3]
    own = packs[0].shape[1]
    place_conv(packs, base, 53, w2s)
    for slot in range(nc):
        row = rows_of(slot, base, own)
        ups[pl.ds(row, own), :] = packs[slot][62]
        for jb in range(8):
            pooled_all[pl.ds(row, own), jb * 128 : (jb + 1) * 128] = packs[slot][45 + jb]
        for other in range(mores[slot].shape[0] - 5):
            prims[pl.ds(row, own), other * 128 : (other + 1) * 128] = mores[slot][5 + other]

    def put(slot, ref, index):
        rims_all[slot] = ref[index]

    if len(rims) == 9:
        core = me & 1
        rims_all[1, pl.ds(pl.multiple_of(core * 128, 128), 128), :] = rims[4][0]
        rims_all[1, pl.ds(pl.multiple_of(128 - core * 128, 128), 128), :] = rims[8][0]
        rims = rims[:4] + rims[5:8]
    hold(rims, spots, me & 1, put)
    got = []
    for side in range(8):
        partner, turn, there = side_of(codes_ref, tile, side)
        piece = rims_all[
            partner ^ tile_base, pl.ds(pl.multiple_of(turn * HALF, HALF), HALF), :
        ].astype(F32)
        got.append(jnp.where(there, piece, 0.0))
    spread_columns(
        a3,
        left,
        right,
        act2_ref[...].astype(F32),
        got[0],
        flip32(got[2].astype(BF16)),
        flip32(got[3].astype(BF16)),
        got[1],
        (got[4][0:1], got[5][HALF - 1 : HALF], got[6][0:1], got[7][HALF - 1 : HALF]),
    )
    for a in range(3):
        w2t[a * 384 : (a + 1) * 384, :] = jnp.transpose(w2s[a * 128 : (a + 1) * 128, :])
    pooled = jnp.transpose(pooled_all[...])
    g3pad[0 : 2 * HALF, :] = jnp.zeros((2 * HALF, 128), BF16)
    g3pad[CELLS + 2 * HALF : CELLS + 4 * HALF, :] = jnp.zeros((2 * HALF, 128), BF16)
    for index in range(4):
        start = index * 256
        z3 = mm(
            jnp.concatenate(
                [a3[start + a * HALF : start + a * HALF + 256, :] for a in range(3)], axis=1
            ),
            w2t[...],
        )
        value, slope = gelu_and_slope(z3)
        coarse[start : start + 256, :] = value.astype(BF16)
        back_up = mm(pooled[start : start + 256, :], ups[...])
        g3pad[2 * HALF + start : 2 * HALF + start + 256, :] = (slope * back_up).astype(BF16)
    step = 34 * HALF // 4
    for index in range(4):
        start = index * step
        lhs = jnp.concatenate(
            [g3pad[start + (2 - a) * HALF : start + (2 - a) * HALF + step, :] for a in range(3)], axis=1
        )
        sums[start : start + step, :] = mm(lhs, w2s[...])
    rows = 34 * HALF
    column = iota((rows, 128), 0) % HALF
    middle = (
        sums[:, 128:256]
        + jnp.where(column == HALF - 1, 0.0, pltpu.roll(sums[:, 0:128], rows - 1, 0))
        + jnp.where(column == 0, 0.0, pltpu.roll(sums[:, 256:384], 1, 0))
    )
    field[...] = middle[HALF : HALF + CELLS, :]

    back[...] = jnp.zeros_like(back)
    tiles = codes_ref.shape[0]

    def following(before):
        found = []
        for side in range(4):
            spot = jnp.int32(tiles)
            for other in reversed(range(tiles)):
                take = is_owing(codes_ref, other, side, tile) & (other > before[side])
                spot = jnp.where(take, other, spot)
            found.append(spot)
        return tuple(found)

    def left_over(found):
        return (
            (found[0] < tiles) | (found[1] < tiles) | (found[2] < tiles) | (found[3] < tiles)
        )

    def visit(found):
        others = [jnp.minimum(spot, tiles - 1) for spot in found]
        others = others + [jnp.where(spot < tiles, 1, 0) for spot in found]
        back_from(others, codes_ref, tile, tile_base, rims_all, prims, w2s, w2t, ups, back)
        return following(found)

    lax.while_loop(left_over, visit, following((jnp.int32(-1),) * 4))
    anti = jnp.where(iota((HALF, HALF), 0) + iota((HALF, HALF), 1) == HALF - 1, 1.0, 0.0)

    def flip(values):
        return lax.dot_general(
            anti,
            values,
            (((1,), (0,)), ((), ())),
            preferred_element_type=F32,
            precision=lax.Precision.HIGHEST,
        )

    field[CELLS - HALF : CELLS, :] += back[0:32, :]
    field[0:HALF, :] += flip(back[64:96, :])
    first = pl.ds(0, HALF, stride=HALF)
    last = pl.ds(HALF - 1, HALF, stride=HALF)
    field[first, :] = field[first, :] + back[32:64, :]
    field[last, :] = field[last, :] + flip(back[96:128, :])

    g2 = (slope2_ref[...] * field[...]).astype(BF16)
    pick = own_rows(me, own, 128)
    g2_turned = mm_nt(one_hot(iota((128, 128), 0) == iota((128, 128), 1)), g2).astype(BF16)
    g2_own = mm_nt(pick, g2).astype(BF16)
    grads = jnp.zeros((3 * own, 384), F32)
    for ph in range(4):
        grad_ref[(9 + ph) * own : (10 + ph) * own, :] = mm(g2_own, act_ref[ph]).astype(BF16)
        turned = wdt_ref[pl.ds(pl.multiple_of(ph * 128 + me * own, own), own), :]
        cells = slice(ph * CELLS, (ph + 1) * CELLS)
        g1 = slope1_ref[:, cells] * (og_ref[:, cells].astype(F32) + mm(turned, g2_turned))
        grads = grads + mm(shifted_stack(g1), x3_ref[ph])
    own_taps(grad_ref, 0, grads, own)
    g3 = mm_nt(pick, g3pad[2 * HALF : 2 * HALF + CELLS, :])
    own_taps(grad_ref, 13, mm(shifted_stack(g3), a3[...]), own)
    own_spot = pl.ds(pl.multiple_of(me * own, own), own)
    grad_ref[22 * own : 23 * own, :] = mm(pooled_all[own_spot, :], coarse[...]).astype(BF16)
    if grad_ref.shape[0] > 23 * own:
        grad_ref[23 * own :, :] = jnp.zeros((grad_ref.shape[0] - 23 * own, 128), BF16)

    lifted = mm_nt(ups[own_spot, :], coarse[...])
    total = [
        own_ref[:, ph * CELLS : (ph + 1) * CELLS].astype(F32) + lifted for ph in range(4)
    ]
    stack = jnp.concatenate(
        [
            jnp.concatenate([total[ph][:, jb * 128 : (jb + 1) * 128] for ph in range(4)], axis=1)
            for jb in range(8)
        ],
        axis=0,
    ).astype(BF16)
    natural = mm_nt(stack, m_ref[:, 0:BLOCK]).astype(BF16)
    for jb in range(8):
        out_ref[:, jb * BLOCK : (jb + 1) * BLOCK] = natural[jb * own : (jb + 1) * own]


def sum_kernel(scale, in_ref, out_ref):
    total = in_ref[0].astype(F32)
    for slot in range(1, in_ref.shape[0]):
        total = total + in_ref[slot].astype(F32)
    out_ref[...] = (total * scale).astype(BF16)


def unpack_kernel(flat, one_ref, down_ref, two_ref, up_ref):
    own = up_ref.shape[0]
    for tap in range(9):
        one_ref[tap] = flat[tap * own : (tap + 1) * own, :].astype(F32)
        two_ref[tap] = flat[(13 + tap) * own : (14 + tap) * own, :].astype(F32)
    for ph in range(4):
        down_ref[ph] = flat[(9 + ph) * own : (10 + ph) * own, :].astype(F32)
    up_ref[...] = flat[22 * own : 23 * own, :].astype(F32)


def call(kernel, outs, *args, scratch=(), far=(), room=24, alias={}):
    specs = [
        pl.BlockSpec(
            memory_space=pltpu.SMEM if a.dtype == jnp.int32 else pltpu.HBM if i in far else pltpu.VMEM
        )
        for i, a in enumerate(args)
    ]
    many = isinstance(outs, list)
    vmem = pl.BlockSpec(memory_space=pltpu.VMEM)
    return pl.pallas_call(
        kernel,
        out_shape=outs,
        in_specs=specs,
        out_specs=[vmem] * len(outs) if many else vmem,
        scratch_shapes=list(scratch),
        input_output_aliases=alias,
        compiler_params=pltpu.CompilerParams(vmem_limit_bytes=room * 1024 * 1024),
    )(*args)


def shape(dims, kind=BF16):
    return jax.ShapeDtypeStruct(dims, kind)


def sort_matrix():
    table = np.zeros((BLOCK, 2 * BLOCK), np.float32)

    def lane(a, b, q, k):
        return q * 128 + a * 64 + 2 * k + b

    for a in range(2):
        for b in range(2):
            for q in range(4):
                for k in range(HALF):
                    table[lane(a, b, q, k), (2 * a + b) * 128 + q * HALF + k] = 1
    for x in range(2):
        for y in range(2):
            for j in range(HALF):
                spot = BLOCK + (2 * x + y) * HALF + j
                back = HALF - 1 - j
                table[lane(x, y, 3, j), spot] = 1
                table[lane(y, 1 - x, j % 4, 0), spot + 128] = 1
                table[lane(1 - x, 1 - y, 0, back), spot + 256] = 1
                table[lane(1 - y, x, back % 4, HALF - 1), spot + 384] = 1
    return jnp.asarray(table, BF16)


def paired(values, axis, bit):
    count = lax.axis_size(axis)
    return lax.ppermute(values, axis, [(i, i ^ bit) for i in range(count)])


FIRST, SECOND = (7, 4, 2), (6, 5, 3)


def is_split():
    return lax.axis_size("tile") == 8 and lax.axis_size("chan") % 2 == 0


def spots_of():
    tiles = lax.axis_size("tile")
    if not is_split():
        return [[(slot, slot) for slot in range(tiles)]]
    pairs = list(zip(FIRST, SECOND))
    return [[(0, 0)]] + [[pair] for pair in pairs] + [[pair[::-1]] for pair in pairs]


def copies(block, half=None, beside=()):
    tiles, nc = lax.axis_size("tile"), lax.axis_size("chan")
    if not is_split():
        return [swap(jnp.broadcast_to(block, (tiles,) + block.shape[1:]))], beside
    got = []
    for slots in zip(FIRST, SECOND):
        perm = [
            (tile * nc + chan, (tile ^ slots[chan & 1]) * nc + chan)
            for tile in range(tiles)
            for chan in range(nc)
        ]
        got.append(lax.ppermute(block, ("tile", "chan"), perm))
    got.append(paired(half, "tile", 1))
    got, beside = lax.optimization_barrier((got, beside))
    return [block] + got + [paired(part, "chan", 1) for part in got], beside


def swap(values):
    return lax.all_to_all(values, "tile", split_axis=0, concat_axis=0)


def gathered(values, axis):
    slots = {0: values}
    bit = lax.axis_size(axis) // 2
    while bit:
        slots.update({slot ^ bit: paired(held, axis, bit) for slot, held in list(slots.items())})
        bit //= 2
    return [slots[slot] for slot in range(len(slots))]


def per_device(features, conv1_weight, down_weight, conv2_weight, up_weight, out_grad, adjacency):
    own = features.shape[0]
    tiles, nc = lax.axis_size("tile"), lax.axis_size("chan")
    scale = float((tiles * SIDE * SIDE) ** (-0.5))
    tile, chan = lax.axis_index("tile"), lax.axis_index("chan")
    where = jnp.stack([tile, chan, tile if is_split() else tile * 0, chan]).astype(jnp.int32)
    matrix = sort_matrix()
    half = nc // 2

    pack, rims, sorted_g = call(
        sort_kernel,
        [shape((63, own, 128)), shape((1, 5, own, 128)), shape((own, 4 * CELLS))],
        features,
        out_grad,
        conv1_weight,
        down_weight,
        conv2_weight,
        up_weight,
        matrix,
        far=range(7),
        room=60,
        scratch=[
            pltpu.VMEM((own, 4 * CELLS), BF16),
            pltpu.VMEM((own, 4 * CELLS), BF16),
            pltpu.VMEM((BLOCK, 2 * BLOCK), BF16),
            pltpu.SemaphoreType.DMA((7,)),
        ],
    )
    pack_far = paired(pack, "chan", half)
    if is_split():
        far, near = paired(rims, "tile", 4), paired(rims, "tile", 2)
        cross = paired(far, "tile", 2)
        pack_near, pair = call(
            stage_kernel, [shape(pack.shape), shape((2,) + rims.shape[1:])], pack, rims, far
        )
        beside = paired(pair, "tile", 1)
        cross, near, pack_near, adjacency = lax.optimization_barrier((cross, near, pack_near, adjacency))
        last = [paired(near, "tile", 1), paired(cross, "tile", 1)]
        all_rims = [pair, near, cross, beside] + last
        rim_spots = [[(slot, slot) for slot in group] for group in ((0, 4), (2,), (6,), (1, 5), (3,), (7,))]
    else:
        all_rims, rim_spots = copies(rims)[0], spots_of()
        pack_near = pack
    turns = (adjacency[:, :, 1] + jnp.array(side_turns, jnp.int32)) & 3
    codes = jnp.where(adjacency[:, :, 0] < 0, -1, adjacency[:, :, 0] * 4 + turns)
    ring = call(
        partial(pick_kernel, rim_spots),
        shape((5 + tiles, own, 128)),
        codes,
        where,
        *all_rims,
        scratch=[pltpu.VMEM((tiles + 1, 5, own, 128), BF16)],
    )
    pack_far, ring = lax.optimization_barrier((pack_far, ring))
    ring_far = paired(ring, "chan", half)

    def whole(near, far, held=None):
        return [near if held is None else held, paired(near, "chan", 1), far, paired(far, "chan", 1)]

    packs = whole(pack, pack_far, pack_near)
    x3, z1c, w1t, wdt = call(
        partial(fine_center_kernel, nc),
        [
            shape((4, PADDED, 384)),
            shape((4, CELLS, 128), F32),
            shape((1152, 128)),
            shape((512, 128)),
        ],
        where,
        *packs,
        scratch=[
            pltpu.VMEM((384, 384), BF16),
            pltpu.VMEM((128, 512), BF16),
            pltpu.VMEM((128, 4 * CELLS), BF16),
        ],
    )
    x3, ring_far = lax.optimization_barrier((x3, ring_far))
    rings = whole(ring, ring_far)
    act, slope2, act2, rims2, half2, ring_sorted = call(
        partial(fine_ring_kernel, nc),
        [
            shape((4, CELLS, 128)),
            shape((CELLS, 128), F32),
            shape((CELLS, 128)),
            shape((1, 256, 128)),
            shape((1, 128, 128)),
            shape((5, 128, 128), F32),
        ],
        where,
        z1c,
        w1t,
        wdt,
        *rings,
        scratch=[
            pltpu.VMEM((5, 128, 128), BF16),
            pltpu.VMEM((4, CELLS, 128), F32),
            pltpu.VMEM((CELLS, 128), F32),
        ],
    )
    act1, slope1, x3 = call(
        own_fine_kernel,
        [shape((own, 4 * CELLS)), shape((own, 4 * CELLS), F32), shape((4, PADDED, 384))],
        conv1_weight,
        ring_sorted,
        x3,
        alias={2: 2},
    )
    all_rims2, (act1, slope1, x3) = copies(rims2, half2, (act1, slope1, x3))
    rows = -(-23 * own // (16 * tiles)) * 16
    output, late = call(
        partial(level_kernel, nc, spots_of()),
        [shape((own, 4 * CELLS)), shape((rows * tiles, 128))],
        codes,
        where,
        act2,
        slope2,
        act,
        wdt,
        act1,
        slope1,
        sorted_g,
        x3,
        matrix,
        *packs,
        *rings,
        *all_rims2,
        scratch=[
            pltpu.VMEM((384, 384), BF16),
            pltpu.VMEM((1152, 128), BF16),
            pltpu.VMEM((128, 128), BF16),
            pltpu.VMEM((128, CELLS), BF16),
            pltpu.VMEM((128, tiles * 128), BF16),
            pltpu.VMEM((tiles, 256, 128), BF16),
            pltpu.VMEM((34 * HALF, 128), F32),
            pltpu.VMEM((34 * HALF, 128), F32),
            pltpu.VMEM((CELLS + 4 * HALF, 128), BF16),
            pltpu.VMEM((34 * HALF, 384), F32),
            pltpu.VMEM((PADDED, 384), BF16),
            pltpu.VMEM((CELLS, 128), BF16),
            pltpu.VMEM((CELLS, 128), F32),
            pltpu.VMEM((128, 128), F32),
        ],
    )
    pieces = swap(late.reshape(tiles, rows, 128))
    total = call(partial(sum_kernel, scale), shape((rows, 128)), pieces)
    total = swap(jnp.broadcast_to(total[None], (tiles, rows, 128)))
    grads = call(
        unpack_kernel,
        [
            shape((9, own, 128), F32),
            shape((4, own, 128), F32),
            shape((9, own, 128), F32),
            shape((own, 128), F32),
        ],
        total.reshape(tiles * rows, 128),
    )
    return (output, *grads)


def solution(mesh):
    placed = (
        P("chan", "tile"),
        P(None, "chan", None),
        P(None, "chan", None),
        P(None, "chan", None),
        P("chan", None),
        P("chan", "tile"),
        P(),
    )
    return jax.shard_map(
        per_device,
        mesh=mesh,
        in_specs=placed,
        out_specs=(
            P("chan", "tile"),
            P(None, "chan", None),
            P(None, "chan", None),
            P(None, "chan", None),
            P("chan", None),
        ),
        check_vma=False,
    )
```

```python
from functools import partial

import jax
import jax.numpy as jnp
import numpy as np
from jax import lax
from jax.experimental import pallas as pl
from jax.experimental.pallas import tpu as pltpu
from jax.sharding import PartitionSpec as P

SIDE = 64
HALF = 32
CELLS = HALF * HALF
PADDED = 36 * HALF
BLOCK = 8 * SIDE
BF16 = jnp.bfloat16
F32 = jnp.float32
NT = (((1,), (1,)), ((), ()))
ROOT = float(np.sqrt(2.0 / np.pi))
CUBE = 0.044715
side_turns = (0, 1, 2, 3, 0, 2, 2, 0)


def mm(left, right):
    return jnp.dot(left, right, preferred_element_type=F32)


def mm_nt(left, right):
    return lax.dot_general(left, right, NT, preferred_element_type=F32)


def gelu(v):
    return 0.5 * v * (1.0 + jnp.tanh(ROOT * (v + CUBE * (v * v * v))))


def gelu_slope(v):
    square = v * v
    t = jnp.tanh(ROOT * (v + CUBE * (square * v)))
    return 0.5 * (1.0 + t) + (0.5 * ROOT) * v * (1.0 - t * t) * (1.0 + 3.0 * CUBE * square)


def gelu_and_slope(v):
    square = v * v
    t = jnp.tanh(ROOT * (v + CUBE * (square * v)))
    both = 0.5 * (1.0 + t)
    return v * both, both + (0.5 * ROOT) * v * (1.0 - t * t) * (1.0 + 3.0 * CUBE * square)


def iota(shape, dim):
    return lax.broadcasted_iota(jnp.int32, shape, dim)


def one_hot(mask):
    return jnp.where(mask, 1.0, 0.0).astype(BF16)


def flip32(rows):
    anti = one_hot(iota((HALF, HALF), 0) + iota((HALF, HALF), 1) == HALF - 1)
    return mm(anti, rows)


def own_rows(me, own, chans):
    return one_hot(iota((own, chans), 0) + me * own == iota((own, chans), 1))


def side_of(codes_ref, tile, side):
    code = codes_ref[tile, side]
    return jnp.maximum(code, 0) // 4, code & 3, code >= 0


def is_beside(codes_ref, tile, side, partner):
    code = codes_ref[tile, side]
    return (code >= partner * 4) & (code < partner * 4 + 4)


def rows_of(slot, base, own):
    return pl.multiple_of((slot ^ base) * own, own)


def place_conv(packs, base, start, dst_ref):
    own = packs[0].shape[1]
    for slot, pack in enumerate(packs):
        row = rows_of(slot, base, own)
        for a in range(3):
            for b in range(3):
                dst_ref[pl.ds(a * 128 + row, own), b * 128 : (b + 1) * 128] = pack[start + 3 * a + b]


def spread_columns(dst, left, right, center, north, south, west, east, corners):
    rows = 34 * HALF
    middle = jnp.concatenate([north, center, south], axis=0)
    north_east, south_east, south_west, north_west = corners
    left[...] = pltpu.roll(middle, 1, 0)
    right[...] = pltpu.roll(middle, rows - 1, 0)
    left[pl.ds(HALF, HALF, stride=HALF), :] = west
    left[0:1, :] = north_west
    left[33 * HALF : 33 * HALF + 1, :] = south_west
    right[pl.ds(2 * HALF - 1, HALF, stride=HALF), :] = east
    right[HALF - 1 : HALF, :] = north_east
    right[rows - 1 : rows, :] = south_east
    dst[0:rows, 0:128] = left[...].astype(BF16)
    dst[0:rows, 128:256] = middle.astype(BF16)
    dst[0:rows, 256:384] = right[...].astype(BF16)
    dst[rows:PADDED, :] = jnp.zeros((PADDED - rows, 384), BF16)


def fetch(pairs, sems):
    started = [
        pltpu.make_async_copy(source, target, sems.at[index])
        for index, (source, target) in enumerate(pairs)
    ]
    for copy in started:
        copy.start()
    return started


def stacked(ref):
    return jnp.concatenate([ref[:, jb * BLOCK : (jb + 1) * BLOCK] for jb in range(8)], axis=0)


def fill_table(m_ref):
    lane = iota((16, BLOCK), 1)
    quarter, k = (lane >> 5) & 3, lane & 31
    sort_place = quarter * 128 + (lane >> 8) * 64 + 2 * k + ((lane >> 7) & 1)
    turn, x, y, back = lane >> 7, (lane >> 6) & 1, (lane >> 5) & 1, 31 - k
    rim_place = jnp.where(
        turn == 0,
        384 + x * 64 + 2 * k + y,
        jnp.where(
            turn == 1,
            (k & 3) * 128 + y * 64 + 1 - x,
            jnp.where(
                turn == 2,
                (1 - x) * 64 + 2 * back + 1 - y,
                (back & 3) * 128 + (1 - y) * 64 + 62 + x,
            ),
        ),
    )
    place = jnp.concatenate([sort_place, rim_place], axis=1)
    row = iota((16, 2 * BLOCK), 0)
    for group in range(BLOCK // 16):
        m_ref[group * 16 : (group + 1) * 16, :] = one_hot(row + group * 16 == place)


def sort_kernel(
    f_hbm, g_hbm, w1_hbm, wd_hbm, w2_hbm, up_hbm, pack_ref, rims_ref, sorted_ref, pack2_ref, f_ref, g_ref, m_ref, sems
):
    count = f_ref.shape[0]
    started = fetch(
        [
            (f_hbm, f_ref),
            (g_hbm, g_ref),
            (w1_hbm, pack_ref.at[32:41]),
            (wd_hbm, pack_ref.at[41:45]),
            (w2_hbm, pack2_ref.at[8:17]),
            (up_hbm, pack2_ref.at[17]),
        ],
        sems,
    )
    lane = iota((count, BLOCK), 1)
    turn, slot = lane // 128, lane % HALF
    wanted = jnp.where(
        turn == 0, 7, jnp.where(turn == 1, slot // 4, jnp.where(turn == 2, 0, (HALF - 1 - slot) // 4))
    )
    spot, cell = iota((BLOCK, 128), 0), iota((BLOCK, 128), 1)
    pooling = one_hot((spot // 128 == cell // HALF) & (spot % HALF == cell % HALF))

    def moved(ref):
        stack = jnp.concatenate([ref[:, jb * BLOCK : (jb + 1) * BLOCK] for jb in range(8)], axis=0)
        both = mm(stack, m_ref[...])
        parts = [both[jb * count : (jb + 1) * count] for jb in range(8)]
        rims = jnp.zeros((count, BLOCK), F32)
        for jb in range(8):
            rims = rims + jnp.where(wanted == jb, parts[jb][:, BLOCK:], 0.0)
        return [[part[:, ph * 128 : (ph + 1) * 128] for ph in range(4)] for part in parts], rims.astype(BF16)

    fill_table(m_ref)
    started[0].wait()
    pieces, rims = moved(f_ref)
    for turn_index in range(4):
        rims_ref[0, turn_index] = rims[:, turn_index * 128 : (turn_index + 1) * 128]
    for jb in range(8):
        for ph in range(4):
            pack_ref[ph * 8 + jb] = pieces[jb][ph].astype(BF16)
    started[1].wait()
    pieces, rims = moved(g_ref)
    rims_ref[0, 4] = mm(rims, pooling).astype(BF16)
    for jb in range(8):
        for ph in range(4):
            sorted_ref[:, ph * CELLS + jb * 128 : ph * CELLS + (jb + 1) * 128] = pieces[jb][ph].astype(BF16)
        pack2_ref[jb] = ((pieces[jb][0] + pieces[jb][1]) + (pieces[jb][2] + pieces[jb][3])).astype(BF16)
    for copy in started[2:]:
        copy.wait()


def hold(refs, spots, core, put):
    for ref, slots in zip(refs, spots):
        for index, (even, odd) in enumerate(slots):
            slot = even if even == odd else jnp.where(core == 0, even, odd)
            put(slot, ref, index)


def pick_kernel(spots, codes_ref, where_ref, *refs):
    *rims, out_ref, held = refs
    tile, base, core = where_ref[0], where_ref[2], where_ref[1] & 1

    def put(slot, ref, index):
        held[slot] = ref[index]

    hold(rims, spots, core, put)
    lane = iota(out_ref.shape[1:], 1) % HALF
    corners = jnp.zeros(lane.shape, F32)
    for side in range(8):
        partner, turn, there = side_of(codes_ref, tile, side)
        picked = jnp.where(there, held[partner ^ base, turn].astype(F32), 0.0)
        if side < 4:
            out_ref[side] = picked.astype(BF16)
        else:
            shift, spot = ((0, 0), (0, HALF - 1), (1, 1), (127, HALF - 2))[side - 4]
            moved = pltpu.roll(picked, shift, 1) if shift else picked
            corners = corners + jnp.where(lane == spot, moved, 0.0)
    out_ref[4] = corners.astype(BF16)
    for other in range(out_ref.shape[0] - 5):
        out_ref[5 + other] = held[other ^ base, 4]


def stage_kernel(pack_ref, rims_ref, far_ref, near_ref, pair_ref):
    near_ref[...] = pack_ref[...]
    pair_ref[0:1] = rims_ref[...]
    pair_ref[1:2] = far_ref[...]


def fine_center_kernel(nc, where_ref, *refs):
    packs, refs = refs[:nc], refs[nc:]
    x3_ref, z1_ref, w1t, wdt, w1s, wds, f_all = refs
    base = where_ref[3]
    own = packs[0].shape[1]
    for slot, pack in enumerate(packs):
        row = rows_of(slot, base, own)
        for block in range(32):
            f_all[pl.ds(row, own), block * 128 : (block + 1) * 128] = pack[block]
        for a in range(3):
            for b in range(3):
                w1s[pl.ds(a * 128 + row, own), b * 128 : (b + 1) * 128] = pack[32 + 3 * a + b]
        for ph in range(4):
            wds[pl.ds(row, own), ph * 128 : (ph + 1) * 128] = pack[41 + ph]
    for a in range(3):
        w1t[a * 384 : (a + 1) * 384, :] = jnp.transpose(w1s[a * 128 : (a + 1) * 128, :])
    wdt[...] = jnp.transpose(wds[...])
    column = iota((CELLS, 128), 0) % HALF
    for ph in range(4):
        center = jnp.transpose(f_all[:, ph * CELLS : (ph + 1) * CELLS]).astype(F32)
        left = jnp.where(column == 0, 0.0, pltpu.roll(center, 1, 0))
        right = jnp.where(column == HALF - 1, 0.0, pltpu.roll(center, CELLS - 1, 0))
        x3_ref[ph, 0:HALF, :] = jnp.zeros((HALF, 384), BF16)
        x3_ref[ph, HALF : HALF + CELLS, 0:128] = left.astype(BF16)
        x3_ref[ph, HALF : HALF + CELLS, 128:256] = center.astype(BF16)
        x3_ref[ph, HALF : HALF + CELLS, 256:384] = right.astype(BF16)
        x3_ref[ph, HALF + CELLS : PADDED, :] = jnp.zeros((PADDED - HALF - CELLS, 384), BF16)
        for start in range(0, CELLS, 256):
            window = jnp.concatenate(
                [x3_ref[ph, start + a * HALF : start + a * HALF + 256, :] for a in range(3)], axis=1
            )
            z1_ref[ph, start : start + 256, :] = mm(window, w1t[...])


def ring_pieces(ring, ph):
    a, b = ph // 2, ph % 2
    near, far = ph * HALF, ((1 - a) * 2 + (1 - b)) * HALF
    east, west = ((1 - b) * 2 + a) * HALF, (b * 2 + (1 - a)) * HALF
    return (
        ring[0, near : near + HALF],
        ring[1, east : east + HALF],
        ring[2, far : far + HALF],
        ring[3, west : west + HALF],
        (
            ring[4, near : near + 1],
            ring[4, far + HALF - 1 : far + HALF],
            ring[4, far + 1 : far + 2],
            ring[4, near + HALF - 2 : near + HALF - 1],
        ),
    )


def windows_of(row, first, final):
    place = iota((HALF, 128), 0)
    return jnp.concatenate(
        [
            jnp.where(place == 0, first, pltpu.roll(row, 1, 0)),
            row,
            jnp.where(place == HALF - 1, final, pltpu.roll(row, HALF - 1, 0)),
        ],
        axis=1,
    ).astype(BF16)


def fine_ring_kernel(nc, where_ref, z1_in, w1t, wdt, *refs):
    rings, refs = refs[:nc], refs[nc:]
    act_ref, slope2_ref, act2_ref, rims_ref, half_ref, ring, ring_all, z1, wide = refs
    base = where_ref[3]
    own = rings[0].shape[1]
    for slot in range(nc):
        row = rows_of(slot, base, own)
        for side in range(5):
            ring_all[side, pl.ds(row, own), :] = rings[slot][side]
    row, col = iota((128, 128), 0), iota((128, 128), 1)
    same = one_hot(row == col)
    turned = one_hot((row // HALF == col // HALF) & (row % HALF + col % HALF == HALF - 1))
    for side in range(5):
        ring[side] = mm_nt(turned if side in (2, 3) else same, ring_all[side])
    z1[...] = z1_in[...]
    pieces = [ring_pieces(ring, ph) for ph in range(4)]

    def owed(rows, weights):
        return mm(jnp.concatenate(rows, axis=0), weights)

    def column(tap):
        return jnp.concatenate(
            [w1t[a * 384 + tap * 128 : a * 384 + (tap + 1) * 128, :] for a in range(3)], axis=0
        )

    north = owed([windows_of(p[0], p[4][3], p[4][0]) for p in pieces], w1t[0:384, :])
    south = owed([windows_of(p[2], p[4][2], p[4][1]) for p in pieces], w1t[768:1152, :])
    west = owed([windows_of(p[3], 0.0, 0.0) for p in pieces], column(0))
    east = owed([windows_of(p[1], 0.0, 0.0) for p in pieces], column(2))
    first = pl.ds(0, HALF, stride=HALF)
    last = pl.ds(HALF - 1, HALF, stride=HALF)
    for ph in range(4):
        rows = slice(ph * HALF, (ph + 1) * HALF)
        z1[ph, 0:HALF, :] += north[rows]
        z1[ph, CELLS - HALF : CELLS, :] += south[rows]
        z1[ph, first, :] = z1[ph, first, :] + west[rows]
        z1[ph, last, :] = z1[ph, last, :] + east[rows]

    def chunk(index, carry):
        start = index * 256
        acts = []
        for ph in range(4):
            act = gelu(z1[ph, pl.ds(start, 256), :]).astype(BF16)
            act_ref[ph, pl.ds(start, 256), :] = act
            acts.append(act)
        z2 = mm(jnp.concatenate(acts, axis=1), wdt[...])
        value, slope = gelu_and_slope(z2)
        slope2_ref[pl.ds(start, 256), :] = slope
        act2 = value.astype(BF16)
        act2_ref[pl.ds(start, 256), :] = act2
        wide[pl.ds(start, 256), :] = act2.astype(F32)
        return carry

    lax.fori_loop(0, 4, chunk, 0)
    for deep in range(2):
        start = CELLS - (deep + 1) * HALF
        rims_ref[0, deep * 128 : deep * 128 + 32, :] = act2_ref[start : start + HALF, :]
        rims_ref[0, deep * 128 + 32 : deep * 128 + 64, :] = wide[
            pl.ds(deep, HALF, stride=HALF), :
        ].astype(BF16)
        rims_ref[0, deep * 128 + 64 : deep * 128 + 96, :] = flip32(
            act2_ref[deep * HALF : (deep + 1) * HALF, :]
        ).astype(BF16)
        rims_ref[0, deep * 128 + 96 : deep * 128 + 128, :] = flip32(
            wide[pl.ds(HALF - 1 - deep, HALF, stride=HALF), :].astype(BF16)
        ).astype(BF16)
    half_ref[0] = rims_ref[0, pl.ds(pl.multiple_of((where_ref[1] & 1) * 128, 128), 128), :]


def own_fine_kernel(w1_ref, ring, x3_in, act_ref, slope_ref, x3_ref):
    own = w1_ref.shape[1]
    row, col = iota((CELLS, HALF), 0), iota((CELLS, HALF), 1)
    at_first, at_last = one_hot(row == col * HALF), one_hot(row == col * HALF + HALF - 1)
    inner = slice(HALF, HALF + CELLS)
    stack = jnp.concatenate(
        [
            jnp.concatenate([w1_ref[3 * a + b] for b in range(3)], axis=1)
            for a in range(3)
        ],
        axis=0,
    )
    for ph in range(4):
        north, east, south, west, corners = ring_pieces(ring, ph)
        x3_ref[ph, inner, 128:256] = x3_in[ph, inner, 128:256]
        x3_ref[ph, 2 * HALF + CELLS : PADDED, :] = jnp.zeros((PADDED - 2 * HALF - CELLS, 384), BF16)
        x3_ref[ph, 0:HALF, :] = windows_of(north, corners[3], corners[0])
        x3_ref[ph, HALF + CELLS : 2 * HALF + CELLS, :] = windows_of(south, corners[2], corners[1])
        x3_ref[ph, inner, 0:128] = x3_in[ph, inner, 0:128] + mm(at_first, west.astype(BF16)).astype(BF16)
        x3_ref[ph, inner, 256:384] = x3_in[ph, inner, 256:384] + mm(at_last, east.astype(BF16)).astype(
            BF16
        )
        terms = mm_nt(stack, x3_ref[ph])
        total = terms[0:own, 0:CELLS]
        for a in range(1, 3):
            moved = pltpu.roll(terms[a * own : (a + 1) * own], PADDED - a * HALF, 1)
            total = total + moved[:, 0:CELLS]
        value, slope = gelu_and_slope(total)
        act_ref[:, ph * CELLS : (ph + 1) * CELLS] = value.astype(BF16)
        slope_ref[:, ph * CELLS : (ph + 1) * CELLS] = slope


def turned_tap(turn, a, b):
    return ((a, b), (b, 2 - a), (2 - a, 2 - b), (2 - b, a))[turn]


CORNER_ENDS = {4: 0, 5: HALF - 1, 6: 0, 7: HALF - 1}
LOW_LEFT = (4, 5, 6, 7)
LOW_RIGHT = (7, 4, 5, 6)


def is_owing(codes_ref, other, side, tile):
    owing = is_beside(codes_ref, other, side, tile)
    if side in (0, 2):
        owing = owing | is_beside(codes_ref, other, LOW_LEFT[side], tile)
        owing = owing | is_beside(codes_ref, other, LOW_RIGHT[side], tile)
    return owing


def strip_of(side, other, codes_ref, base, rims_all):
    turn = (side + 2) % 4

    def rim(partner, slot):
        return rims_all[partner ^ base, pl.ds(pl.multiple_of(slot * HALF, HALF), HALF), :]

    partner, slot, _ = side_of(codes_ref, other, side)
    left_partner, left_slot, _ = side_of(codes_ref, other, (side + 1) % 4)
    right_partner, right_slot, _ = side_of(codes_ref, other, (side + 3) % 4)
    ends = []
    for corner in (LOW_LEFT[side], LOW_RIGHT[side]):
        corner_partner, corner_slot, there = side_of(codes_ref, other, corner)
        spot = CORNER_ENDS[corner]
        row = rim(corner_partner, corner_slot).astype(F32)[spot : spot + 1]
        ends.append(jnp.where(there, row, 0.0))
    left, right = rim(left_partner, left_slot).astype(F32), rim(right_partner, right_slot).astype(F32)
    last = HALF - 1
    here = rims_all[other ^ base, turn * HALF : (turn + 1) * HALF, :].astype(F32)
    above = rims_all[other ^ base, 128 + turn * HALF : 128 + (turn + 1) * HALF, :].astype(F32)
    below = flip32(rim(partner, slot))
    place = iota((HALF, 128), 0)
    by_tap = {}
    for a, (row, first, final) in enumerate(
        (
            (above, left[1:2], right[last - 1 : last]),
            (here, left[0:1], right[last : last + 1]),
            (below, ends[0], ends[1]),
        )
    ):
        by_tap[turned_tap(turn, a, 0)] = jnp.where(place == 0, first, pltpu.roll(row, 1, 0))
        by_tap[turned_tap(turn, a, 1)] = row
        by_tap[turned_tap(turn, a, 2)] = jnp.where(place == last, final, pltpu.roll(row, last, 0))
    return jnp.concatenate([by_tap[a, b] for a in range(3) for b in range(3)], axis=1).astype(BF16)


def back_from(others, codes_ref, tile, base, rims_all, prims, w2s, w2t, ups, back):
    last = HALF - 1
    place = iota((HALF, 128), 0)
    z3 = mm(
        jnp.concatenate([strip_of(side, others[side], codes_ref, base, rims_all) for side in range(4)], axis=0),
        w2t[...],
    )
    pooled = []
    for side in range(4):
        turn = (side + 2) % 4
        select = one_hot(iota((HALF, 128), 0) + turn * HALF == iota((HALF, 128), 1))
        cells = prims[:, pl.ds(pl.multiple_of(others[side] * 128, 128), 128)]
        pooled.append(mm_nt(select, cells))
    g3 = gelu_slope(z3) * mm(jnp.concatenate(pooled, axis=0).astype(BF16), ups[...])
    row, col = iota((128, 128), 0), iota((128, 128), 1)
    turned = one_hot((row // HALF == col // HALF) & (row % HALF + col % HALF == HALF - 1))
    g3 = mm(turned, g3.astype(BF16)).astype(BF16)
    for side in range(4):
        other = others[side]
        owed = []
        for b in range(3):
            r, c = turned_tap((side + 2) % 4, 2, b)
            owed.append(
                mm(
                    g3[side * HALF : (side + 1) * HALF],
                    w2s[r * 128 : (r + 1) * 128, c * 128 : (c + 1) * 128],
                )
            )
        total = (
            jnp.where(place == 0, 0.0, pltpu.roll(owed[0], 1, 0))
            + owed[1]
            + jnp.where(place == last, 0.0, pltpu.roll(owed[2], last, 0))
        )
        _, slot, _ = side_of(codes_ref, other, side)
        counts = is_beside(codes_ref, other, side, tile) & (others[side + 4] == 1)
        back[pl.ds(pl.multiple_of(slot * HALF, HALF), HALF), :] += jnp.where(counts, total, 0.0)
        if side in (0, 2):
            for corner, line in (
                (LOW_LEFT[side], owed[0][last : last + 1]),
                (LOW_RIGHT[side], owed[2][0:1]),
            ):
                _, corner_slot, _ = side_of(codes_ref, other, corner)
                counts = is_beside(codes_ref, other, corner, tile) & (others[side + 4] == 1)

                @pl.when(counts)
                def _():
                    back[pl.ds(pl.multiple_of(corner_slot * HALF, HALF), HALF), :] += jnp.where(
                        place == CORNER_ENDS[corner], line, 0.0
                    )


def own_taps(grad_ref, start, grads, own):
    for a in range(3):
        for b in range(3):
            row = (start + 3 * a + b) * own
            grad_ref[row : row + own, :] = grads[
                a * own : (a + 1) * own, b * 128 : (b + 1) * 128
            ].astype(BF16)


def shifted_stack(values):
    wide = jnp.concatenate([values, jnp.zeros((values.shape[0], PADDED - CELLS), F32)], axis=1)
    return jnp.concatenate(
        [(pltpu.roll(wide, a * HALF, 1) if a else wide).astype(BF16) for a in range(3)], axis=0
    )


def level_kernel(
    nc,
    spots,
    codes_ref,
    where_ref,
    act2_ref,
    slope2_ref,
    act_ref,
    wdt_ref,
    own_ref,
    slope1_ref,
    og_ref,
    x3_ref,
    m_ref,
    *refs,
):
    packs, mores, refs = refs[:nc], refs[nc : 2 * nc], refs[2 * nc :]
    *rims, out_ref, grad_ref, w2s, w2t, ups, pooled_all, prims, rims_all, left, right, g3pad, sums, a3, coarse, field, back = refs
    tile, me, tile_base, base = where_ref[0], where_ref[1], where_ref[2], where_ref[3]
    own = packs[0].shape[1]
    place_conv(packs, base, 8, w2s)
    for slot in range(nc):
        row = rows_of(slot, base, own)
        ups[pl.ds(row, own), :] = packs[slot][17]
        for jb in range(8):
            pooled_all[pl.ds(row, own), jb * 128 : (jb + 1) * 128] = packs[slot][jb]
        for other in range(mores[slot].shape[0] - 5):
            prims[pl.ds(row, own), other * 128 : (other + 1) * 128] = mores[slot][5 + other]

    def put(slot, ref, index):
        rims_all[slot] = ref[index]

    if len(rims) == 9:
        core = me & 1
        rims_all[1, pl.ds(pl.multiple_of(core * 128, 128), 128), :] = rims[4][0]
        rims_all[1, pl.ds(pl.multiple_of(128 - core * 128, 128), 128), :] = rims[8][0]
        rims = rims[:4] + rims[5:8]
    hold(rims, spots, me & 1, put)
    got = []
    for side in range(8):
        partner, turn, there = side_of(codes_ref, tile, side)
        piece = rims_all[
            partner ^ tile_base, pl.ds(pl.multiple_of(turn * HALF, HALF), HALF), :
        ].astype(F32)
        got.append(jnp.where(there, piece, 0.0))
    spread_columns(
        a3,
        left,
        right,
        act2_ref[...].astype(F32),
        got[0],
        flip32(got[2].astype(BF16)),
        flip32(got[3].astype(BF16)),
        got[1],
        (got[4][0:1], got[5][HALF - 1 : HALF], got[6][0:1], got[7][HALF - 1 : HALF]),
    )
    for a in range(3):
        w2t[a * 384 : (a + 1) * 384, :] = jnp.transpose(w2s[a * 128 : (a + 1) * 128, :])
    pooled = jnp.transpose(pooled_all[...])
    g3pad[0 : 2 * HALF, :] = jnp.zeros((2 * HALF, 128), BF16)
    g3pad[CELLS + 2 * HALF : CELLS + 4 * HALF, :] = jnp.zeros((2 * HALF, 128), BF16)
    for index in range(4):
        start = index * 256
        z3 = mm(
            jnp.concatenate(
                [a3[start + a * HALF : start + a * HALF + 256, :] for a in range(3)], axis=1
            ),
            w2t[...],
        )
        value, slope = gelu_and_slope(z3)
        coarse[start : start + 256, :] = value.astype(BF16)
        back_up = mm(pooled[start : start + 256, :], ups[...])
        g3pad[2 * HALF + start : 2 * HALF + start + 256, :] = (slope * back_up).astype(BF16)
    step = 34 * HALF // 4
    for index in range(4):
        start = index * step
        lhs = jnp.concatenate(
            [g3pad[start + (2 - a) * HALF : start + (2 - a) * HALF + step, :] for a in range(3)], axis=1
        )
        sums[start : start + step, :] = mm(lhs, w2s[...])
    rows = 34 * HALF
    column = iota((rows, 128), 0) % HALF
    middle = (
        sums[:, 128:256]
        + jnp.where(column == HALF - 1, 0.0, pltpu.roll(sums[:, 0:128], rows - 1, 0))
        + jnp.where(column == 0, 0.0, pltpu.roll(sums[:, 256:384], 1, 0))
    )
    field[...] = middle[HALF : HALF + CELLS, :]

    back[...] = jnp.zeros_like(back)
    tiles = codes_ref.shape[0]

    def following(before):
        found = []
        for side in range(4):
            spot = jnp.int32(tiles)
            for other in reversed(range(tiles)):
                take = is_owing(codes_ref, other, side, tile) & (other > before[side])
                spot = jnp.where(take, other, spot)
            found.append(spot)
        return tuple(found)

    def left_over(found):
        return (
            (found[0] < tiles) | (found[1] < tiles) | (found[2] < tiles) | (found[3] < tiles)
        )

    def visit(found):
        others = [jnp.minimum(spot, tiles - 1) for spot in found]
        others = others + [jnp.where(spot < tiles, 1, 0) for spot in found]
        back_from(others, codes_ref, tile, tile_base, rims_all, prims, w2s, w2t, ups, back)
        return following(found)

    lax.while_loop(left_over, visit, following((jnp.int32(-1),) * 4))
    anti = jnp.where(iota((HALF, HALF), 0) + iota((HALF, HALF), 1) == HALF - 1, 1.0, 0.0)

    def flip(values):
        return lax.dot_general(
            anti,
            values,
            (((1,), (0,)), ((), ())),
            preferred_element_type=F32,
            precision=lax.Precision.HIGHEST,
        )

    field[CELLS - HALF : CELLS, :] += back[0:32, :]
    field[0:HALF, :] += flip(back[64:96, :])
    first = pl.ds(0, HALF, stride=HALF)
    last = pl.ds(HALF - 1, HALF, stride=HALF)
    field[first, :] = field[first, :] + back[32:64, :]
    field[last, :] = field[last, :] + flip(back[96:128, :])

    g2 = (slope2_ref[...] * field[...]).astype(BF16)
    pick = own_rows(me, own, 128)
    g2_turned = mm_nt(one_hot(iota((128, 128), 0) == iota((128, 128), 1)), g2).astype(BF16)
    g2_own = mm_nt(pick, g2).astype(BF16)
    grads = jnp.zeros((3 * own, 384), F32)
    for ph in range(4):
        grad_ref[(9 + ph) * own : (10 + ph) * own, :] = mm(g2_own, act_ref[ph]).astype(BF16)
        turned = wdt_ref[pl.ds(pl.multiple_of(ph * 128 + me * own, own), own), :]
        cells = slice(ph * CELLS, (ph + 1) * CELLS)
        g1 = slope1_ref[:, cells] * (og_ref[:, cells].astype(F32) + mm(turned, g2_turned))
        grads = grads + mm(shifted_stack(g1), x3_ref[ph])
    own_taps(grad_ref, 0, grads, own)
    g3 = mm_nt(pick, g3pad[2 * HALF : 2 * HALF + CELLS, :])
    own_taps(grad_ref, 13, mm(shifted_stack(g3), a3[...]), own)
    own_spot = pl.ds(pl.multiple_of(me * own, own), own)
    grad_ref[22 * own : 23 * own, :] = mm(pooled_all[own_spot, :], coarse[...]).astype(BF16)
    if grad_ref.shape[0] > 23 * own:
        grad_ref[23 * own :, :] = jnp.zeros((grad_ref.shape[0] - 23 * own, 128), BF16)

    lifted = mm_nt(ups[own_spot, :], coarse[...])
    total = [
        own_ref[:, ph * CELLS : (ph + 1) * CELLS].astype(F32) + lifted for ph in range(4)
    ]
    stack = jnp.concatenate(
        [
            jnp.concatenate([total[ph][:, jb * 128 : (jb + 1) * 128] for ph in range(4)], axis=1)
            for jb in range(8)
        ],
        axis=0,
    ).astype(BF16)
    natural = mm_nt(stack, m_ref[...]).astype(BF16)
    for jb in range(8):
        out_ref[:, jb * BLOCK : (jb + 1) * BLOCK] = natural[jb * own : (jb + 1) * own]


def sum_kernel(scale, in_ref, out_ref):
    total = in_ref[0].astype(F32)
    for slot in range(1, in_ref.shape[0]):
        total = total + in_ref[slot].astype(F32)
    out_ref[...] = (total * scale).astype(BF16)


def unpack_kernel(flat, one_ref, down_ref, two_ref, up_ref):
    own = up_ref.shape[0]
    for tap in range(9):
        one_ref[tap] = flat[tap * own : (tap + 1) * own, :].astype(F32)
        two_ref[tap] = flat[(13 + tap) * own : (14 + tap) * own, :].astype(F32)
    for ph in range(4):
        down_ref[ph] = flat[(9 + ph) * own : (10 + ph) * own, :].astype(F32)
    up_ref[...] = flat[22 * own : 23 * own, :].astype(F32)


def call(kernel, outs, *args, scratch=(), far=(), room=24, alias={}):
    specs = [
        pl.BlockSpec(
            memory_space=pltpu.SMEM if a.dtype == jnp.int32 else pltpu.HBM if i in far else pltpu.VMEM
        )
        for i, a in enumerate(args)
    ]
    many = isinstance(outs, list)
    vmem = pl.BlockSpec(memory_space=pltpu.VMEM)
    return pl.pallas_call(
        kernel,
        out_shape=outs,
        in_specs=specs,
        out_specs=[vmem] * len(outs) if many else vmem,
        scratch_shapes=list(scratch),
        input_output_aliases=alias,
        compiler_params=pltpu.CompilerParams(vmem_limit_bytes=room * 1024 * 1024),
    )(*args)


def shape(dims, kind=BF16):
    return jax.ShapeDtypeStruct(dims, kind)


def sort_matrix():
    table = np.zeros((BLOCK, BLOCK), np.float32)
    for a in range(2):
        for b in range(2):
            for q in range(4):
                for k in range(HALF):
                    table[q * 128 + a * 64 + 2 * k + b, (2 * a + b) * 128 + q * HALF + k] = 1
    return jnp.asarray(table, BF16)


def paired(values, axis, bit):
    count = lax.axis_size(axis)
    return lax.ppermute(values, axis, [(i, i ^ bit) for i in range(count)])


FIRST, SECOND = (7, 4, 2), (6, 5, 3)


def is_split():
    return lax.axis_size("tile") == 8 and lax.axis_size("chan") % 2 == 0


def spots_of():
    tiles = lax.axis_size("tile")
    if not is_split():
        return [[(slot, slot) for slot in range(tiles)]]
    pairs = list(zip(FIRST, SECOND))
    return [[(0, 0)]] + [[pair] for pair in pairs] + [[pair[::-1]] for pair in pairs]


def copies(block, half=None, beside=()):
    tiles, nc = lax.axis_size("tile"), lax.axis_size("chan")
    if not is_split():
        return [swap(jnp.broadcast_to(block, (tiles,) + block.shape[1:]))], beside
    got = []
    for slots in zip(FIRST, SECOND):
        perm = [
            (tile * nc + chan, (tile ^ slots[chan & 1]) * nc + chan)
            for tile in range(tiles)
            for chan in range(nc)
        ]
        got.append(lax.ppermute(block, ("tile", "chan"), perm))
    got.append(paired(half, "tile", 1))
    got, beside = lax.optimization_barrier((got, beside))
    return [block] + got + [paired(part, "chan", 1) for part in got], beside


def swap(values):
    return lax.all_to_all(values, "tile", split_axis=0, concat_axis=0)


def gathered(values, axis):
    slots = {0: values}
    bit = lax.axis_size(axis) // 2
    while bit:
        slots.update({slot ^ bit: paired(held, axis, bit) for slot, held in list(slots.items())})
        bit //= 2
    return [slots[slot] for slot in range(len(slots))]


def per_device(features, conv1_weight, down_weight, conv2_weight, up_weight, out_grad, adjacency):
    own = features.shape[0]
    tiles, nc = lax.axis_size("tile"), lax.axis_size("chan")
    scale = float((tiles * SIDE * SIDE) ** (-0.5))
    tile, chan = lax.axis_index("tile"), lax.axis_index("chan")
    where = jnp.stack([tile, chan, tile if is_split() else tile * 0, chan]).astype(jnp.int32)
    matrix = sort_matrix()
    half = nc // 2

    pack, rims, sorted_g, pack2 = call(
        sort_kernel,
        [
            shape((45, own, 128)),
            shape((1, 5, own, 128)),
            shape((own, 4 * CELLS)),
            shape((18, own, 128)),
        ],
        features,
        out_grad,
        conv1_weight,
        down_weight,
        conv2_weight,
        up_weight,
        far=range(6),
        room=60,
        scratch=[
            pltpu.VMEM((own, 4 * CELLS), BF16),
            pltpu.VMEM((own, 4 * CELLS), BF16),
            pltpu.VMEM((BLOCK, 2 * BLOCK), BF16),
            pltpu.SemaphoreType.DMA((6,)),
        ],
    )
    pack_far = paired(pack, "chan", half)
    if is_split():
        far, near = paired(rims, "tile", 4), paired(rims, "tile", 2)
        cross = paired(far, "tile", 2)
        pack_near, pair = call(
            stage_kernel, [shape(pack.shape), shape((2,) + rims.shape[1:])], pack, rims, far
        )
        beside = paired(pair, "tile", 1)
        cross, near, pack_near, pack2, adjacency = lax.optimization_barrier(
            (cross, near, pack_near, pack2, adjacency)
        )
        last = [paired(near, "tile", 1), paired(cross, "tile", 1)]
        all_rims = [pair, near, cross, beside] + last
        rim_spots = [[(slot, slot) for slot in group] for group in ((0, 4), (2,), (6,), (1, 5), (3,), (7,))]
    else:
        all_rims, rim_spots = copies(rims)[0], spots_of()
        pack_near = pack
    turns = (adjacency[:, :, 1] + jnp.array(side_turns, jnp.int32)) & 3
    codes = jnp.where(adjacency[:, :, 0] < 0, -1, adjacency[:, :, 0] * 4 + turns)
    ring = call(
        partial(pick_kernel, rim_spots),
        shape((5 + tiles, own, 128)),
        codes,
        where,
        *all_rims,
        scratch=[pltpu.VMEM((tiles + 1, 5, own, 128), BF16)],
    )
    pack_far, ring = lax.optimization_barrier((pack_far, ring))
    ring_far = paired(ring, "chan", half)

    def whole(near, far, held=None):
        return [near if held is None else held, paired(near, "chan", 1), far, paired(far, "chan", 1)]

    packs = whole(pack, pack_far, pack_near)
    x3, z1c, w1t, wdt = call(
        partial(fine_center_kernel, nc),
        [
            shape((4, PADDED, 384)),
            shape((4, CELLS, 128), F32),
            shape((1152, 128)),
            shape((512, 128)),
        ],
        where,
        *packs,
        scratch=[
            pltpu.VMEM((384, 384), BF16),
            pltpu.VMEM((128, 512), BF16),
            pltpu.VMEM((128, 4 * CELLS), BF16),
        ],
    )
    x3, ring_far, pack2 = lax.optimization_barrier((x3, ring_far, pack2))
    pack2_far, pack2_side = paired(pack2, "chan", half), paired(pack2, "chan", 1)
    rings = whole(ring, ring_far)
    act, slope2, act2, rims2, half2, ring_sorted = call(
        partial(fine_ring_kernel, nc),
        [
            shape((4, CELLS, 128)),
            shape((CELLS, 128), F32),
            shape((CELLS, 128)),
            shape((1, 256, 128)),
            shape((1, 128, 128)),
            shape((5, 128, 128), F32),
        ],
        where,
        z1c,
        w1t,
        wdt,
        *rings,
        scratch=[
            pltpu.VMEM((5, 128, 128), BF16),
            pltpu.VMEM((4, CELLS, 128), F32),
            pltpu.VMEM((CELLS, 128), F32),
        ],
    )
    rims2, half2, pack2_side = lax.optimization_barrier((rims2, half2, pack2_side))
    act1, slope1, x3 = call(
        own_fine_kernel,
        [shape((own, 4 * CELLS)), shape((own, 4 * CELLS), F32), shape((4, PADDED, 384))],
        conv1_weight,
        ring_sorted,
        x3,
        alias={2: 2},
    )
    all_rims2, (act1, slope1, x3, pack2_far) = copies(rims2, half2, (act1, slope1, x3, pack2_far))
    packs2 = [pack2, pack2_side, pack2_far, paired(pack2_far, "chan", 1)]
    rows = -(-23 * own // (16 * tiles)) * 16
    output, late = call(
        partial(level_kernel, nc, spots_of()),
        [shape((own, 4 * CELLS)), shape((rows * tiles, 128))],
        codes,
        where,
        act2,
        slope2,
        act,
        wdt,
        act1,
        slope1,
        sorted_g,
        x3,
        matrix,
        *packs2,
        *rings,
        *all_rims2,
        scratch=[
            pltpu.VMEM((384, 384), BF16),
            pltpu.VMEM((1152, 128), BF16),
            pltpu.VMEM((128, 128), BF16),
            pltpu.VMEM((128, CELLS), BF16),
            pltpu.VMEM((128, tiles * 128), BF16),
            pltpu.VMEM((tiles, 256, 128), BF16),
            pltpu.VMEM((34 * HALF, 128), F32),
            pltpu.VMEM((34 * HALF, 128), F32),
            pltpu.VMEM((CELLS + 4 * HALF, 128), BF16),
            pltpu.VMEM((34 * HALF, 384), F32),
            pltpu.VMEM((PADDED, 384), BF16),
            pltpu.VMEM((CELLS, 128), BF16),
            pltpu.VMEM((CELLS, 128), F32),
            pltpu.VMEM((128, 128), F32),
        ],
    )
    pieces = swap(late.reshape(tiles, rows, 128))
    total = call(partial(sum_kernel, scale), shape((rows, 128)), pieces)
    total = swap(jnp.broadcast_to(total[None], (tiles, rows, 128)))
    grads = call(
        unpack_kernel,
        [
            shape((9, own, 128), F32),
            shape((4, own, 128), F32),
            shape((9, own, 128), F32),
            shape((own, 128), F32),
        ],
        total.reshape(tiles * rows, 128),
    )
    return (output, *grads)


def solution(mesh):
    placed = (
        P("chan", "tile"),
        P(None, "chan", None),
        P(None, "chan", None),
        P(None, "chan", None),
        P("chan", None),
        P("chan", "tile"),
        P(),
    )
    return jax.shard_map(
        per_device,
        mesh=mesh,
        in_specs=placed,
        out_specs=(
            P("chan", "tile"),
            P(None, "chan", None),
            P(None, "chan", None),
            P(None, "chan", None),
            P("chan", None),
        ),
        check_vma=False,
    )
```

```python
from functools import partial

import jax
import jax.numpy as jnp
import numpy as np
from jax import lax
from jax.experimental import pallas as pl
from jax.experimental.pallas import tpu as pltpu
from jax.sharding import PartitionSpec as P

SIDE = 64
HALF = 32
CELLS = HALF * HALF
PADDED = 36 * HALF
BLOCK = 8 * SIDE
BF16 = jnp.bfloat16
F32 = jnp.float32
NT = (((1,), (1,)), ((), ()))
ROOT = float(np.sqrt(2.0 / np.pi))
CUBE = 0.044715
side_turns = (0, 1, 2, 3, 0, 2, 2, 0)


def mm(left, right):
    return jnp.dot(left, right, preferred_element_type=F32)


def mm_nt(left, right):
    return lax.dot_general(left, right, NT, preferred_element_type=F32)


def gelu(v):
    return 0.5 * v * (1.0 + jnp.tanh(ROOT * (v + CUBE * (v * v * v))))


def gelu_slope(v):
    square = v * v
    t = jnp.tanh(ROOT * (v + CUBE * (square * v)))
    return 0.5 * (1.0 + t) + (0.5 * ROOT) * v * (1.0 - t * t) * (1.0 + 3.0 * CUBE * square)


def gelu_and_slope(v):
    square = v * v
    t = jnp.tanh(ROOT * (v + CUBE * (square * v)))
    both = 0.5 * (1.0 + t)
    return v * both, both + (0.5 * ROOT) * v * (1.0 - t * t) * (1.0 + 3.0 * CUBE * square)


def iota(shape, dim):
    return lax.broadcasted_iota(jnp.int32, shape, dim)


def one_hot(mask):
    return jnp.where(mask, 1.0, 0.0).astype(BF16)


def flip32(rows):
    anti = one_hot(iota((HALF, HALF), 0) + iota((HALF, HALF), 1) == HALF - 1)
    return mm(anti, rows)


def own_rows(me, own, chans):
    return one_hot(iota((own, chans), 0) + me * own == iota((own, chans), 1))


def side_of(codes_ref, tile, side):
    code = codes_ref[tile, side]
    return jnp.maximum(code, 0) // 4, code & 3, code >= 0


def is_beside(codes_ref, tile, side, partner):
    code = codes_ref[tile, side]
    return (code >= partner * 4) & (code < partner * 4 + 4)


def rows_of(slot, base, own):
    return pl.multiple_of((slot ^ base) * own, own)


def place_conv(packs, base, start, dst_ref):
    own = packs[0].shape[1]
    for slot, pack in enumerate(packs):
        row = rows_of(slot, base, own)
        for a in range(3):
            for b in range(3):
                dst_ref[pl.ds(a * 128 + row, own), b * 128 : (b + 1) * 128] = pack[start + 3 * a + b]


def spread_columns(dst, left, right, center, north, south, west, east, corners):
    rows = 34 * HALF
    middle = jnp.concatenate([north, center, south], axis=0)
    north_east, south_east, south_west, north_west = corners
    left[...] = pltpu.roll(middle, 1, 0)
    right[...] = pltpu.roll(middle, rows - 1, 0)
    left[pl.ds(HALF, HALF, stride=HALF), :] = west
    left[0:1, :] = north_west
    left[33 * HALF : 33 * HALF + 1, :] = south_west
    right[pl.ds(2 * HALF - 1, HALF, stride=HALF), :] = east
    right[HALF - 1 : HALF, :] = north_east
    right[rows - 1 : rows, :] = south_east
    dst[0:rows, 0:128] = left[...].astype(BF16)
    dst[0:rows, 128:256] = middle.astype(BF16)
    dst[0:rows, 256:384] = right[...].astype(BF16)
    dst[rows:PADDED, :] = jnp.zeros((PADDED - rows, 384), BF16)


def fetch(pairs, sems):
    started = [
        pltpu.make_async_copy(source, target, sems.at[index])
        for index, (source, target) in enumerate(pairs)
    ]
    for copy in started:
        copy.start()
    return started


def stacked(ref):
    return jnp.concatenate([ref[:, jb * BLOCK : (jb + 1) * BLOCK] for jb in range(8)], axis=0)


def fill_table(m_ref):
    lane = iota((16, BLOCK), 1)
    quarter, k = (lane >> 5) & 3, lane & 31
    sort_place = quarter * 128 + (lane >> 8) * 64 + 2 * k + ((lane >> 7) & 1)
    turn, x, y, back = lane >> 7, (lane >> 6) & 1, (lane >> 5) & 1, 31 - k
    rim_place = jnp.where(
        turn == 0,
        384 + x * 64 + 2 * k + y,
        jnp.where(
            turn == 1,
            (k & 3) * 128 + y * 64 + 1 - x,
            jnp.where(
                turn == 2,
                (1 - x) * 64 + 2 * back + 1 - y,
                (back & 3) * 128 + (1 - y) * 64 + 62 + x,
            ),
        ),
    )
    place = jnp.concatenate([sort_place, rim_place], axis=1)
    row = iota((16, 2 * BLOCK), 0)
    for group in range(BLOCK // 16):
        m_ref[group * 16 : (group + 1) * 16, :] = one_hot(row + group * 16 == place)


def sort_kernel(
    f_hbm, g_hbm, w1_hbm, wd_hbm, w2_hbm, up_hbm, pack_ref, rims_ref, sorted_ref, pack2_ref, f_ref, g_ref, m_ref, sems
):
    count = f_ref.shape[0]
    started = fetch(
        [
            (f_hbm, f_ref),
            (g_hbm, g_ref),
            (w1_hbm, pack_ref.at[32:41]),
            (wd_hbm, pack_ref.at[41:45]),
            (w2_hbm, pack2_ref.at[8:17]),
            (up_hbm, pack2_ref.at[17]),
        ],
        sems,
    )
    lane = iota((count, BLOCK), 1)
    turn, slot = lane // 128, lane % HALF
    wanted = jnp.where(
        turn == 0, 7, jnp.where(turn == 1, slot // 4, jnp.where(turn == 2, 0, (HALF - 1 - slot) // 4))
    )
    spot, cell = iota((BLOCK, 128), 0), iota((BLOCK, 128), 1)
    pooling = one_hot((spot // 128 == cell // HALF) & (spot % HALF == cell % HALF))

    def moved(ref):
        stack = jnp.concatenate([ref[:, jb * BLOCK : (jb + 1) * BLOCK] for jb in range(8)], axis=0)
        both = mm(stack, m_ref[...])
        parts = [both[jb * count : (jb + 1) * count] for jb in range(8)]
        rims = jnp.zeros((count, BLOCK), F32)
        for jb in range(8):
            rims = rims + jnp.where(wanted == jb, parts[jb][:, BLOCK:], 0.0)
        return [[part[:, ph * 128 : (ph + 1) * 128] for ph in range(4)] for part in parts], rims.astype(BF16)

    fill_table(m_ref)
    started[0].wait()
    pieces, rims = moved(f_ref)
    for turn_index in range(4):
        rims_ref[0, turn_index] = rims[:, turn_index * 128 : (turn_index + 1) * 128]
    for jb in range(8):
        for ph in range(4):
            pack_ref[ph * 8 + jb] = pieces[jb][ph].astype(BF16)
    started[1].wait()
    pieces, rims = moved(g_ref)
    rims_ref[0, 4] = mm(rims, pooling).astype(BF16)
    for jb in range(8):
        for ph in range(4):
            sorted_ref[:, ph * CELLS + jb * 128 : ph * CELLS + (jb + 1) * 128] = pieces[jb][ph].astype(BF16)
        pack2_ref[jb] = ((pieces[jb][0] + pieces[jb][1]) + (pieces[jb][2] + pieces[jb][3])).astype(BF16)
    for copy in started[2:]:
        copy.wait()


def hold(refs, spots, core, put):
    for ref, slots in zip(refs, spots):
        for index, (even, odd) in enumerate(slots):
            slot = even if even == odd else jnp.where(core == 0, even, odd)
            put(slot, ref, index)


def pick_kernel(spots, codes_ref, where_ref, *refs):
    *rims, out_ref, held = refs
    tile, base, core = where_ref[0], where_ref[2], where_ref[1] & 1

    def put(slot, ref, index):
        held[slot] = ref[index]

    hold(rims, spots, core, put)
    lane = iota(out_ref.shape[1:], 1) % HALF
    corners = jnp.zeros(lane.shape, F32)
    for side in range(8):
        partner, turn, there = side_of(codes_ref, tile, side)
        picked = jnp.where(there, held[partner ^ base, turn].astype(F32), 0.0)
        if side < 4:
            out_ref[side] = picked.astype(BF16)
        else:
            shift, spot = ((0, 0), (0, HALF - 1), (1, 1), (127, HALF - 2))[side - 4]
            moved = pltpu.roll(picked, shift, 1) if shift else picked
            corners = corners + jnp.where(lane == spot, moved, 0.0)
    out_ref[4] = corners.astype(BF16)
    for other in range(out_ref.shape[0] - 5):
        out_ref[5 + other] = held[other ^ base, 4]


def stage_kernel(pack_ref, rims_ref, far_ref, near_ref, pair_ref):
    near_ref[...] = pack_ref[...]
    pair_ref[0:1] = rims_ref[...]
    pair_ref[1:2] = far_ref[...]


def fine_center_kernel(nc, where_ref, *refs):
    packs, refs = refs[:nc], refs[nc:]
    x3_ref, z1_ref, w1t, wdt, w1s, wds, f_all = refs
    base = where_ref[3]
    own = packs[0].shape[1]
    for slot, pack in enumerate(packs):
        row = rows_of(slot, base, own)
        for block in range(32):
            f_all[pl.ds(row, own), block * 128 : (block + 1) * 128] = pack[block]
        for a in range(3):
            for b in range(3):
                w1s[pl.ds(a * 128 + row, own), b * 128 : (b + 1) * 128] = pack[32 + 3 * a + b]
        for ph in range(4):
            wds[pl.ds(row, own), ph * 128 : (ph + 1) * 128] = pack[41 + ph]
    for a in range(3):
        w1t[a * 384 : (a + 1) * 384, :] = jnp.transpose(w1s[a * 128 : (a + 1) * 128, :])
    wdt[...] = jnp.transpose(wds[...])
    column = iota((CELLS, 128), 0) % HALF
    for ph in range(4):
        center = jnp.transpose(f_all[:, ph * CELLS : (ph + 1) * CELLS]).astype(F32)
        left = jnp.where(column == 0, 0.0, pltpu.roll(center, 1, 0))
        right = jnp.where(column == HALF - 1, 0.0, pltpu.roll(center, CELLS - 1, 0))
        x3_ref[ph, 0:HALF, :] = jnp.zeros((HALF, 384), BF16)
        x3_ref[ph, HALF : HALF + CELLS, 0:128] = left.astype(BF16)
        x3_ref[ph, HALF : HALF + CELLS, 128:256] = center.astype(BF16)
        x3_ref[ph, HALF : HALF + CELLS, 256:384] = right.astype(BF16)
        x3_ref[ph, HALF + CELLS : PADDED, :] = jnp.zeros((PADDED - HALF - CELLS, 384), BF16)
        for start in range(0, CELLS, 256):
            window = jnp.concatenate(
                [x3_ref[ph, start + a * HALF : start + a * HALF + 256, :] for a in range(3)], axis=1
            )
            z1_ref[ph, start : start + 256, :] = mm(window, w1t[...])


def ring_pieces(ring, ph):
    a, b = ph // 2, ph % 2
    near, far = ph * HALF, ((1 - a) * 2 + (1 - b)) * HALF
    east, west = ((1 - b) * 2 + a) * HALF, (b * 2 + (1 - a)) * HALF
    return (
        ring[0, near : near + HALF],
        ring[1, east : east + HALF],
        ring[2, far : far + HALF],
        ring[3, west : west + HALF],
        (
            ring[4, near : near + 1],
            ring[4, far + HALF - 1 : far + HALF],
            ring[4, far + 1 : far + 2],
            ring[4, near + HALF - 2 : near + HALF - 1],
        ),
    )


def windows_of(row, first, final):
    place = iota((HALF, 128), 0)
    return jnp.concatenate(
        [
            jnp.where(place == 0, first, pltpu.roll(row, 1, 0)),
            row,
            jnp.where(place == HALF - 1, final, pltpu.roll(row, HALF - 1, 0)),
        ],
        axis=1,
    ).astype(BF16)


def fine_ring_kernel(nc, where_ref, z1_in, w1t, wdt, *refs):
    rings, refs = refs[:nc], refs[nc:]
    act_ref, slope2_ref, act2_ref, rims_ref, half_ref, ring, ring_all, z1, wide = refs
    base = where_ref[3]
    own = rings[0].shape[1]
    for slot in range(nc):
        row = rows_of(slot, base, own)
        for side in range(5):
            ring_all[side, pl.ds(row, own), :] = rings[slot][side]
    row, col = iota((128, 128), 0), iota((128, 128), 1)
    same = one_hot(row == col)
    turned = one_hot((row // HALF == col // HALF) & (row % HALF + col % HALF == HALF - 1))
    for side in range(5):
        ring[side] = mm_nt(turned if side in (2, 3) else same, ring_all[side])
    z1[...] = z1_in[...]
    pieces = [ring_pieces(ring, ph) for ph in range(4)]

    def owed(rows, weights):
        return mm(jnp.concatenate(rows, axis=0), weights)

    def column(tap):
        return jnp.concatenate(
            [w1t[a * 384 + tap * 128 : a * 384 + (tap + 1) * 128, :] for a in range(3)], axis=0
        )

    north = owed([windows_of(p[0], p[4][3], p[4][0]) for p in pieces], w1t[0:384, :])
    south = owed([windows_of(p[2], p[4][2], p[4][1]) for p in pieces], w1t[768:1152, :])
    west = owed([windows_of(p[3], 0.0, 0.0) for p in pieces], column(0))
    east = owed([windows_of(p[1], 0.0, 0.0) for p in pieces], column(2))
    first = pl.ds(0, HALF, stride=HALF)
    last = pl.ds(HALF - 1, HALF, stride=HALF)
    for ph in range(4):
        rows = slice(ph * HALF, (ph + 1) * HALF)
        z1[ph, 0:HALF, :] += north[rows]
        z1[ph, CELLS - HALF : CELLS, :] += south[rows]
        z1[ph, first, :] = z1[ph, first, :] + west[rows]
        z1[ph, last, :] = z1[ph, last, :] + east[rows]

    def chunk(index, carry):
        start = index * 256
        acts = []
        for ph in range(4):
            act = gelu(z1[ph, pl.ds(start, 256), :]).astype(BF16)
            act_ref[ph, pl.ds(start, 256), :] = act
            acts.append(act)
        z2 = mm(jnp.concatenate(acts, axis=1), wdt[...])
        value, slope = gelu_and_slope(z2)
        slope2_ref[pl.ds(start, 256), :] = slope
        act2 = value.astype(BF16)
        act2_ref[pl.ds(start, 256), :] = act2
        wide[pl.ds(start, 256), :] = act2.astype(F32)
        return carry

    lax.fori_loop(0, 4, chunk, 0)
    for deep in range(2):
        start = CELLS - (deep + 1) * HALF
        rims_ref[0, deep * 128 : deep * 128 + 32, :] = act2_ref[start : start + HALF, :]
        rims_ref[0, deep * 128 + 32 : deep * 128 + 64, :] = wide[
            pl.ds(deep, HALF, stride=HALF), :
        ].astype(BF16)
        rims_ref[0, deep * 128 + 64 : deep * 128 + 96, :] = flip32(
            act2_ref[deep * HALF : (deep + 1) * HALF, :]
        ).astype(BF16)
        rims_ref[0, deep * 128 + 96 : deep * 128 + 128, :] = flip32(
            wide[pl.ds(HALF - 1 - deep, HALF, stride=HALF), :].astype(BF16)
        ).astype(BF16)
    half_ref[0] = rims_ref[0, pl.ds(pl.multiple_of((where_ref[1] & 1) * 128, 128), 128), :]


def own_fine_kernel(w1_ref, ring, x3_in, act_ref, slope_ref, x3_ref):
    own = w1_ref.shape[1]
    row, col = iota((CELLS, HALF), 0), iota((CELLS, HALF), 1)
    at_first, at_last = one_hot(row == col * HALF), one_hot(row == col * HALF + HALF - 1)
    inner = slice(HALF, HALF + CELLS)
    stack = jnp.concatenate(
        [
            jnp.concatenate([w1_ref[3 * a + b] for b in range(3)], axis=1)
            for a in range(3)
        ],
        axis=0,
    )
    for ph in range(4):
        north, east, south, west, corners = ring_pieces(ring, ph)
        x3_ref[ph, inner, 128:256] = x3_in[ph, inner, 128:256]
        x3_ref[ph, 2 * HALF + CELLS : PADDED, :] = jnp.zeros((PADDED - 2 * HALF - CELLS, 384), BF16)
        x3_ref[ph, 0:HALF, :] = windows_of(north, corners[3], corners[0])
        x3_ref[ph, HALF + CELLS : 2 * HALF + CELLS, :] = windows_of(south, corners[2], corners[1])
        x3_ref[ph, inner, 0:128] = x3_in[ph, inner, 0:128] + mm(at_first, west.astype(BF16)).astype(BF16)
        x3_ref[ph, inner, 256:384] = x3_in[ph, inner, 256:384] + mm(at_last, east.astype(BF16)).astype(
            BF16
        )
        terms = mm_nt(stack, x3_ref[ph])
        total = terms[0:own, 0:CELLS]
        for a in range(1, 3):
            moved = pltpu.roll(terms[a * own : (a + 1) * own], PADDED - a * HALF, 1)
            total = total + moved[:, 0:CELLS]
        value, slope = gelu_and_slope(total)
        act_ref[:, ph * CELLS : (ph + 1) * CELLS] = value.astype(BF16)
        slope_ref[:, ph * CELLS : (ph + 1) * CELLS] = slope


def turned_tap(turn, a, b):
    return ((a, b), (b, 2 - a), (2 - a, 2 - b), (2 - b, a))[turn]


CORNER_ENDS = {4: 0, 5: HALF - 1, 6: 0, 7: HALF - 1}
LOW_LEFT = (4, 5, 6, 7)
LOW_RIGHT = (7, 4, 5, 6)


def is_owing(codes_ref, other, side, tile):
    owing = is_beside(codes_ref, other, side, tile)
    if side in (0, 2):
        owing = owing | is_beside(codes_ref, other, LOW_LEFT[side], tile)
        owing = owing | is_beside(codes_ref, other, LOW_RIGHT[side], tile)
    return owing


def strip_of(side, other, codes_ref, base, rims_all):
    turn = (side + 2) % 4

    def rim(partner, slot):
        return rims_all[partner ^ base, pl.ds(pl.multiple_of(slot * HALF, HALF), HALF), :]

    partner, slot, _ = side_of(codes_ref, other, side)
    left_partner, left_slot, _ = side_of(codes_ref, other, (side + 1) % 4)
    right_partner, right_slot, _ = side_of(codes_ref, other, (side + 3) % 4)
    ends = []
    for corner in (LOW_LEFT[side], LOW_RIGHT[side]):
        corner_partner, corner_slot, there = side_of(codes_ref, other, corner)
        spot = CORNER_ENDS[corner]
        row = rim(corner_partner, corner_slot).astype(F32)[spot : spot + 1]
        ends.append(jnp.where(there, row, 0.0))
    left, right = rim(left_partner, left_slot).astype(F32), rim(right_partner, right_slot).astype(F32)
    last = HALF - 1
    here = rims_all[other ^ base, turn * HALF : (turn + 1) * HALF, :].astype(F32)
    above = rims_all[other ^ base, 128 + turn * HALF : 128 + (turn + 1) * HALF, :].astype(F32)
    below = flip32(rim(partner, slot))
    place = iota((HALF, 128), 0)
    by_tap = {}
    for a, (row, first, final) in enumerate(
        (
            (above, left[1:2], right[last - 1 : last]),
            (here, left[0:1], right[last : last + 1]),
            (below, ends[0], ends[1]),
        )
    ):
        by_tap[turned_tap(turn, a, 0)] = jnp.where(place == 0, first, pltpu.roll(row, 1, 0))
        by_tap[turned_tap(turn, a, 1)] = row
        by_tap[turned_tap(turn, a, 2)] = jnp.where(place == last, final, pltpu.roll(row, last, 0))
    return jnp.concatenate([by_tap[a, b] for a in range(3) for b in range(3)], axis=1).astype(BF16)


def back_from(others, codes_ref, tile, base, rims_all, prims, w2s, w2t, ups, back):
    last = HALF - 1
    place = iota((HALF, 128), 0)
    z3 = mm(
        jnp.concatenate([strip_of(side, others[side], codes_ref, base, rims_all) for side in range(4)], axis=0),
        w2t[...],
    )
    pooled = []
    for side in range(4):
        turn = (side + 2) % 4
        select = one_hot(iota((HALF, 128), 0) + turn * HALF == iota((HALF, 128), 1))
        cells = prims[:, pl.ds(pl.multiple_of(others[side] * 128, 128), 128)]
        pooled.append(mm_nt(select, cells))
    g3 = gelu_slope(z3) * mm(jnp.concatenate(pooled, axis=0).astype(BF16), ups[...])
    row, col = iota((128, 128), 0), iota((128, 128), 1)
    turned = one_hot((row // HALF == col // HALF) & (row % HALF + col % HALF == HALF - 1))
    g3 = mm(turned, g3.astype(BF16)).astype(BF16)
    for side in range(4):
        other = others[side]
        owed = []
        for b in range(3):
            r, c = turned_tap((side + 2) % 4, 2, b)
            owed.append(
                mm(
                    g3[side * HALF : (side + 1) * HALF],
                    w2s[r * 128 : (r + 1) * 128, c * 128 : (c + 1) * 128],
                )
            )
        total = (
            jnp.where(place == 0, 0.0, pltpu.roll(owed[0], 1, 0))
            + owed[1]
            + jnp.where(place == last, 0.0, pltpu.roll(owed[2], last, 0))
        )
        _, slot, _ = side_of(codes_ref, other, side)
        counts = is_beside(codes_ref, other, side, tile) & (others[side + 4] == 1)
        back[pl.ds(pl.multiple_of(slot * HALF, HALF), HALF), :] += jnp.where(counts, total, 0.0)
        if side in (0, 2):
            for corner, line in (
                (LOW_LEFT[side], owed[0][last : last + 1]),
                (LOW_RIGHT[side], owed[2][0:1]),
            ):
                _, corner_slot, _ = side_of(codes_ref, other, corner)
                counts = is_beside(codes_ref, other, corner, tile) & (others[side + 4] == 1)

                @pl.when(counts)
                def _():
                    back[pl.ds(pl.multiple_of(corner_slot * HALF, HALF), HALF), :] += jnp.where(
                        place == CORNER_ENDS[corner], line, 0.0
                    )


def own_taps(grad_ref, start, grads, own):
    for a in range(3):
        for b in range(3):
            row = (start + 3 * a + b) * own
            grad_ref[row : row + own, :] = grads[
                a * own : (a + 1) * own, b * 128 : (b + 1) * 128
            ].astype(BF16)


def shifted_stack(values):
    wide = jnp.concatenate([values, jnp.zeros((values.shape[0], PADDED - CELLS), F32)], axis=1)
    return jnp.concatenate(
        [(pltpu.roll(wide, a * HALF, 1) if a else wide).astype(BF16) for a in range(3)], axis=0
    )


def level_kernel(
    nc,
    spots,
    codes_ref,
    where_ref,
    act2_ref,
    slope2_ref,
    act_ref,
    wdt_ref,
    own_ref,
    slope1_ref,
    og_ref,
    x3_ref,
    m_ref,
    *refs,
):
    packs, mores, refs = refs[:nc], refs[nc : 2 * nc], refs[2 * nc :]
    *rims, out_ref, grad_ref, w2s, w2t, ups, pooled_all, prims, rims_all, left, right, g3pad, sums, a3, coarse, field, back = refs
    tile, me, tile_base, base = where_ref[0], where_ref[1], where_ref[2], where_ref[3]
    own = packs[0].shape[1]
    place_conv(packs, base, 8, w2s)
    for slot in range(nc):
        row = rows_of(slot, base, own)
        ups[pl.ds(row, own), :] = packs[slot][17]
        for jb in range(8):
            pooled_all[pl.ds(row, own), jb * 128 : (jb + 1) * 128] = packs[slot][jb]
        for other in range(mores[slot].shape[0] - 5):
            prims[pl.ds(row, own), other * 128 : (other + 1) * 128] = mores[slot][5 + other]

    def put(slot, ref, index):
        rims_all[slot] = ref[index]

    if len(rims) == 9:
        core = me & 1
        rims_all[1, pl.ds(pl.multiple_of(core * 128, 128), 128), :] = rims[4][0]
        rims_all[1, pl.ds(pl.multiple_of(128 - core * 128, 128), 128), :] = rims[8][0]
        rims = rims[:4] + rims[5:8]
    hold(rims, spots, me & 1, put)
    got = []
    for side in range(8):
        partner, turn, there = side_of(codes_ref, tile, side)
        piece = rims_all[
            partner ^ tile_base, pl.ds(pl.multiple_of(turn * HALF, HALF), HALF), :
        ].astype(F32)
        got.append(jnp.where(there, piece, 0.0))
    spread_columns(
        a3,
        left,
        right,
        act2_ref[...].astype(F32),
        got[0],
        flip32(got[2].astype(BF16)),
        flip32(got[3].astype(BF16)),
        got[1],
        (got[4][0:1], got[5][HALF - 1 : HALF], got[6][0:1], got[7][HALF - 1 : HALF]),
    )
    for a in range(3):
        w2t[a * 384 : (a + 1) * 384, :] = jnp.transpose(w2s[a * 128 : (a + 1) * 128, :])
    pooled = jnp.transpose(pooled_all[...])
    g3pad[0 : 2 * HALF, :] = jnp.zeros((2 * HALF, 128), BF16)
    g3pad[CELLS + 2 * HALF : CELLS + 4 * HALF, :] = jnp.zeros((2 * HALF, 128), BF16)
    for index in range(4):
        start = index * 256
        z3 = mm(
            jnp.concatenate(
                [a3[start + a * HALF : start + a * HALF + 256, :] for a in range(3)], axis=1
            ),
            w2t[...],
        )
        value, slope = gelu_and_slope(z3)
        coarse[start : start + 256, :] = value.astype(BF16)
        back_up = mm(pooled[start : start + 256, :], ups[...])
        g3pad[2 * HALF + start : 2 * HALF + start + 256, :] = (slope * back_up).astype(BF16)
    step = 34 * HALF // 4
    for index in range(4):
        start = index * step
        lhs = jnp.concatenate(
            [g3pad[start + (2 - a) * HALF : start + (2 - a) * HALF + step, :] for a in range(3)], axis=1
        )
        sums[start : start + step, :] = mm(lhs, w2s[...])
    rows = 34 * HALF
    column = iota((rows, 128), 0) % HALF
    middle = (
        sums[:, 128:256]
        + jnp.where(column == HALF - 1, 0.0, pltpu.roll(sums[:, 0:128], rows - 1, 0))
        + jnp.where(column == 0, 0.0, pltpu.roll(sums[:, 256:384], 1, 0))
    )
    field[...] = middle[HALF : HALF + CELLS, :]

    back[...] = jnp.zeros_like(back)
    tiles = codes_ref.shape[0]

    def following(before):
        found = []
        for side in range(4):
            spot = jnp.int32(tiles)
            for other in reversed(range(tiles)):
                take = is_owing(codes_ref, other, side, tile) & (other > before[side])
                spot = jnp.where(take, other, spot)
            found.append(spot)
        return tuple(found)

    def left_over(found):
        return (
            (found[0] < tiles) | (found[1] < tiles) | (found[2] < tiles) | (found[3] < tiles)
        )

    def visit(found):
        others = [jnp.minimum(spot, tiles - 1) for spot in found]
        others = others + [jnp.where(spot < tiles, 1, 0) for spot in found]
        back_from(others, codes_ref, tile, tile_base, rims_all, prims, w2s, w2t, ups, back)
        return following(found)

    lax.while_loop(left_over, visit, following((jnp.int32(-1),) * 4))
    anti = jnp.where(iota((HALF, HALF), 0) + iota((HALF, HALF), 1) == HALF - 1, 1.0, 0.0)

    def flip(values):
        return lax.dot_general(
            anti,
            values,
            (((1,), (0,)), ((), ())),
            preferred_element_type=F32,
            precision=lax.Precision.HIGHEST,
        )

    field[CELLS - HALF : CELLS, :] += back[0:32, :]
    field[0:HALF, :] += flip(back[64:96, :])
    first = pl.ds(0, HALF, stride=HALF)
    last = pl.ds(HALF - 1, HALF, stride=HALF)
    field[first, :] = field[first, :] + back[32:64, :]
    field[last, :] = field[last, :] + flip(back[96:128, :])

    g2 = (slope2_ref[...] * field[...]).astype(BF16)
    pick = own_rows(me, own, 128)
    g2_turned = mm_nt(one_hot(iota((128, 128), 0) == iota((128, 128), 1)), g2).astype(BF16)
    g2_own = mm_nt(pick, g2).astype(BF16)
    grads = jnp.zeros((3 * own, 384), F32)
    for ph in range(4):
        grad_ref[(9 + ph) * own : (10 + ph) * own, :] = mm(g2_own, act_ref[ph]).astype(BF16)
        turned = wdt_ref[pl.ds(pl.multiple_of(ph * 128 + me * own, own), own), :]
        cells = slice(ph * CELLS, (ph + 1) * CELLS)
        g1 = slope1_ref[:, cells] * (og_ref[:, cells].astype(F32) + mm(turned, g2_turned))
        grads = grads + mm(shifted_stack(g1), x3_ref[ph])
    own_taps(grad_ref, 0, grads, own)
    g3 = mm_nt(pick, g3pad[2 * HALF : 2 * HALF + CELLS, :])
    own_taps(grad_ref, 13, mm(shifted_stack(g3), a3[...]), own)
    own_spot = pl.ds(pl.multiple_of(me * own, own), own)
    grad_ref[22 * own : 23 * own, :] = mm(pooled_all[own_spot, :], coarse[...]).astype(BF16)
    if grad_ref.shape[0] > 23 * own:
        grad_ref[23 * own :, :] = jnp.zeros((grad_ref.shape[0] - 23 * own, 128), BF16)

    lifted = mm_nt(ups[own_spot, :], coarse[...])
    total = [
        own_ref[:, ph * CELLS : (ph + 1) * CELLS].astype(F32) + lifted for ph in range(4)
    ]
    stack = jnp.concatenate(
        [
            jnp.concatenate([total[ph][:, jb * 128 : (jb + 1) * 128] for ph in range(4)], axis=1)
            for jb in range(8)
        ],
        axis=0,
    ).astype(BF16)
    natural = mm_nt(stack, m_ref[...]).astype(BF16)
    for jb in range(8):
        out_ref[:, jb * BLOCK : (jb + 1) * BLOCK] = natural[jb * own : (jb + 1) * own]


def sum_kernel(scale, in_ref, out_ref):
    total = in_ref[0].astype(F32)
    for slot in range(1, in_ref.shape[0]):
        total = total + in_ref[slot].astype(F32)
    out_ref[...] = (total * scale).astype(BF16)


def unpack_kernel(flat, one_ref, down_ref, two_ref, up_ref):
    own = up_ref.shape[0]
    for tap in range(9):
        one_ref[tap] = flat[tap * own : (tap + 1) * own, :].astype(F32)
        two_ref[tap] = flat[(13 + tap) * own : (14 + tap) * own, :].astype(F32)
    for ph in range(4):
        down_ref[ph] = flat[(9 + ph) * own : (10 + ph) * own, :].astype(F32)
    up_ref[...] = flat[22 * own : 23 * own, :].astype(F32)


def call(kernel, outs, *args, scratch=(), far=(), room=24, alias={}):
    specs = [
        pl.BlockSpec(
            memory_space=pltpu.SMEM if a.dtype == jnp.int32 else pltpu.HBM if i in far else pltpu.VMEM
        )
        for i, a in enumerate(args)
    ]
    many = isinstance(outs, list)
    vmem = pl.BlockSpec(memory_space=pltpu.VMEM)
    return pl.pallas_call(
        kernel,
        out_shape=outs,
        in_specs=specs,
        out_specs=[vmem] * len(outs) if many else vmem,
        scratch_shapes=list(scratch),
        input_output_aliases=alias,
        compiler_params=pltpu.CompilerParams(vmem_limit_bytes=room * 1024 * 1024),
    )(*args)


def shape(dims, kind=BF16):
    return jax.ShapeDtypeStruct(dims, kind)


def sort_matrix():
    table = np.zeros((BLOCK, BLOCK), np.float32)
    for a in range(2):
        for b in range(2):
            for q in range(4):
                for k in range(HALF):
                    table[q * 128 + a * 64 + 2 * k + b, (2 * a + b) * 128 + q * HALF + k] = 1
    return jnp.asarray(table, BF16)


def paired(values, axis, bit):
    count = lax.axis_size(axis)
    return lax.ppermute(values, axis, [(i, i ^ bit) for i in range(count)])


FIRST, SECOND = (2, 4, 7), (3, 5, 6)


def is_split():
    return lax.axis_size("tile") == 8 and lax.axis_size("chan") % 2 == 0


def spots_of():
    tiles = lax.axis_size("tile")
    if not is_split():
        return [[(slot, slot) for slot in range(tiles)]]
    pairs = list(zip(FIRST, SECOND))
    return [[(0, 0)]] + [[pair] for pair in pairs] + [[pair[::-1]] for pair in pairs]


def copies(block, half=None, beside=()):
    tiles, nc = lax.axis_size("tile"), lax.axis_size("chan")
    if not is_split():
        return [swap(jnp.broadcast_to(block, (tiles,) + block.shape[1:]))], beside
    got = []
    for slots in zip(FIRST, SECOND):
        perm = [
            (tile * nc + chan, (tile ^ slots[chan & 1]) * nc + chan)
            for tile in range(tiles)
            for chan in range(nc)
        ]
        got.append(lax.ppermute(block, ("tile", "chan"), perm))
    got.append(paired(half, "tile", 1))
    got, beside = lax.optimization_barrier((got, beside))
    return [block] + got + [paired(part, "chan", 1) for part in got], beside


def swap(values):
    return lax.all_to_all(values, "tile", split_axis=0, concat_axis=0)


def gathered(values, axis):
    slots = {0: values}
    bit = lax.axis_size(axis) // 2
    while bit:
        slots.update({slot ^ bit: paired(held, axis, bit) for slot, held in list(slots.items())})
        bit //= 2
    return [slots[slot] for slot in range(len(slots))]


def per_device(features, conv1_weight, down_weight, conv2_weight, up_weight, out_grad, adjacency):
    own = features.shape[0]
    tiles, nc = lax.axis_size("tile"), lax.axis_size("chan")
    scale = float((tiles * SIDE * SIDE) ** (-0.5))
    tile, chan = lax.axis_index("tile"), lax.axis_index("chan")
    where = jnp.stack([tile, chan, tile if is_split() else tile * 0, chan]).astype(jnp.int32)
    matrix = sort_matrix()
    half = nc // 2

    pack, rims, sorted_g, pack2 = call(
        sort_kernel,
        [
            shape((45, own, 128)),
            shape((1, 5, own, 128)),
            shape((own, 4 * CELLS)),
            shape((18, own, 128)),
        ],
        features,
        out_grad,
        conv1_weight,
        down_weight,
        conv2_weight,
        up_weight,
        far=range(6),
        room=60,
        scratch=[
            pltpu.VMEM((own, 4 * CELLS), BF16),
            pltpu.VMEM((own, 4 * CELLS), BF16),
            pltpu.VMEM((BLOCK, 2 * BLOCK), BF16),
            pltpu.SemaphoreType.DMA((6,)),
        ],
    )
    pack_far = paired(pack, "chan", half)
    if is_split():
        far, near = paired(rims, "tile", 4), paired(rims, "tile", 2)
        cross = paired(far, "tile", 2)
        pack_near, pair = call(
            stage_kernel, [shape(pack.shape), shape((2,) + rims.shape[1:])], pack, rims, far
        )
        beside = paired(pair, "tile", 1)
        cross, near, pack_near, pack2, adjacency = lax.optimization_barrier(
            (cross, near, pack_near, pack2, adjacency)
        )
        last = [paired(near, "tile", 1), paired(cross, "tile", 1)]
        all_rims = [pair, near, cross, beside] + last
        rim_spots = [[(slot, slot) for slot in group] for group in ((0, 4), (2,), (6,), (1, 5), (3,), (7,))]
    else:
        all_rims, rim_spots = copies(rims)[0], spots_of()
        pack_near = pack
    turns = (adjacency[:, :, 1] + jnp.array(side_turns, jnp.int32)) & 3
    codes = jnp.where(adjacency[:, :, 0] < 0, -1, adjacency[:, :, 0] * 4 + turns)
    ring = call(
        partial(pick_kernel, rim_spots),
        shape((5 + tiles, own, 128)),
        codes,
        where,
        *all_rims,
        scratch=[pltpu.VMEM((tiles + 1, 5, own, 128), BF16)],
    )
    pack_far, ring = lax.optimization_barrier((pack_far, ring))
    ring_far = paired(ring, "chan", half)

    def whole(near, far, held=None):
        return [near if held is None else held, paired(near, "chan", 1), far, paired(far, "chan", 1)]

    packs = whole(pack, pack_far, pack_near)
    x3, z1c, w1t, wdt = call(
        partial(fine_center_kernel, nc),
        [
            shape((4, PADDED, 384)),
            shape((4, CELLS, 128), F32),
            shape((1152, 128)),
            shape((512, 128)),
        ],
        where,
        *packs,
        scratch=[
            pltpu.VMEM((384, 384), BF16),
            pltpu.VMEM((128, 512), BF16),
            pltpu.VMEM((128, 4 * CELLS), BF16),
        ],
    )
    x3, ring_far, pack2 = lax.optimization_barrier((x3, ring_far, pack2))
    pack2_far, pack2_side = paired(pack2, "chan", half), paired(pack2, "chan", 1)
    rings = whole(ring, ring_far)
    act, slope2, act2, rims2, half2, ring_sorted = call(
        partial(fine_ring_kernel, nc),
        [
            shape((4, CELLS, 128)),
            shape((CELLS, 128), F32),
            shape((CELLS, 128)),
            shape((1, 256, 128)),
            shape((1, 128, 128)),
            shape((5, 128, 128), F32),
        ],
        where,
        z1c,
        w1t,
        wdt,
        *rings,
        scratch=[
            pltpu.VMEM((5, 128, 128), BF16),
            pltpu.VMEM((4, CELLS, 128), F32),
            pltpu.VMEM((CELLS, 128), F32),
        ],
    )
    rims2, half2, pack2_side = lax.optimization_barrier((rims2, half2, pack2_side))
    act1, slope1, x3 = call(
        own_fine_kernel,
        [shape((own, 4 * CELLS)), shape((own, 4 * CELLS), F32), shape((4, PADDED, 384))],
        conv1_weight,
        ring_sorted,
        x3,
        alias={2: 2},
    )
    all_rims2, (act1, slope1, x3, pack2_far) = copies(rims2, half2, (act1, slope1, x3, pack2_far))
    packs2 = [pack2, pack2_side, pack2_far, paired(pack2_far, "chan", 1)]
    rows = -(-23 * own // (16 * tiles)) * 16
    output, late = call(
        partial(level_kernel, nc, spots_of()),
        [shape((own, 4 * CELLS)), shape((rows * tiles, 128))],
        codes,
        where,
        act2,
        slope2,
        act,
        wdt,
        act1,
        slope1,
        sorted_g,
        x3,
        matrix,
        *packs2,
        *rings,
        *all_rims2,
        scratch=[
            pltpu.VMEM((384, 384), BF16),
            pltpu.VMEM((1152, 128), BF16),
            pltpu.VMEM((128, 128), BF16),
            pltpu.VMEM((128, CELLS), BF16),
            pltpu.VMEM((128, tiles * 128), BF16),
            pltpu.VMEM((tiles, 256, 128), BF16),
            pltpu.VMEM((34 * HALF, 128), F32),
            pltpu.VMEM((34 * HALF, 128), F32),
            pltpu.VMEM((CELLS + 4 * HALF, 128), BF16),
            pltpu.VMEM((34 * HALF, 384), F32),
            pltpu.VMEM((PADDED, 384), BF16),
            pltpu.VMEM((CELLS, 128), BF16),
            pltpu.VMEM((CELLS, 128), F32),
            pltpu.VMEM((128, 128), F32),
        ],
    )
    pieces = swap(late.reshape(tiles, rows, 128))
    total = call(partial(sum_kernel, scale), shape((rows, 128)), pieces)
    total = swap(jnp.broadcast_to(total[None], (tiles, rows, 128)))
    grads = call(
        unpack_kernel,
        [
            shape((9, own, 128), F32),
            shape((4, own, 128), F32),
            shape((9, own, 128), F32),
            shape((own, 128), F32),
        ],
        total.reshape(tiles * rows, 128),
    )
    return (output, *grads)


def solution(mesh):
    placed = (
        P("chan", "tile"),
        P(None, "chan", None),
        P(None, "chan", None),
        P(None, "chan", None),
        P("chan", None),
        P("chan", "tile"),
        P(),
    )
    return jax.shard_map(
        per_device,
        mesh=mesh,
        in_specs=placed,
        out_specs=(
            P("chan", "tile"),
            P(None, "chan", None),
            P(None, "chan", None),
            P(None, "chan", None),
            P("chan", None),
        ),
        check_vma=False,
    )
```

```python
from functools import partial

import jax
import jax.numpy as jnp
import numpy as np
from jax import lax
from jax.experimental import pallas as pl
from jax.experimental.pallas import tpu as pltpu
from jax.sharding import PartitionSpec as P

SIDE = 64
HALF = 32
CELLS = HALF * HALF
PADDED = 36 * HALF
BLOCK = 8 * SIDE
BF16 = jnp.bfloat16
F32 = jnp.float32
NT = (((1,), (1,)), ((), ()))
ROOT = float(np.sqrt(2.0 / np.pi))
CUBE = 0.044715
side_turns = (0, 1, 2, 3, 0, 2, 2, 0)


def mm(left, right):
    return jnp.dot(left, right, preferred_element_type=F32)


def mm_nt(left, right):
    return lax.dot_general(left, right, NT, preferred_element_type=F32)


def gelu(v):
    return 0.5 * v * (1.0 + jnp.tanh(ROOT * (v + CUBE * (v * v * v))))


def gelu_slope(v):
    square = v * v
    t = jnp.tanh(ROOT * (v + CUBE * (square * v)))
    return 0.5 * (1.0 + t) + (0.5 * ROOT) * v * (1.0 - t * t) * (1.0 + 3.0 * CUBE * square)


def gelu_and_slope(v):
    square = v * v
    t = jnp.tanh(ROOT * (v + CUBE * (square * v)))
    both = 0.5 * (1.0 + t)
    return v * both, both + (0.5 * ROOT) * v * (1.0 - t * t) * (1.0 + 3.0 * CUBE * square)


def iota(shape, dim):
    return lax.broadcasted_iota(jnp.int32, shape, dim)


def one_hot(mask):
    return jnp.where(mask, 1.0, 0.0).astype(BF16)


def flip32(rows):
    anti = one_hot(iota((HALF, HALF), 0) + iota((HALF, HALF), 1) == HALF - 1)
    return mm(anti, rows)


def own_rows(me, own, chans):
    return one_hot(iota((own, chans), 0) + me * own == iota((own, chans), 1))


def side_of(codes_ref, tile, side):
    code = codes_ref[tile, side]
    return jnp.maximum(code, 0) // 4, code & 3, code >= 0


def is_beside(codes_ref, tile, side, partner):
    code = codes_ref[tile, side]
    return (code >= partner * 4) & (code < partner * 4 + 4)


def rows_of(slot, base, own):
    return pl.multiple_of((slot ^ base) * own, own)


def place_conv(packs, base, start, dst_ref):
    own = packs[0].shape[1]
    for slot, pack in enumerate(packs):
        row = rows_of(slot, base, own)
        for a in range(3):
            for b in range(3):
                dst_ref[pl.ds(a * 128 + row, own), b * 128 : (b + 1) * 128] = pack[start + 3 * a + b]


def spread_columns(dst, left, right, center, north, south, west, east, corners):
    rows = 34 * HALF
    middle = jnp.concatenate([north, center, south], axis=0)
    north_east, south_east, south_west, north_west = corners
    left[...] = pltpu.roll(middle, 1, 0)
    right[...] = pltpu.roll(middle, rows - 1, 0)
    left[pl.ds(HALF, HALF, stride=HALF), :] = west
    left[0:1, :] = north_west
    left[33 * HALF : 33 * HALF + 1, :] = south_west
    right[pl.ds(2 * HALF - 1, HALF, stride=HALF), :] = east
    right[HALF - 1 : HALF, :] = north_east
    right[rows - 1 : rows, :] = south_east
    dst[0:rows, 0:128] = left[...].astype(BF16)
    dst[0:rows, 128:256] = middle.astype(BF16)
    dst[0:rows, 256:384] = right[...].astype(BF16)
    dst[rows:PADDED, :] = jnp.zeros((PADDED - rows, 384), BF16)


def fetch(pairs, sems):
    started = [
        pltpu.make_async_copy(source, target, sems.at[index])
        for index, (source, target) in enumerate(pairs)
    ]
    for copy in started:
        copy.start()
    return started


def stacked(ref):
    return jnp.concatenate([ref[:, jb * BLOCK : (jb + 1) * BLOCK] for jb in range(8)], axis=0)


def fill_table(m_ref):
    lane = iota((16, BLOCK), 1)
    quarter, k = (lane >> 5) & 3, lane & 31
    sort_place = quarter * 128 + (lane >> 8) * 64 + 2 * k + ((lane >> 7) & 1)
    turn, x, y, back = lane >> 7, (lane >> 6) & 1, (lane >> 5) & 1, 31 - k
    rim_place = jnp.where(
        turn == 0,
        384 + x * 64 + 2 * k + y,
        jnp.where(
            turn == 1,
            (k & 3) * 128 + y * 64 + 1 - x,
            jnp.where(
                turn == 2,
                (1 - x) * 64 + 2 * back + 1 - y,
                (back & 3) * 128 + (1 - y) * 64 + 62 + x,
            ),
        ),
    )
    place = jnp.concatenate([sort_place, rim_place], axis=1)
    row = iota((16, 2 * BLOCK), 0)
    for group in range(BLOCK // 16):
        m_ref[group * 16 : (group + 1) * 16, :] = one_hot(row + group * 16 == place)


def sort_kernel(
    f_hbm, g_hbm, w1_hbm, wd_hbm, w2_hbm, up_hbm, pack_ref, rims_ref, sorted_ref, pooled_ref, f_ref, g_ref, m_ref, sems
):
    count = f_ref.shape[0]
    started = fetch(
        [
            (f_hbm, f_ref),
            (g_hbm, g_ref),
            (w1_hbm, pack_ref.at[32:41]),
            (wd_hbm, pack_ref.at[41:45]),
            (w2_hbm, pack_ref.at[45:54]),
            (up_hbm, pack_ref.at[54]),
        ],
        sems,
    )
    lane = iota((count, BLOCK), 1)
    turn, slot = lane // 128, lane % HALF
    wanted = jnp.where(
        turn == 0, 7, jnp.where(turn == 1, slot // 4, jnp.where(turn == 2, 0, (HALF - 1 - slot) // 4))
    )
    spot, cell = iota((BLOCK, 128), 0), iota((BLOCK, 128), 1)
    pooling = one_hot((spot // 128 == cell // HALF) & (spot % HALF == cell % HALF))

    def moved(ref):
        stack = jnp.concatenate([ref[:, jb * BLOCK : (jb + 1) * BLOCK] for jb in range(8)], axis=0)
        both = mm(stack, m_ref[...])
        parts = [both[jb * count : (jb + 1) * count] for jb in range(8)]
        rims = jnp.zeros((count, BLOCK), F32)
        for jb in range(8):
            rims = rims + jnp.where(wanted == jb, parts[jb][:, BLOCK:], 0.0)
        return [[part[:, ph * 128 : (ph + 1) * 128] for ph in range(4)] for part in parts], rims.astype(BF16)

    fill_table(m_ref)
    started[0].wait()
    pieces, rims = moved(f_ref)
    for turn_index in range(4):
        rims_ref[0, turn_index] = rims[:, turn_index * 128 : (turn_index + 1) * 128]
    for jb in range(8):
        for ph in range(4):
            pack_ref[ph * 8 + jb] = pieces[jb][ph].astype(BF16)
    started[1].wait()
    pieces, rims = moved(g_ref)
    rims_ref[0, 4] = mm(rims, pooling).astype(BF16)
    for jb in range(8):
        for ph in range(4):
            sorted_ref[:, ph * CELLS + jb * 128 : ph * CELLS + (jb + 1) * 128] = pieces[jb][ph].astype(BF16)
        pooled_ref[jb] = ((pieces[jb][0] + pieces[jb][1]) + (pieces[jb][2] + pieces[jb][3])).astype(BF16)
    for copy in started[2:]:
        copy.wait()


def hold(refs, spots, core, put):
    for ref, slots in zip(refs, spots):
        for index, (even, odd) in enumerate(slots):
            slot = even if even == odd else jnp.where(core == 0, even, odd)
            put(slot, ref, index)


def pick_kernel(spots, codes_ref, where_ref, pooled_ref, *refs):
    *rims, out_ref, held = refs
    tile, base, core = where_ref[0], where_ref[2], where_ref[1] & 1

    def put(slot, ref, index):
        held[slot] = ref[index]

    hold(rims, spots, core, put)
    lane = iota(out_ref.shape[1:], 1) % HALF
    corners = jnp.zeros(lane.shape, F32)
    for side in range(8):
        partner, turn, there = side_of(codes_ref, tile, side)
        picked = jnp.where(there, held[partner ^ base, turn].astype(F32), 0.0)
        if side < 4:
            out_ref[side] = picked.astype(BF16)
        else:
            shift, spot = ((0, 0), (0, HALF - 1), (1, 1), (127, HALF - 2))[side - 4]
            moved = pltpu.roll(picked, shift, 1) if shift else picked
            corners = corners + jnp.where(lane == spot, moved, 0.0)
    out_ref[4] = corners.astype(BF16)
    out_ref[5:13] = pooled_ref[...]
    for other in range(out_ref.shape[0] - 13):
        out_ref[13 + other] = held[other ^ base, 4]


def stage_kernel(pack_ref, pooled_ref, rims_ref, far_ref, near_ref, near_pooled_ref, pair_ref):
    near_ref[...] = pack_ref[...]
    near_pooled_ref[...] = pooled_ref[...]
    pair_ref[0:1] = rims_ref[...]
    pair_ref[1:2] = far_ref[...]


def fine_center_kernel(nc, where_ref, *refs):
    packs, refs = refs[:nc], refs[nc:]
    x3_ref, z1_ref, w1t, wdt, w1s, wds, f_all = refs
    base = where_ref[3]
    own = packs[0].shape[1]
    for slot, pack in enumerate(packs):
        row = rows_of(slot, base, own)
        for block in range(32):
            f_all[pl.ds(row, own), block * 128 : (block + 1) * 128] = pack[block]
        for a in range(3):
            for b in range(3):
                w1s[pl.ds(a * 128 + row, own), b * 128 : (b + 1) * 128] = pack[32 + 3 * a + b]
        for ph in range(4):
            wds[pl.ds(row, own), ph * 128 : (ph + 1) * 128] = pack[41 + ph]
    for a in range(3):
        w1t[a * 384 : (a + 1) * 384, :] = jnp.transpose(w1s[a * 128 : (a + 1) * 128, :])
    wdt[...] = jnp.transpose(wds[...])
    column = iota((CELLS, 128), 0) % HALF
    for ph in range(4):
        center = jnp.transpose(f_all[:, ph * CELLS : (ph + 1) * CELLS]).astype(F32)
        left = jnp.where(column == 0, 0.0, pltpu.roll(center, 1, 0))
        right = jnp.where(column == HALF - 1, 0.0, pltpu.roll(center, CELLS - 1, 0))
        x3_ref[ph, 0:HALF, :] = jnp.zeros((HALF, 384), BF16)
        x3_ref[ph, HALF : HALF + CELLS, 0:128] = left.astype(BF16)
        x3_ref[ph, HALF : HALF + CELLS, 128:256] = center.astype(BF16)
        x3_ref[ph, HALF : HALF + CELLS, 256:384] = right.astype(BF16)
        x3_ref[ph, HALF + CELLS : PADDED, :] = jnp.zeros((PADDED - HALF - CELLS, 384), BF16)
        for start in range(0, CELLS, 256):
            window = jnp.concatenate(
                [x3_ref[ph, start + a * HALF : start + a * HALF + 256, :] for a in range(3)], axis=1
            )
            z1_ref[ph, start : start + 256, :] = mm(window, w1t[...])


def ring_pieces(ring, ph):
    a, b = ph // 2, ph % 2
    near, far = ph * HALF, ((1 - a) * 2 + (1 - b)) * HALF
    east, west = ((1 - b) * 2 + a) * HALF, (b * 2 + (1 - a)) * HALF
    return (
        ring[0, near : near + HALF],
        ring[1, east : east + HALF],
        ring[2, far : far + HALF],
        ring[3, west : west + HALF],
        (
            ring[4, near : near + 1],
            ring[4, far + HALF - 1 : far + HALF],
            ring[4, far + 1 : far + 2],
            ring[4, near + HALF - 2 : near + HALF - 1],
        ),
    )


def windows_of(row, first, final):
    place = iota((HALF, 128), 0)
    return jnp.concatenate(
        [
            jnp.where(place == 0, first, pltpu.roll(row, 1, 0)),
            row,
            jnp.where(place == HALF - 1, final, pltpu.roll(row, HALF - 1, 0)),
        ],
        axis=1,
    ).astype(BF16)


def fine_ring_kernel(nc, where_ref, z1_in, w1t, wdt, *refs):
    rings, refs = refs[:nc], refs[nc:]
    act_ref, slope2_ref, act2_ref, rims_ref, half_ref, ring, ring_all, z1, wide = refs
    base = where_ref[3]
    own = rings[0].shape[1]
    for slot in range(nc):
        row = rows_of(slot, base, own)
        for side in range(5):
            ring_all[side, pl.ds(row, own), :] = rings[slot][side]
    row, col = iota((128, 128), 0), iota((128, 128), 1)
    same = one_hot(row == col)
    turned = one_hot((row // HALF == col // HALF) & (row % HALF + col % HALF == HALF - 1))
    for side in range(5):
        ring[side] = mm_nt(turned if side in (2, 3) else same, ring_all[side])
    z1[...] = z1_in[...]
    pieces = [ring_pieces(ring, ph) for ph in range(4)]

    def owed(rows, weights):
        return mm(jnp.concatenate(rows, axis=0), weights)

    def column(tap):
        return jnp.concatenate(
            [w1t[a * 384 + tap * 128 : a * 384 + (tap + 1) * 128, :] for a in range(3)], axis=0
        )

    north = owed([windows_of(p[0], p[4][3], p[4][0]) for p in pieces], w1t[0:384, :])
    south = owed([windows_of(p[2], p[4][2], p[4][1]) for p in pieces], w1t[768:1152, :])
    west = owed([windows_of(p[3], 0.0, 0.0) for p in pieces], column(0))
    east = owed([windows_of(p[1], 0.0, 0.0) for p in pieces], column(2))
    first = pl.ds(0, HALF, stride=HALF)
    last = pl.ds(HALF - 1, HALF, stride=HALF)
    for ph in range(4):
        rows = slice(ph * HALF, (ph + 1) * HALF)
        z1[ph, 0:HALF, :] += north[rows]
        z1[ph, CELLS - HALF : CELLS, :] += south[rows]
        z1[ph, first, :] = z1[ph, first, :] + west[rows]
        z1[ph, last, :] = z1[ph, last, :] + east[rows]

    def chunk(index, carry):
        start = index * 256
        acts = []
        for ph in range(4):
            act = gelu(z1[ph, pl.ds(start, 256), :]).astype(BF16)
            act_ref[ph, pl.ds(start, 256), :] = act
            acts.append(act)
        z2 = mm(jnp.concatenate(acts, axis=1), wdt[...])
        value, slope = gelu_and_slope(z2)
        slope2_ref[pl.ds(start, 256), :] = slope
        act2 = value.astype(BF16)
        act2_ref[pl.ds(start, 256), :] = act2
        wide[pl.ds(start, 256), :] = act2.astype(F32)
        return carry

    lax.fori_loop(0, 4, chunk, 0)
    for deep in range(2):
        start = CELLS - (deep + 1) * HALF
        rims_ref[0, deep * 128 : deep * 128 + 32, :] = act2_ref[start : start + HALF, :]
        rims_ref[0, deep * 128 + 32 : deep * 128 + 64, :] = wide[
            pl.ds(deep, HALF, stride=HALF), :
        ].astype(BF16)
        rims_ref[0, deep * 128 + 64 : deep * 128 + 96, :] = flip32(
            act2_ref[deep * HALF : (deep + 1) * HALF, :]
        ).astype(BF16)
        rims_ref[0, deep * 128 + 96 : deep * 128 + 128, :] = flip32(
            wide[pl.ds(HALF - 1 - deep, HALF, stride=HALF), :].astype(BF16)
        ).astype(BF16)
    half_ref[0] = rims_ref[0, pl.ds(pl.multiple_of((where_ref[1] & 1) * 128, 128), 128), :]


def own_fine_kernel(w1_ref, ring, x3_in, act_ref, slope_ref, x3_ref):
    own = w1_ref.shape[1]
    row, col = iota((CELLS, HALF), 0), iota((CELLS, HALF), 1)
    at_first, at_last = one_hot(row == col * HALF), one_hot(row == col * HALF + HALF - 1)
    inner = slice(HALF, HALF + CELLS)
    stack = jnp.concatenate(
        [
            jnp.concatenate([w1_ref[3 * a + b] for b in range(3)], axis=1)
            for a in range(3)
        ],
        axis=0,
    )
    for ph in range(4):
        north, east, south, west, corners = ring_pieces(ring, ph)
        x3_ref[ph, inner, 128:256] = x3_in[ph, inner, 128:256]
        x3_ref[ph, 2 * HALF + CELLS : PADDED, :] = jnp.zeros((PADDED - 2 * HALF - CELLS, 384), BF16)
        x3_ref[ph, 0:HALF, :] = windows_of(north, corners[3], corners[0])
        x3_ref[ph, HALF + CELLS : 2 * HALF + CELLS, :] = windows_of(south, corners[2], corners[1])
        x3_ref[ph, inner, 0:128] = x3_in[ph, inner, 0:128] + mm(at_first, west.astype(BF16)).astype(BF16)
        x3_ref[ph, inner, 256:384] = x3_in[ph, inner, 256:384] + mm(at_last, east.astype(BF16)).astype(
            BF16
        )
        terms = mm_nt(stack, x3_ref[ph])
        total = terms[0:own, 0:CELLS]
        for a in range(1, 3):
            moved = pltpu.roll(terms[a * own : (a + 1) * own], PADDED - a * HALF, 1)
            total = total + moved[:, 0:CELLS]
        value, slope = gelu_and_slope(total)
        act_ref[:, ph * CELLS : (ph + 1) * CELLS] = value.astype(BF16)
        slope_ref[:, ph * CELLS : (ph + 1) * CELLS] = slope


def turned_tap(turn, a, b):
    return ((a, b), (b, 2 - a), (2 - a, 2 - b), (2 - b, a))[turn]


CORNER_ENDS = {4: 0, 5: HALF - 1, 6: 0, 7: HALF - 1}
LOW_LEFT = (4, 5, 6, 7)
LOW_RIGHT = (7, 4, 5, 6)


def is_owing(codes_ref, other, side, tile):
    owing = is_beside(codes_ref, other, side, tile)
    if side in (0, 2):
        owing = owing | is_beside(codes_ref, other, LOW_LEFT[side], tile)
        owing = owing | is_beside(codes_ref, other, LOW_RIGHT[side], tile)
    return owing


def strip_of(side, other, codes_ref, base, rims_all):
    turn = (side + 2) % 4

    def rim(partner, slot):
        return rims_all[partner ^ base, pl.ds(pl.multiple_of(slot * HALF, HALF), HALF), :]

    partner, slot, _ = side_of(codes_ref, other, side)
    left_partner, left_slot, _ = side_of(codes_ref, other, (side + 1) % 4)
    right_partner, right_slot, _ = side_of(codes_ref, other, (side + 3) % 4)
    ends = []
    for corner in (LOW_LEFT[side], LOW_RIGHT[side]):
        corner_partner, corner_slot, there = side_of(codes_ref, other, corner)
        spot = CORNER_ENDS[corner]
        row = rim(corner_partner, corner_slot).astype(F32)[spot : spot + 1]
        ends.append(jnp.where(there, row, 0.0))
    left, right = rim(left_partner, left_slot).astype(F32), rim(right_partner, right_slot).astype(F32)
    last = HALF - 1
    here = rims_all[other ^ base, turn * HALF : (turn + 1) * HALF, :].astype(F32)
    above = rims_all[other ^ base, 128 + turn * HALF : 128 + (turn + 1) * HALF, :].astype(F32)
    below = flip32(rim(partner, slot))
    place = iota((HALF, 128), 0)
    by_tap = {}
    for a, (row, first, final) in enumerate(
        (
            (above, left[1:2], right[last - 1 : last]),
            (here, left[0:1], right[last : last + 1]),
            (below, ends[0], ends[1]),
        )
    ):
        by_tap[turned_tap(turn, a, 0)] = jnp.where(place == 0, first, pltpu.roll(row, 1, 0))
        by_tap[turned_tap(turn, a, 1)] = row
        by_tap[turned_tap(turn, a, 2)] = jnp.where(place == last, final, pltpu.roll(row, last, 0))
    return jnp.concatenate([by_tap[a, b] for a in range(3) for b in range(3)], axis=1).astype(BF16)


def back_from(others, codes_ref, tile, base, rims_all, prims, w2s, w2t, ups, back):
    last = HALF - 1
    place = iota((HALF, 128), 0)
    z3 = mm(
        jnp.concatenate([strip_of(side, others[side], codes_ref, base, rims_all) for side in range(4)], axis=0),
        w2t[...],
    )
    pooled = []
    for side in range(4):
        turn = (side + 2) % 4
        select = one_hot(iota((HALF, 128), 0) + turn * HALF == iota((HALF, 128), 1))
        cells = prims[:, pl.ds(pl.multiple_of(others[side] * 128, 128), 128)]
        pooled.append(mm_nt(select, cells))
    g3 = gelu_slope(z3) * mm(jnp.concatenate(pooled, axis=0).astype(BF16), ups[...])
    row, col = iota((128, 128), 0), iota((128, 128), 1)
    turned = one_hot((row // HALF == col // HALF) & (row % HALF + col % HALF == HALF - 1))
    g3 = mm(turned, g3.astype(BF16)).astype(BF16)
    for side in range(4):
        other = others[side]
        owed = []
        for b in range(3):
            r, c = turned_tap((side + 2) % 4, 2, b)
            owed.append(
                mm(
                    g3[side * HALF : (side + 1) * HALF],
                    w2s[r * 128 : (r + 1) * 128, c * 128 : (c + 1) * 128],
                )
            )
        total = (
            jnp.where(place == 0, 0.0, pltpu.roll(owed[0], 1, 0))
            + owed[1]
            + jnp.where(place == last, 0.0, pltpu.roll(owed[2], last, 0))
        )
        _, slot, _ = side_of(codes_ref, other, side)
        counts = is_beside(codes_ref, other, side, tile) & (others[side + 4] == 1)
        back[pl.ds(pl.multiple_of(slot * HALF, HALF), HALF), :] += jnp.where(counts, total, 0.0)
        if side in (0, 2):
            for corner, line in (
                (LOW_LEFT[side], owed[0][last : last + 1]),
                (LOW_RIGHT[side], owed[2][0:1]),
            ):
                _, corner_slot, _ = side_of(codes_ref, other, corner)
                counts = is_beside(codes_ref, other, corner, tile) & (others[side + 4] == 1)

                @pl.when(counts)
                def _():
                    back[pl.ds(pl.multiple_of(corner_slot * HALF, HALF), HALF), :] += jnp.where(
                        place == CORNER_ENDS[corner], line, 0.0
                    )


def own_taps(grad_ref, start, grads, own):
    for a in range(3):
        for b in range(3):
            row = (start + 3 * a + b) * own
            grad_ref[row : row + own, :] = grads[
                a * own : (a + 1) * own, b * 128 : (b + 1) * 128
            ].astype(BF16)


def shifted_stack(values):
    wide = jnp.concatenate([values, jnp.zeros((values.shape[0], PADDED - CELLS), F32)], axis=1)
    return jnp.concatenate(
        [(pltpu.roll(wide, a * HALF, 1) if a else wide).astype(BF16) for a in range(3)], axis=0
    )


def level_kernel(
    nc,
    spots,
    codes_ref,
    where_ref,
    act2_ref,
    slope2_ref,
    act_ref,
    wdt_ref,
    own_ref,
    slope1_ref,
    og_ref,
    x3_ref,
    m_ref,
    *refs,
):
    packs, mores, refs = refs[:nc], refs[nc : 2 * nc], refs[2 * nc :]
    *rims, out_ref, grad_ref, w2s, w2t, ups, pooled_all, prims, rims_all, left, right, g3pad, sums, a3, coarse, field, back = refs
    tile, me, tile_base, base = where_ref[0], where_ref[1], where_ref[2], where_ref[3]
    own = packs[0].shape[1]
    place_conv(packs, base, 45, w2s)
    for slot in range(nc):
        row = rows_of(slot, base, own)
        ups[pl.ds(row, own), :] = packs[slot][54]
        for jb in range(8):
            pooled_all[pl.ds(row, own), jb * 128 : (jb + 1) * 128] = mores[slot][5 + jb]
        for other in range(mores[slot].shape[0] - 13):
            prims[pl.ds(row, own), other * 128 : (other + 1) * 128] = mores[slot][13 + other]

    def put(slot, ref, index):
        rims_all[slot] = ref[index]

    if len(rims) == 9:
        core = me & 1
        rims_all[1, pl.ds(pl.multiple_of(core * 128, 128), 128), :] = rims[4][0]
        rims_all[1, pl.ds(pl.multiple_of(128 - core * 128, 128), 128), :] = rims[8][0]
        rims = rims[:4] + rims[5:8]
    hold(rims, spots, me & 1, put)
    got = []
    for side in range(8):
        partner, turn, there = side_of(codes_ref, tile, side)
        piece = rims_all[
            partner ^ tile_base, pl.ds(pl.multiple_of(turn * HALF, HALF), HALF), :
        ].astype(F32)
        got.append(jnp.where(there, piece, 0.0))
    spread_columns(
        a3,
        left,
        right,
        act2_ref[...].astype(F32),
        got[0],
        flip32(got[2].astype(BF16)),
        flip32(got[3].astype(BF16)),
        got[1],
        (got[4][0:1], got[5][HALF - 1 : HALF], got[6][0:1], got[7][HALF - 1 : HALF]),
    )
    for a in range(3):
        w2t[a * 384 : (a + 1) * 384, :] = jnp.transpose(w2s[a * 128 : (a + 1) * 128, :])
    pooled = jnp.transpose(pooled_all[...])
    g3pad[0 : 2 * HALF, :] = jnp.zeros((2 * HALF, 128), BF16)
    g3pad[CELLS + 2 * HALF : CELLS + 4 * HALF, :] = jnp.zeros((2 * HALF, 128), BF16)
    for index in range(4):
        start = index * 256
        z3 = mm(
            jnp.concatenate(
                [a3[start + a * HALF : start + a * HALF + 256, :] for a in range(3)], axis=1
            ),
            w2t[...],
        )
        value, slope = gelu_and_slope(z3)
        coarse[start : start + 256, :] = value.astype(BF16)
        back_up = mm(pooled[start : start + 256, :], ups[...])
        g3pad[2 * HALF + start : 2 * HALF + start + 256, :] = (slope * back_up).astype(BF16)
    step = 34 * HALF // 4
    for index in range(4):
        start = index * step
        lhs = jnp.concatenate(
            [g3pad[start + (2 - a) * HALF : start + (2 - a) * HALF + step, :] for a in range(3)], axis=1
        )
        sums[start : start + step, :] = mm(lhs, w2s[...])
    rows = 34 * HALF
    column = iota((rows, 128), 0) % HALF
    middle = (
        sums[:, 128:256]
        + jnp.where(column == HALF - 1, 0.0, pltpu.roll(sums[:, 0:128], rows - 1, 0))
        + jnp.where(column == 0, 0.0, pltpu.roll(sums[:, 256:384], 1, 0))
    )
    field[...] = middle[HALF : HALF + CELLS, :]

    back[...] = jnp.zeros_like(back)
    tiles = codes_ref.shape[0]

    def following(before):
        found = []
        for side in range(4):
            spot = jnp.int32(tiles)
            for other in reversed(range(tiles)):
                take = is_owing(codes_ref, other, side, tile) & (other > before[side])
                spot = jnp.where(take, other, spot)
            found.append(spot)
        return tuple(found)

    def left_over(found):
        return (
            (found[0] < tiles) | (found[1] < tiles) | (found[2] < tiles) | (found[3] < tiles)
        )

    def visit(found):
        others = [jnp.minimum(spot, tiles - 1) for spot in found]
        others = others + [jnp.where(spot < tiles, 1, 0) for spot in found]
        back_from(others, codes_ref, tile, tile_base, rims_all, prims, w2s, w2t, ups, back)
        return following(found)

    lax.while_loop(left_over, visit, following((jnp.int32(-1),) * 4))
    anti = jnp.where(iota((HALF, HALF), 0) + iota((HALF, HALF), 1) == HALF - 1, 1.0, 0.0)

    def flip(values):
        return lax.dot_general(
            anti,
            values,
            (((1,), (0,)), ((), ())),
            preferred_element_type=F32,
            precision=lax.Precision.HIGHEST,
        )

    field[CELLS - HALF : CELLS, :] += back[0:32, :]
    field[0:HALF, :] += flip(back[64:96, :])
    first = pl.ds(0, HALF, stride=HALF)
    last = pl.ds(HALF - 1, HALF, stride=HALF)
    field[first, :] = field[first, :] + back[32:64, :]
    field[last, :] = field[last, :] + flip(back[96:128, :])

    g2 = (slope2_ref[...] * field[...]).astype(BF16)
    pick = own_rows(me, own, 128)
    g2_turned = mm_nt(one_hot(iota((128, 128), 0) == iota((128, 128), 1)), g2).astype(BF16)
    g2_own = mm_nt(pick, g2).astype(BF16)
    grads = jnp.zeros((3 * own, 384), F32)
    for ph in range(4):
        grad_ref[(9 + ph) * own : (10 + ph) * own, :] = mm(g2_own, act_ref[ph]).astype(BF16)
        turned = wdt_ref[pl.ds(pl.multiple_of(ph * 128 + me * own, own), own), :]
        cells = slice(ph * CELLS, (ph + 1) * CELLS)
        g1 = slope1_ref[:, cells] * (og_ref[:, cells].astype(F32) + mm(turned, g2_turned))
        grads = grads + mm(shifted_stack(g1), x3_ref[ph])
    own_taps(grad_ref, 0, grads, own)
    g3 = mm_nt(pick, g3pad[2 * HALF : 2 * HALF + CELLS, :])
    own_taps(grad_ref, 13, mm(shifted_stack(g3), a3[...]), own)
    own_spot = pl.ds(pl.multiple_of(me * own, own), own)
    grad_ref[22 * own : 23 * own, :] = mm(pooled_all[own_spot, :], coarse[...]).astype(BF16)
    if grad_ref.shape[0] > 23 * own:
        grad_ref[23 * own :, :] = jnp.zeros((grad_ref.shape[0] - 23 * own, 128), BF16)

    lifted = mm_nt(ups[own_spot, :], coarse[...])
    total = [
        own_ref[:, ph * CELLS : (ph + 1) * CELLS].astype(F32) + lifted for ph in range(4)
    ]
    stack = jnp.concatenate(
        [
            jnp.concatenate([total[ph][:, jb * 128 : (jb + 1) * 128] for ph in range(4)], axis=1)
            for jb in range(8)
        ],
        axis=0,
    ).astype(BF16)
    natural = mm_nt(stack, m_ref[...]).astype(BF16)
    for jb in range(8):
        out_ref[:, jb * BLOCK : (jb + 1) * BLOCK] = natural[jb * own : (jb + 1) * own]


def sum_kernel(scale, in_ref, out_ref):
    total = in_ref[0].astype(F32)
    for slot in range(1, in_ref.shape[0]):
        total = total + in_ref[slot].astype(F32)
    out_ref[...] = (total * scale).astype(BF16)


def unpack_kernel(flat, one_ref, down_ref, two_ref, up_ref):
    own = up_ref.shape[0]
    for tap in range(9):
        one_ref[tap] = flat[tap * own : (tap + 1) * own, :].astype(F32)
        two_ref[tap] = flat[(13 + tap) * own : (14 + tap) * own, :].astype(F32)
    for ph in range(4):
        down_ref[ph] = flat[(9 + ph) * own : (10 + ph) * own, :].astype(F32)
    up_ref[...] = flat[22 * own : 23 * own, :].astype(F32)


def call(kernel, outs, *args, scratch=(), far=(), room=24, alias={}):
    specs = [
        pl.BlockSpec(
            memory_space=pltpu.SMEM if a.dtype == jnp.int32 else pltpu.HBM if i in far else pltpu.VMEM
        )
        for i, a in enumerate(args)
    ]
    many = isinstance(outs, list)
    vmem = pl.BlockSpec(memory_space=pltpu.VMEM)
    return pl.pallas_call(
        kernel,
        out_shape=outs,
        in_specs=specs,
        out_specs=[vmem] * len(outs) if many else vmem,
        scratch_shapes=list(scratch),
        input_output_aliases=alias,
        compiler_params=pltpu.CompilerParams(vmem_limit_bytes=room * 1024 * 1024),
    )(*args)


def shape(dims, kind=BF16):
    return jax.ShapeDtypeStruct(dims, kind)


def sort_matrix():
    table = np.zeros((BLOCK, BLOCK), np.float32)
    for a in range(2):
        for b in range(2):
            for q in range(4):
                for k in range(HALF):
                    table[q * 128 + a * 64 + 2 * k + b, (2 * a + b) * 128 + q * HALF + k] = 1
    return jnp.asarray(table, BF16)


def paired(values, axis, bit):
    count = lax.axis_size(axis)
    return lax.ppermute(values, axis, [(i, i ^ bit) for i in range(count)])


FIRST, SECOND = (7, 4, 2), (6, 5, 3)


def is_split():
    return lax.axis_size("tile") == 8 and lax.axis_size("chan") % 2 == 0


def spots_of():
    tiles = lax.axis_size("tile")
    if not is_split():
        return [[(slot, slot) for slot in range(tiles)]]
    pairs = list(zip(FIRST, SECOND))
    return [[(0, 0)]] + [[pair] for pair in pairs] + [[pair[::-1]] for pair in pairs]


def copies(block, half=None, beside=()):
    tiles, nc = lax.axis_size("tile"), lax.axis_size("chan")
    if not is_split():
        return [swap(jnp.broadcast_to(block, (tiles,) + block.shape[1:]))], beside
    got = []
    for slots in zip(FIRST, SECOND):
        perm = [
            (tile * nc + chan, (tile ^ slots[chan & 1]) * nc + chan)
            for tile in range(tiles)
            for chan in range(nc)
        ]
        got.append(lax.ppermute(block, ("tile", "chan"), perm))
    got.append(paired(half, "tile", 1))
    got, beside = lax.optimization_barrier((got, beside))
    return [block] + got + [paired(part, "chan", 1) for part in got], beside


def swap(values):
    return lax.all_to_all(values, "tile", split_axis=0, concat_axis=0)


def gathered(values, axis):
    slots = {0: values}
    bit = lax.axis_size(axis) // 2
    while bit:
        slots.update({slot ^ bit: paired(held, axis, bit) for slot, held in list(slots.items())})
        bit //= 2
    return [slots[slot] for slot in range(len(slots))]


def per_device(features, conv1_weight, down_weight, conv2_weight, up_weight, out_grad, adjacency):
    own = features.shape[0]
    tiles, nc = lax.axis_size("tile"), lax.axis_size("chan")
    scale = float((tiles * SIDE * SIDE) ** (-0.5))
    tile, chan = lax.axis_index("tile"), lax.axis_index("chan")
    where = jnp.stack([tile, chan, tile if is_split() else tile * 0, chan]).astype(jnp.int32)
    matrix = sort_matrix()
    half = nc // 2

    pack, rims, sorted_g, pooled = call(
        sort_kernel,
        [
            shape((55, own, 128)),
            shape((1, 5, own, 128)),
            shape((own, 4 * CELLS)),
            shape((8, own, 128)),
        ],
        features,
        out_grad,
        conv1_weight,
        down_weight,
        conv2_weight,
        up_weight,
        far=range(6),
        room=60,
        scratch=[
            pltpu.VMEM((own, 4 * CELLS), BF16),
            pltpu.VMEM((own, 4 * CELLS), BF16),
            pltpu.VMEM((BLOCK, 2 * BLOCK), BF16),
            pltpu.SemaphoreType.DMA((6,)),
        ],
    )
    pack_far = paired(pack, "chan", half)
    if is_split():
        far, near = paired(rims, "tile", 4), paired(rims, "tile", 2)
        cross = paired(far, "tile", 2)
        pack_near, pooled, pair = call(
            stage_kernel,
            [shape(pack.shape), shape(pooled.shape), shape((2,) + rims.shape[1:])],
            pack,
            pooled,
            rims,
            far,
        )
        beside = paired(pair, "tile", 1)
        cross, near, pack_near, adjacency = lax.optimization_barrier((cross, near, pack_near, adjacency))
        last = [paired(near, "tile", 1), paired(cross, "tile", 1)]
        all_rims = [pair, near, cross, beside] + last
        rim_spots = [[(slot, slot) for slot in group] for group in ((0, 4), (2,), (6,), (1, 5), (3,), (7,))]
    else:
        all_rims, rim_spots = copies(rims)[0], spots_of()
        pack_near = pack
    turns = (adjacency[:, :, 1] + jnp.array(side_turns, jnp.int32)) & 3
    codes = jnp.where(adjacency[:, :, 0] < 0, -1, adjacency[:, :, 0] * 4 + turns)
    ring = call(
        partial(pick_kernel, rim_spots),
        shape((13 + tiles, own, 128)),
        codes,
        where,
        pooled,
        *all_rims,
        scratch=[pltpu.VMEM((tiles + 1, 5, own, 128), BF16)],
    )
    pack_far, ring = lax.optimization_barrier((pack_far, ring))
    ring_far = paired(ring, "chan", half)

    def whole(near, far, held=None):
        return [near if held is None else held, paired(near, "chan", 1), far, paired(far, "chan", 1)]

    packs = whole(pack, pack_far, pack_near)
    x3, z1c, w1t, wdt = call(
        partial(fine_center_kernel, nc),
        [
            shape((4, PADDED, 384)),
            shape((4, CELLS, 128), F32),
            shape((1152, 128)),
            shape((512, 128)),
        ],
        where,
        *packs,
        scratch=[
            pltpu.VMEM((384, 384), BF16),
            pltpu.VMEM((128, 512), BF16),
            pltpu.VMEM((128, 4 * CELLS), BF16),
        ],
    )
    x3, ring_far = lax.optimization_barrier((x3, ring_far))
    rings = whole(ring, ring_far)
    act, slope2, act2, rims2, half2, ring_sorted = call(
        partial(fine_ring_kernel, nc),
        [
            shape((4, CELLS, 128)),
            shape((CELLS, 128), F32),
            shape((CELLS, 128)),
            shape((1, 256, 128)),
            shape((1, 128, 128)),
            shape((5, 128, 128), F32),
        ],
        where,
        z1c,
        w1t,
        wdt,
        *rings,
        scratch=[
            pltpu.VMEM((5, 128, 128), BF16),
            pltpu.VMEM((4, CELLS, 128), F32),
            pltpu.VMEM((CELLS, 128), F32),
        ],
    )
    act1, slope1, x3 = call(
        own_fine_kernel,
        [shape((own, 4 * CELLS)), shape((own, 4 * CELLS), F32), shape((4, PADDED, 384))],
        conv1_weight,
        ring_sorted,
        x3,
        alias={2: 2},
    )
    all_rims2, (act1, slope1, x3) = copies(rims2, half2, (act1, slope1, x3))
    rows = -(-23 * own // (16 * tiles)) * 16
    output, late = call(
        partial(level_kernel, nc, spots_of()),
        [shape((own, 4 * CELLS)), shape((rows * tiles, 128))],
        codes,
        where,
        act2,
        slope2,
        act,
        wdt,
        act1,
        slope1,
        sorted_g,
        x3,
        matrix,
        *packs,
        *rings,
        *all_rims2,
        scratch=[
            pltpu.VMEM((384, 384), BF16),
            pltpu.VMEM((1152, 128), BF16),
            pltpu.VMEM((128, 128), BF16),
            pltpu.VMEM((128, CELLS), BF16),
            pltpu.VMEM((128, tiles * 128), BF16),
            pltpu.VMEM((tiles, 256, 128), BF16),
            pltpu.VMEM((34 * HALF, 128), F32),
            pltpu.VMEM((34 * HALF, 128), F32),
            pltpu.VMEM((CELLS + 4 * HALF, 128), BF16),
            pltpu.VMEM((34 * HALF, 384), F32),
            pltpu.VMEM((PADDED, 384), BF16),
            pltpu.VMEM((CELLS, 128), BF16),
            pltpu.VMEM((CELLS, 128), F32),
            pltpu.VMEM((128, 128), F32),
        ],
    )
    pieces = swap(late.reshape(tiles, rows, 128))
    total = call(partial(sum_kernel, scale), shape((rows, 128)), pieces)
    total = swap(jnp.broadcast_to(total[None], (tiles, rows, 128)))
    grads = call(
        unpack_kernel,
        [
            shape((9, own, 128), F32),
            shape((4, own, 128), F32),
            shape((9, own, 128), F32),
            shape((own, 128), F32),
        ],
        total.reshape(tiles * rows, 128),
    )
    return (output, *grads)


def solution(mesh):
    placed = (
        P("chan", "tile"),
        P(None, "chan", None),
        P(None, "chan", None),
        P(None, "chan", None),
        P("chan", None),
        P("chan", "tile"),
        P(),
    )
    return jax.shard_map(
        per_device,
        mesh=mesh,
        in_specs=placed,
        out_specs=(
            P("chan", "tile"),
            P(None, "chan", None),
            P(None, "chan", None),
            P(None, "chan", None),
            P("chan", None),
        ),
        check_vma=False,
    )
```

```python
from functools import partial

import jax
import jax.numpy as jnp
import numpy as np
from jax import lax
from jax.experimental import pallas as pl
from jax.experimental.pallas import tpu as pltpu
from jax.sharding import PartitionSpec as P

SIDE = 64
HALF = 32
CELLS = HALF * HALF
PADDED = 36 * HALF
BLOCK = 8 * SIDE
BF16 = jnp.bfloat16
F32 = jnp.float32
NT = (((1,), (1,)), ((), ()))
ROOT = float(np.sqrt(2.0 / np.pi))
CUBE = 0.044715
side_turns = (0, 1, 2, 3, 0, 2, 2, 0)


def mm(left, right):
    return jnp.dot(left, right, preferred_element_type=F32)


def mm_nt(left, right):
    return lax.dot_general(left, right, NT, preferred_element_type=F32)


def gelu(v):
    return 0.5 * v * (1.0 + jnp.tanh(ROOT * (v + CUBE * (v * v * v))))


def gelu_slope(v):
    square = v * v
    t = jnp.tanh(ROOT * (v + CUBE * (square * v)))
    return 0.5 * (1.0 + t) + (0.5 * ROOT) * v * (1.0 - t * t) * (1.0 + 3.0 * CUBE * square)


def gelu_and_slope(v):
    square = v * v
    t = jnp.tanh(ROOT * (v + CUBE * (square * v)))
    both = 0.5 * (1.0 + t)
    return v * both, both + (0.5 * ROOT) * v * (1.0 - t * t) * (1.0 + 3.0 * CUBE * square)


def iota(shape, dim):
    return lax.broadcasted_iota(jnp.int32, shape, dim)


def one_hot(mask):
    return jnp.where(mask, 1.0, 0.0).astype(BF16)


def flip32(rows):
    anti = one_hot(iota((HALF, HALF), 0) + iota((HALF, HALF), 1) == HALF - 1)
    return mm(anti, rows)


def own_rows(me, own, chans):
    return one_hot(iota((own, chans), 0) + me * own == iota((own, chans), 1))


def side_of(codes_ref, tile, side):
    code = codes_ref[tile, side]
    return jnp.maximum(code, 0) // 4, code & 3, code >= 0


def is_beside(codes_ref, tile, side, partner):
    code = codes_ref[tile, side]
    return (code >= partner * 4) & (code < partner * 4 + 4)


def rows_of(slot, base, own):
    return pl.multiple_of((slot ^ base) * own, own)


def place_conv(packs, base, start, dst_ref):
    own = packs[0].shape[1]
    for slot, pack in enumerate(packs):
        row = rows_of(slot, base, own)
        for a in range(3):
            for b in range(3):
                dst_ref[pl.ds(a * 128 + row, own), b * 128 : (b + 1) * 128] = pack[start + 3 * a + b]


def spread_columns(dst, left, right, center, north, south, west, east, corners):
    rows = 34 * HALF
    middle = jnp.concatenate([north, center, south], axis=0)
    north_east, south_east, south_west, north_west = corners
    left[...] = pltpu.roll(middle, 1, 0)
    right[...] = pltpu.roll(middle, rows - 1, 0)
    left[pl.ds(HALF, HALF, stride=HALF), :] = west
    left[0:1, :] = north_west
    left[33 * HALF : 33 * HALF + 1, :] = south_west
    right[pl.ds(2 * HALF - 1, HALF, stride=HALF), :] = east
    right[HALF - 1 : HALF, :] = north_east
    right[rows - 1 : rows, :] = south_east
    dst[0:rows, 0:128] = left[...].astype(BF16)
    dst[0:rows, 128:256] = middle.astype(BF16)
    dst[0:rows, 256:384] = right[...].astype(BF16)
    dst[rows:PADDED, :] = jnp.zeros((PADDED - rows, 384), BF16)


def fetch(pairs, sems):
    started = [
        pltpu.make_async_copy(source, target, sems.at[index])
        for index, (source, target) in enumerate(pairs)
    ]
    for copy in started:
        copy.start()
    return started


def stacked(ref):
    return jnp.concatenate([ref[:, jb * BLOCK : (jb + 1) * BLOCK] for jb in range(8)], axis=0)


def fill_table(m_ref):
    lane = iota((16, BLOCK), 1)
    quarter, k = (lane >> 5) & 3, lane & 31
    sort_place = quarter * 128 + (lane >> 8) * 64 + 2 * k + ((lane >> 7) & 1)
    turn, x, y, back = lane >> 7, (lane >> 6) & 1, (lane >> 5) & 1, 31 - k
    rim_place = jnp.where(
        turn == 0,
        384 + x * 64 + 2 * k + y,
        jnp.where(
            turn == 1,
            (k & 3) * 128 + y * 64 + 1 - x,
            jnp.where(
                turn == 2,
                (1 - x) * 64 + 2 * back + 1 - y,
                (back & 3) * 128 + (1 - y) * 64 + 62 + x,
            ),
        ),
    )
    place = jnp.concatenate([sort_place, rim_place], axis=1)[:, : m_ref.shape[1]]
    row = iota(place.shape, 0)
    for group in range(BLOCK // 16):
        m_ref[group * 16 : (group + 1) * 16, :] = one_hot(row + group * 16 == place)


def sort_kernel(
    f_hbm, g_hbm, w1_hbm, wd_hbm, w2_hbm, up_hbm, pack_ref, rims_ref, sorted_ref, pack2_ref, f_ref, g_ref, m_ref, sems
):
    count = f_ref.shape[0]
    started = fetch(
        [
            (f_hbm, f_ref),
            (g_hbm, g_ref),
            (w1_hbm, pack_ref.at[32:41]),
            (wd_hbm, pack_ref.at[41:45]),
            (w2_hbm, pack2_ref.at[8:17]),
            (up_hbm, pack2_ref.at[17]),
        ],
        sems,
    )
    lane = iota((count, BLOCK), 1)
    turn, slot = lane // 128, lane % HALF
    wanted = jnp.where(
        turn == 0, 7, jnp.where(turn == 1, slot // 4, jnp.where(turn == 2, 0, (HALF - 1 - slot) // 4))
    )
    spot, cell = iota((BLOCK, 128), 0), iota((BLOCK, 128), 1)
    pooling = one_hot((spot // 128 == cell // HALF) & (spot % HALF == cell % HALF))

    def moved(ref):
        stack = jnp.concatenate([ref[:, jb * BLOCK : (jb + 1) * BLOCK] for jb in range(8)], axis=0)
        both = mm(stack, m_ref[...])
        parts = [both[jb * count : (jb + 1) * count] for jb in range(8)]
        rims = jnp.zeros((count, BLOCK), F32)
        for jb in range(8):
            rims = rims + jnp.where(wanted == jb, parts[jb][:, BLOCK:], 0.0)
        return [[part[:, ph * 128 : (ph + 1) * 128] for ph in range(4)] for part in parts], rims.astype(BF16)

    fill_table(m_ref)
    started[0].wait()
    pieces, rims = moved(f_ref)
    for turn_index in range(4):
        rims_ref[0, turn_index] = rims[:, turn_index * 128 : (turn_index + 1) * 128]
    for jb in range(8):
        for ph in range(4):
            pack_ref[ph * 8 + jb] = pieces[jb][ph].astype(BF16)
    started[1].wait()
    pieces, rims = moved(g_ref)
    rims_ref[0, 4] = mm(rims, pooling).astype(BF16)
    for jb in range(8):
        for ph in range(4):
            sorted_ref[:, ph * CELLS + jb * 128 : ph * CELLS + (jb + 1) * 128] = pieces[jb][ph].astype(BF16)
        pack2_ref[jb] = ((pieces[jb][0] + pieces[jb][1]) + (pieces[jb][2] + pieces[jb][3])).astype(BF16)
    for copy in started[2:]:
        copy.wait()


def hold(refs, spots, core, put):
    for ref, slots in zip(refs, spots):
        for index, (even, odd) in enumerate(slots):
            slot = even if even == odd else jnp.where(core == 0, even, odd)
            put(slot, ref, index)


def pick_kernel(spots, codes_ref, where_ref, *refs):
    *rims, out_ref, held = refs
    tile, base, core = where_ref[0], where_ref[2], where_ref[1] & 1

    def put(slot, ref, index):
        held[slot] = ref[index]

    hold(rims, spots, core, put)
    lane = iota(out_ref.shape[1:], 1) % HALF
    corners = jnp.zeros(lane.shape, F32)
    for side in range(8):
        partner, turn, there = side_of(codes_ref, tile, side)
        picked = jnp.where(there, held[partner ^ base, turn].astype(F32), 0.0)
        if side < 4:
            out_ref[side] = picked.astype(BF16)
        else:
            shift, spot = ((0, 0), (0, HALF - 1), (1, 1), (127, HALF - 2))[side - 4]
            moved = pltpu.roll(picked, shift, 1) if shift else picked
            corners = corners + jnp.where(lane == spot, moved, 0.0)
    out_ref[4] = corners.astype(BF16)
    for other in range(out_ref.shape[0] - 5):
        out_ref[5 + other] = held[other ^ base, 4]


def stage_kernel(pack_ref, rims_ref, far_ref, near_ref, pair_ref):
    near_ref[...] = pack_ref[...]
    pair_ref[0:1] = rims_ref[...]
    pair_ref[1:2] = far_ref[...]


def fine_center_kernel(nc, where_ref, *refs):
    packs, refs = refs[:nc], refs[nc:]
    x3_ref, z1_ref, w1t, wdt, w1s, wds, f_all = refs
    base = where_ref[3]
    own = packs[0].shape[1]
    for slot, pack in enumerate(packs):
        row = rows_of(slot, base, own)
        for block in range(32):
            f_all[pl.ds(row, own), block * 128 : (block + 1) * 128] = pack[block]
        for a in range(3):
            for b in range(3):
                w1s[pl.ds(a * 128 + row, own), b * 128 : (b + 1) * 128] = pack[32 + 3 * a + b]
        for ph in range(4):
            wds[pl.ds(row, own), ph * 128 : (ph + 1) * 128] = pack[41 + ph]
    for a in range(3):
        w1t[a * 384 : (a + 1) * 384, :] = jnp.transpose(w1s[a * 128 : (a + 1) * 128, :])
    wdt[...] = jnp.transpose(wds[...])
    column = iota((CELLS, 128), 0) % HALF
    for ph in range(4):
        center = jnp.transpose(f_all[:, ph * CELLS : (ph + 1) * CELLS]).astype(F32)
        left = jnp.where(column == 0, 0.0, pltpu.roll(center, 1, 0))
        right = jnp.where(column == HALF - 1, 0.0, pltpu.roll(center, CELLS - 1, 0))
        x3_ref[ph, 0:HALF, :] = jnp.zeros((HALF, 384), BF16)
        x3_ref[ph, HALF : HALF + CELLS, 0:128] = left.astype(BF16)
        x3_ref[ph, HALF : HALF + CELLS, 128:256] = center.astype(BF16)
        x3_ref[ph, HALF : HALF + CELLS, 256:384] = right.astype(BF16)
        x3_ref[ph, HALF + CELLS : PADDED, :] = jnp.zeros((PADDED - HALF - CELLS, 384), BF16)
        for start in range(0, CELLS, 256):
            window = jnp.concatenate(
                [x3_ref[ph, start + a * HALF : start + a * HALF + 256, :] for a in range(3)], axis=1
            )
            z1_ref[ph, start : start + 256, :] = mm(window, w1t[...])


def ring_pieces(ring, ph):
    a, b = ph // 2, ph % 2
    near, far = ph * HALF, ((1 - a) * 2 + (1 - b)) * HALF
    east, west = ((1 - b) * 2 + a) * HALF, (b * 2 + (1 - a)) * HALF
    return (
        ring[0, near : near + HALF],
        ring[1, east : east + HALF],
        ring[2, far : far + HALF],
        ring[3, west : west + HALF],
        (
            ring[4, near : near + 1],
            ring[4, far + HALF - 1 : far + HALF],
            ring[4, far + 1 : far + 2],
            ring[4, near + HALF - 2 : near + HALF - 1],
        ),
    )


def windows_of(row, first, final):
    place = iota((HALF, 128), 0)
    return jnp.concatenate(
        [
            jnp.where(place == 0, first, pltpu.roll(row, 1, 0)),
            row,
            jnp.where(place == HALF - 1, final, pltpu.roll(row, HALF - 1, 0)),
        ],
        axis=1,
    ).astype(BF16)


def fine_ring_kernel(nc, where_ref, z1_in, w1t, wdt, *refs):
    rings, refs = refs[:nc], refs[nc:]
    act_ref, slope2_ref, act2_ref, rims_ref, half_ref, ring, ring_all, z1, wide = refs
    base = where_ref[3]
    own = rings[0].shape[1]
    for slot in range(nc):
        row = rows_of(slot, base, own)
        for side in range(5):
            ring_all[side, pl.ds(row, own), :] = rings[slot][side]
    row, col = iota((128, 128), 0), iota((128, 128), 1)
    same = one_hot(row == col)
    turned = one_hot((row // HALF == col // HALF) & (row % HALF + col % HALF == HALF - 1))
    for side in range(5):
        ring[side] = mm_nt(turned if side in (2, 3) else same, ring_all[side])
    z1[...] = z1_in[...]
    pieces = [ring_pieces(ring, ph) for ph in range(4)]

    def owed(rows, weights):
        return mm(jnp.concatenate(rows, axis=0), weights)

    def column(tap):
        return jnp.concatenate(
            [w1t[a * 384 + tap * 128 : a * 384 + (tap + 1) * 128, :] for a in range(3)], axis=0
        )

    north = owed([windows_of(p[0], p[4][3], p[4][0]) for p in pieces], w1t[0:384, :])
    south = owed([windows_of(p[2], p[4][2], p[4][1]) for p in pieces], w1t[768:1152, :])
    west = owed([windows_of(p[3], 0.0, 0.0) for p in pieces], column(0))
    east = owed([windows_of(p[1], 0.0, 0.0) for p in pieces], column(2))
    first = pl.ds(0, HALF, stride=HALF)
    last = pl.ds(HALF - 1, HALF, stride=HALF)
    for ph in range(4):
        rows = slice(ph * HALF, (ph + 1) * HALF)
        z1[ph, 0:HALF, :] += north[rows]
        z1[ph, CELLS - HALF : CELLS, :] += south[rows]
        z1[ph, first, :] = z1[ph, first, :] + west[rows]
        z1[ph, last, :] = z1[ph, last, :] + east[rows]

    def chunk(index, carry):
        start = index * 256
        acts = []
        for ph in range(4):
            act = gelu(z1[ph, pl.ds(start, 256), :]).astype(BF16)
            act_ref[ph, pl.ds(start, 256), :] = act
            acts.append(act)
        z2 = mm(jnp.concatenate(acts, axis=1), wdt[...])
        value, slope = gelu_and_slope(z2)
        slope2_ref[pl.ds(start, 256), :] = slope
        act2 = value.astype(BF16)
        act2_ref[pl.ds(start, 256), :] = act2
        wide[pl.ds(start, 256), :] = act2.astype(F32)
        return carry

    lax.fori_loop(0, 4, chunk, 0)
    for deep in range(2):
        start = CELLS - (deep + 1) * HALF
        rims_ref[0, deep * 128 : deep * 128 + 32, :] = act2_ref[start : start + HALF, :]
        rims_ref[0, deep * 128 + 32 : deep * 128 + 64, :] = wide[
            pl.ds(deep, HALF, stride=HALF), :
        ].astype(BF16)
        rims_ref[0, deep * 128 + 64 : deep * 128 + 96, :] = flip32(
            act2_ref[deep * HALF : (deep + 1) * HALF, :]
        ).astype(BF16)
        rims_ref[0, deep * 128 + 96 : deep * 128 + 128, :] = flip32(
            wide[pl.ds(HALF - 1 - deep, HALF, stride=HALF), :].astype(BF16)
        ).astype(BF16)
    half_ref[0] = rims_ref[0, pl.ds(pl.multiple_of((where_ref[1] & 1) * 128, 128), 128), :]


def own_fine_kernel(w1_ref, ring, x3_in, act_ref, slope_ref, x3_ref):
    own = w1_ref.shape[1]
    row, col = iota((CELLS, HALF), 0), iota((CELLS, HALF), 1)
    at_first, at_last = one_hot(row == col * HALF), one_hot(row == col * HALF + HALF - 1)
    inner = slice(HALF, HALF + CELLS)
    stack = jnp.concatenate(
        [
            jnp.concatenate([w1_ref[3 * a + b] for b in range(3)], axis=1)
            for a in range(3)
        ],
        axis=0,
    )
    for ph in range(4):
        north, east, south, west, corners = ring_pieces(ring, ph)
        x3_ref[ph, inner, 128:256] = x3_in[ph, inner, 128:256]
        x3_ref[ph, 2 * HALF + CELLS : PADDED, :] = jnp.zeros((PADDED - 2 * HALF - CELLS, 384), BF16)
        x3_ref[ph, 0:HALF, :] = windows_of(north, corners[3], corners[0])
        x3_ref[ph, HALF + CELLS : 2 * HALF + CELLS, :] = windows_of(south, corners[2], corners[1])
        x3_ref[ph, inner, 0:128] = x3_in[ph, inner, 0:128] + mm(at_first, west.astype(BF16)).astype(BF16)
        x3_ref[ph, inner, 256:384] = x3_in[ph, inner, 256:384] + mm(at_last, east.astype(BF16)).astype(
            BF16
        )
        terms = mm_nt(stack, x3_ref[ph])
        total = terms[0:own, 0:CELLS]
        for a in range(1, 3):
            moved = pltpu.roll(terms[a * own : (a + 1) * own], PADDED - a * HALF, 1)
            total = total + moved[:, 0:CELLS]
        value, slope = gelu_and_slope(total)
        act_ref[:, ph * CELLS : (ph + 1) * CELLS] = value.astype(BF16)
        slope_ref[:, ph * CELLS : (ph + 1) * CELLS] = slope


def turned_tap(turn, a, b):
    return ((a, b), (b, 2 - a), (2 - a, 2 - b), (2 - b, a))[turn]


CORNER_ENDS = {4: 0, 5: HALF - 1, 6: 0, 7: HALF - 1}
LOW_LEFT = (4, 5, 6, 7)
LOW_RIGHT = (7, 4, 5, 6)


def is_owing(codes_ref, other, side, tile):
    owing = is_beside(codes_ref, other, side, tile)
    if side in (0, 2):
        owing = owing | is_beside(codes_ref, other, LOW_LEFT[side], tile)
        owing = owing | is_beside(codes_ref, other, LOW_RIGHT[side], tile)
    return owing


def strip_of(side, other, codes_ref, base, rims_all):
    turn = (side + 2) % 4

    def rim(partner, slot):
        return rims_all[partner ^ base, pl.ds(pl.multiple_of(slot * HALF, HALF), HALF), :]

    partner, slot, _ = side_of(codes_ref, other, side)
    left_partner, left_slot, _ = side_of(codes_ref, other, (side + 1) % 4)
    right_partner, right_slot, _ = side_of(codes_ref, other, (side + 3) % 4)
    ends = []
    for corner in (LOW_LEFT[side], LOW_RIGHT[side]):
        corner_partner, corner_slot, there = side_of(codes_ref, other, corner)
        spot = CORNER_ENDS[corner]
        row = rim(corner_partner, corner_slot).astype(F32)[spot : spot + 1]
        ends.append(jnp.where(there, row, 0.0))
    left, right = rim(left_partner, left_slot).astype(F32), rim(right_partner, right_slot).astype(F32)
    last = HALF - 1
    here = rims_all[other ^ base, turn * HALF : (turn + 1) * HALF, :].astype(F32)
    above = rims_all[other ^ base, 128 + turn * HALF : 128 + (turn + 1) * HALF, :].astype(F32)
    below = flip32(rim(partner, slot))
    place = iota((HALF, 128), 0)
    by_tap = {}
    for a, (row, first, final) in enumerate(
        (
            (above, left[1:2], right[last - 1 : last]),
            (here, left[0:1], right[last : last + 1]),
            (below, ends[0], ends[1]),
        )
    ):
        by_tap[turned_tap(turn, a, 0)] = jnp.where(place == 0, first, pltpu.roll(row, 1, 0))
        by_tap[turned_tap(turn, a, 1)] = row
        by_tap[turned_tap(turn, a, 2)] = jnp.where(place == last, final, pltpu.roll(row, last, 0))
    return jnp.concatenate([by_tap[a, b] for a in range(3) for b in range(3)], axis=1).astype(BF16)


def back_from(others, codes_ref, tile, base, rims_all, prims, w2s, w2t, ups, back):
    last = HALF - 1
    place = iota((HALF, 128), 0)
    z3 = mm(
        jnp.concatenate([strip_of(side, others[side], codes_ref, base, rims_all) for side in range(4)], axis=0),
        w2t[...],
    )
    pooled = []
    for side in range(4):
        turn = (side + 2) % 4
        select = one_hot(iota((HALF, 128), 0) + turn * HALF == iota((HALF, 128), 1))
        cells = prims[:, pl.ds(pl.multiple_of(others[side] * 128, 128), 128)]
        pooled.append(mm_nt(select, cells))
    g3 = gelu_slope(z3) * mm(jnp.concatenate(pooled, axis=0).astype(BF16), ups[...])
    row, col = iota((128, 128), 0), iota((128, 128), 1)
    turned = one_hot((row // HALF == col // HALF) & (row % HALF + col % HALF == HALF - 1))
    g3 = mm(turned, g3.astype(BF16)).astype(BF16)
    for side in range(4):
        other = others[side]
        owed = []
        for b in range(3):
            r, c = turned_tap((side + 2) % 4, 2, b)
            owed.append(
                mm(
                    g3[side * HALF : (side + 1) * HALF],
                    w2s[r * 128 : (r + 1) * 128, c * 128 : (c + 1) * 128],
                )
            )
        total = (
            jnp.where(place == 0, 0.0, pltpu.roll(owed[0], 1, 0))
            + owed[1]
            + jnp.where(place == last, 0.0, pltpu.roll(owed[2], last, 0))
        )
        _, slot, _ = side_of(codes_ref, other, side)
        counts = is_beside(codes_ref, other, side, tile) & (others[side + 4] == 1)
        back[pl.ds(pl.multiple_of(slot * HALF, HALF), HALF), :] += jnp.where(counts, total, 0.0)
        if side in (0, 2):
            for corner, line in (
                (LOW_LEFT[side], owed[0][last : last + 1]),
                (LOW_RIGHT[side], owed[2][0:1]),
            ):
                _, corner_slot, _ = side_of(codes_ref, other, corner)
                counts = is_beside(codes_ref, other, corner, tile) & (others[side + 4] == 1)

                @pl.when(counts)
                def _():
                    back[pl.ds(pl.multiple_of(corner_slot * HALF, HALF), HALF), :] += jnp.where(
                        place == CORNER_ENDS[corner], line, 0.0
                    )


def own_taps(grad_ref, start, grads, own):
    for a in range(3):
        for b in range(3):
            row = (start + 3 * a + b) * own
            grad_ref[row : row + own, :] = grads[
                a * own : (a + 1) * own, b * 128 : (b + 1) * 128
            ].astype(BF16)


def shifted_stack(values):
    wide = jnp.concatenate([values, jnp.zeros((values.shape[0], PADDED - CELLS), F32)], axis=1)
    return jnp.concatenate(
        [(pltpu.roll(wide, a * HALF, 1) if a else wide).astype(BF16) for a in range(3)], axis=0
    )


def level_kernel(
    nc,
    spots,
    codes_ref,
    where_ref,
    act2_ref,
    slope2_ref,
    act_ref,
    wdt_ref,
    own_ref,
    slope1_ref,
    og_ref,
    x3_ref,
    *refs,
):
    packs, mores, refs = refs[:nc], refs[nc : 2 * nc], refs[2 * nc :]
    *rims, out_ref, grad_ref, w2s, w2t, ups, pooled_all, prims, rims_all, left, right, g3pad, sums, a3, coarse, field, back, m_ref = refs
    tile, me, tile_base, base = where_ref[0], where_ref[1], where_ref[2], where_ref[3]
    own = packs[0].shape[1]
    place_conv(packs, base, 8, w2s)
    for slot in range(nc):
        row = rows_of(slot, base, own)
        ups[pl.ds(row, own), :] = packs[slot][17]
        for jb in range(8):
            pooled_all[pl.ds(row, own), jb * 128 : (jb + 1) * 128] = packs[slot][jb]
        for other in range(mores[slot].shape[0] - 5):
            prims[pl.ds(row, own), other * 128 : (other + 1) * 128] = mores[slot][5 + other]

    def put(slot, ref, index):
        rims_all[slot] = ref[index]

    if len(rims) == 9:
        core = me & 1
        rims_all[1, pl.ds(pl.multiple_of(core * 128, 128), 128), :] = rims[4][0]
        rims_all[1, pl.ds(pl.multiple_of(128 - core * 128, 128), 128), :] = rims[8][0]
        rims = rims[:4] + rims[5:8]
    hold(rims, spots, me & 1, put)
    got = []
    for side in range(8):
        partner, turn, there = side_of(codes_ref, tile, side)
        piece = rims_all[
            partner ^ tile_base, pl.ds(pl.multiple_of(turn * HALF, HALF), HALF), :
        ].astype(F32)
        got.append(jnp.where(there, piece, 0.0))
    spread_columns(
        a3,
        left,
        right,
        act2_ref[...].astype(F32),
        got[0],
        flip32(got[2].astype(BF16)),
        flip32(got[3].astype(BF16)),
        got[1],
        (got[4][0:1], got[5][HALF - 1 : HALF], got[6][0:1], got[7][HALF - 1 : HALF]),
    )
    for a in range(3):
        w2t[a * 384 : (a + 1) * 384, :] = jnp.transpose(w2s[a * 128 : (a + 1) * 128, :])
    pooled = jnp.transpose(pooled_all[...])
    g3pad[0 : 2 * HALF, :] = jnp.zeros((2 * HALF, 128), BF16)
    g3pad[CELLS + 2 * HALF : CELLS + 4 * HALF, :] = jnp.zeros((2 * HALF, 128), BF16)
    for index in range(4):
        start = index * 256
        z3 = mm(
            jnp.concatenate(
                [a3[start + a * HALF : start + a * HALF + 256, :] for a in range(3)], axis=1
            ),
            w2t[...],
        )
        value, slope = gelu_and_slope(z3)
        coarse[start : start + 256, :] = value.astype(BF16)
        back_up = mm(pooled[start : start + 256, :], ups[...])
        g3pad[2 * HALF + start : 2 * HALF + start + 256, :] = (slope * back_up).astype(BF16)
    step = 34 * HALF // 4
    for index in range(4):
        start = index * step
        lhs = jnp.concatenate(
            [g3pad[start + (2 - a) * HALF : start + (2 - a) * HALF + step, :] for a in range(3)], axis=1
        )
        sums[start : start + step, :] = mm(lhs, w2s[...])
    rows = 34 * HALF
    column = iota((rows, 128), 0) % HALF
    middle = (
        sums[:, 128:256]
        + jnp.where(column == HALF - 1, 0.0, pltpu.roll(sums[:, 0:128], rows - 1, 0))
        + jnp.where(column == 0, 0.0, pltpu.roll(sums[:, 256:384], 1, 0))
    )
    field[...] = middle[HALF : HALF + CELLS, :]

    back[...] = jnp.zeros_like(back)
    tiles = codes_ref.shape[0]

    def following(before):
        found = []
        for side in range(4):
            spot = jnp.int32(tiles)
            for other in reversed(range(tiles)):
                take = is_owing(codes_ref, other, side, tile) & (other > before[side])
                spot = jnp.where(take, other, spot)
            found.append(spot)
        return tuple(found)

    def left_over(found):
        return (
            (found[0] < tiles) | (found[1] < tiles) | (found[2] < tiles) | (found[3] < tiles)
        )

    def visit(found):
        others = [jnp.minimum(spot, tiles - 1) for spot in found]
        others = others + [jnp.where(spot < tiles, 1, 0) for spot in found]
        back_from(others, codes_ref, tile, tile_base, rims_all, prims, w2s, w2t, ups, back)
        return following(found)

    lax.while_loop(left_over, visit, following((jnp.int32(-1),) * 4))
    anti = jnp.where(iota((HALF, HALF), 0) + iota((HALF, HALF), 1) == HALF - 1, 1.0, 0.0)

    def flip(values):
        return lax.dot_general(
            anti,
            values,
            (((1,), (0,)), ((), ())),
            preferred_element_type=F32,
            precision=lax.Precision.HIGHEST,
        )

    field[CELLS - HALF : CELLS, :] += back[0:32, :]
    field[0:HALF, :] += flip(back[64:96, :])
    first = pl.ds(0, HALF, stride=HALF)
    last = pl.ds(HALF - 1, HALF, stride=HALF)
    field[first, :] = field[first, :] + back[32:64, :]
    field[last, :] = field[last, :] + flip(back[96:128, :])

    g2 = (slope2_ref[...] * field[...]).astype(BF16)
    pick = own_rows(me, own, 128)
    g2_turned = mm_nt(one_hot(iota((128, 128), 0) == iota((128, 128), 1)), g2).astype(BF16)
    g2_own = mm_nt(pick, g2).astype(BF16)
    grads = jnp.zeros((3 * own, 384), F32)
    for ph in range(4):
        grad_ref[(9 + ph) * own : (10 + ph) * own, :] = mm(g2_own, act_ref[ph]).astype(BF16)
        turned = wdt_ref[pl.ds(pl.multiple_of(ph * 128 + me * own, own), own), :]
        cells = slice(ph * CELLS, (ph + 1) * CELLS)
        g1 = slope1_ref[:, cells] * (og_ref[:, cells].astype(F32) + mm(turned, g2_turned))
        grads = grads + mm(shifted_stack(g1), x3_ref[ph])
    own_taps(grad_ref, 0, grads, own)
    g3 = mm_nt(pick, g3pad[2 * HALF : 2 * HALF + CELLS, :])
    own_taps(grad_ref, 13, mm(shifted_stack(g3), a3[...]), own)
    own_spot = pl.ds(pl.multiple_of(me * own, own), own)
    grad_ref[22 * own : 23 * own, :] = mm(pooled_all[own_spot, :], coarse[...]).astype(BF16)
    if grad_ref.shape[0] > 23 * own:
        grad_ref[23 * own :, :] = jnp.zeros((grad_ref.shape[0] - 23 * own, 128), BF16)

    fill_table(m_ref)
    lifted = mm_nt(ups[own_spot, :], coarse[...])
    total = [
        own_ref[:, ph * CELLS : (ph + 1) * CELLS].astype(F32) + lifted for ph in range(4)
    ]
    stack = jnp.concatenate(
        [
            jnp.concatenate([total[ph][:, jb * 128 : (jb + 1) * 128] for ph in range(4)], axis=1)
            for jb in range(8)
        ],
        axis=0,
    ).astype(BF16)
    natural = mm_nt(stack, m_ref[...]).astype(BF16)
    for jb in range(8):
        out_ref[:, jb * BLOCK : (jb + 1) * BLOCK] = natural[jb * own : (jb + 1) * own]


def sum_kernel(scale, in_ref, out_ref):
    total = in_ref[0].astype(F32)
    for slot in range(1, in_ref.shape[0]):
        total = total + in_ref[slot].astype(F32)
    out_ref[...] = (total * scale).astype(BF16)


def unpack_kernel(flat, one_ref, down_ref, two_ref, up_ref):
    own = up_ref.shape[0]
    for tap in range(9):
        one_ref[tap] = flat[tap * own : (tap + 1) * own, :].astype(F32)
        two_ref[tap] = flat[(13 + tap) * own : (14 + tap) * own, :].astype(F32)
    for ph in range(4):
        down_ref[ph] = flat[(9 + ph) * own : (10 + ph) * own, :].astype(F32)
    up_ref[...] = flat[22 * own : 23 * own, :].astype(F32)


def call(kernel, outs, *args, scratch=(), far=(), room=24, alias={}):
    specs = [
        pl.BlockSpec(
            memory_space=pltpu.SMEM if a.dtype == jnp.int32 else pltpu.HBM if i in far else pltpu.VMEM
        )
        for i, a in enumerate(args)
    ]
    many = isinstance(outs, list)
    vmem = pl.BlockSpec(memory_space=pltpu.VMEM)
    return pl.pallas_call(
        kernel,
        out_shape=outs,
        in_specs=specs,
        out_specs=[vmem] * len(outs) if many else vmem,
        scratch_shapes=list(scratch),
        input_output_aliases=alias,
        compiler_params=pltpu.CompilerParams(vmem_limit_bytes=room * 1024 * 1024),
    )(*args)


def shape(dims, kind=BF16):
    return jax.ShapeDtypeStruct(dims, kind)


def paired(values, axis, bit):
    count = lax.axis_size(axis)
    return lax.ppermute(values, axis, [(i, i ^ bit) for i in range(count)])


FIRST, SECOND = (7, 4, 2), (6, 5, 3)


def is_split():
    return lax.axis_size("tile") == 8 and lax.axis_size("chan") % 2 == 0


def spots_of():
    tiles = lax.axis_size("tile")
    if not is_split():
        return [[(slot, slot) for slot in range(tiles)]]
    pairs = list(zip(FIRST, SECOND))
    return [[(0, 0)]] + [[pair] for pair in pairs] + [[pair[::-1]] for pair in pairs]


def copies(block, half=None, beside=()):
    tiles, nc = lax.axis_size("tile"), lax.axis_size("chan")
    if not is_split():
        return [swap(jnp.broadcast_to(block, (tiles,) + block.shape[1:]))], beside
    got = []
    for slots in zip(FIRST, SECOND):
        perm = [
            (tile * nc + chan, (tile ^ slots[chan & 1]) * nc + chan)
            for tile in range(tiles)
            for chan in range(nc)
        ]
        got.append(lax.ppermute(block, ("tile", "chan"), perm))
    got.append(paired(half, "tile", 1))
    got, beside = lax.optimization_barrier((got, beside))
    return [block] + got + [paired(part, "chan", 1) for part in got], beside


def swap(values):
    return lax.all_to_all(values, "tile", split_axis=0, concat_axis=0)


def gathered(values, axis):
    slots = {0: values}
    bit = lax.axis_size(axis) // 2
    while bit:
        slots.update({slot ^ bit: paired(held, axis, bit) for slot, held in list(slots.items())})
        bit //= 2
    return [slots[slot] for slot in range(len(slots))]


def per_device(features, conv1_weight, down_weight, conv2_weight, up_weight, out_grad, adjacency):
    own = features.shape[0]
    tiles, nc = lax.axis_size("tile"), lax.axis_size("chan")
    scale = float((tiles * SIDE * SIDE) ** (-0.5))
    tile, chan = lax.axis_index("tile"), lax.axis_index("chan")
    where = jnp.stack([tile, chan, tile if is_split() else tile * 0, chan]).astype(jnp.int32)
    half = nc // 2

    pack, rims, sorted_g, pack2 = call(
        sort_kernel,
        [
            shape((45, own, 128)),
            shape((1, 5, own, 128)),
            shape((own, 4 * CELLS)),
            shape((18, own, 128)),
        ],
        features,
        out_grad,
        conv1_weight,
        down_weight,
        conv2_weight,
        up_weight,
        far=range(6),
        room=60,
        scratch=[
            pltpu.VMEM((own, 4 * CELLS), BF16),
            pltpu.VMEM((own, 4 * CELLS), BF16),
            pltpu.VMEM((BLOCK, 2 * BLOCK), BF16),
            pltpu.SemaphoreType.DMA((6,)),
        ],
    )
    pack_far = paired(pack, "chan", half)
    if is_split():
        far, near = paired(rims, "tile", 4), paired(rims, "tile", 2)
        cross = paired(far, "tile", 2)
        pack_near, pair = call(
            stage_kernel, [shape(pack.shape), shape((2,) + rims.shape[1:])], pack, rims, far
        )
        beside = paired(pair, "tile", 1)
        cross, near, pack_near, pack2, adjacency = lax.optimization_barrier(
            (cross, near, pack_near, pack2, adjacency)
        )
        last = [paired(near, "tile", 1), paired(cross, "tile", 1)]
        all_rims = [pair, near, cross, beside] + last
        rim_spots = [[(slot, slot) for slot in group] for group in ((0, 4), (2,), (6,), (1, 5), (3,), (7,))]
    else:
        all_rims, rim_spots = copies(rims)[0], spots_of()
        pack_near = pack
    turns = (adjacency[:, :, 1] + jnp.array(side_turns, jnp.int32)) & 3
    codes = jnp.where(adjacency[:, :, 0] < 0, -1, adjacency[:, :, 0] * 4 + turns)
    ring = call(
        partial(pick_kernel, rim_spots),
        shape((5 + tiles, own, 128)),
        codes,
        where,
        *all_rims,
        scratch=[pltpu.VMEM((tiles + 1, 5, own, 128), BF16)],
    )
    pack_far, ring = lax.optimization_barrier((pack_far, ring))
    ring_far = paired(ring, "chan", half)

    def whole(near, far, held=None):
        return [near if held is None else held, paired(near, "chan", 1), far, paired(far, "chan", 1)]

    packs = whole(pack, pack_far, pack_near)
    x3, z1c, w1t, wdt = call(
        partial(fine_center_kernel, nc),
        [
            shape((4, PADDED, 384)),
            shape((4, CELLS, 128), F32),
            shape((1152, 128)),
            shape((512, 128)),
        ],
        where,
        *packs,
        scratch=[
            pltpu.VMEM((384, 384), BF16),
            pltpu.VMEM((128, 512), BF16),
            pltpu.VMEM((128, 4 * CELLS), BF16),
        ],
    )
    x3, ring_far, pack2 = lax.optimization_barrier((x3, ring_far, pack2))
    pack2_far, pack2_side = paired(pack2, "chan", half), paired(pack2, "chan", 1)
    rings = whole(ring, ring_far)
    act, slope2, act2, rims2, half2, ring_sorted = call(
        partial(fine_ring_kernel, nc),
        [
            shape((4, CELLS, 128)),
            shape((CELLS, 128), F32),
            shape((CELLS, 128)),
            shape((1, 256, 128)),
            shape((1, 128, 128)),
            shape((5, 128, 128), F32),
        ],
        where,
        z1c,
        w1t,
        wdt,
        *rings,
        scratch=[
            pltpu.VMEM((5, 128, 128), BF16),
            pltpu.VMEM((4, CELLS, 128), F32),
            pltpu.VMEM((CELLS, 128), F32),
        ],
    )
    rims2, half2, pack2_side = lax.optimization_barrier((rims2, half2, pack2_side))
    act1, slope1, x3 = call(
        own_fine_kernel,
        [shape((own, 4 * CELLS)), shape((own, 4 * CELLS), F32), shape((4, PADDED, 384))],
        conv1_weight,
        ring_sorted,
        x3,
        alias={2: 2},
    )
    all_rims2, (act1, slope1, x3, pack2_far) = copies(rims2, half2, (act1, slope1, x3, pack2_far))
    packs2 = [pack2, pack2_side, pack2_far, paired(pack2_far, "chan", 1)]
    rows = -(-23 * own // (16 * tiles)) * 16
    output, late = call(
        partial(level_kernel, nc, spots_of()),
        [shape((own, 4 * CELLS)), shape((rows * tiles, 128))],
        codes,
        where,
        act2,
        slope2,
        act,
        wdt,
        act1,
        slope1,
        sorted_g,
        x3,
        *packs2,
        *rings,
        *all_rims2,
        scratch=[
            pltpu.VMEM((384, 384), BF16),
            pltpu.VMEM((1152, 128), BF16),
            pltpu.VMEM((128, 128), BF16),
            pltpu.VMEM((128, CELLS), BF16),
            pltpu.VMEM((128, tiles * 128), BF16),
            pltpu.VMEM((tiles, 256, 128), BF16),
            pltpu.VMEM((34 * HALF, 128), F32),
            pltpu.VMEM((34 * HALF, 128), F32),
            pltpu.VMEM((CELLS + 4 * HALF, 128), BF16),
            pltpu.VMEM((34 * HALF, 384), F32),
            pltpu.VMEM((PADDED, 384), BF16),
            pltpu.VMEM((CELLS, 128), BF16),
            pltpu.VMEM((CELLS, 128), F32),
            pltpu.VMEM((128, 128), F32),
            pltpu.VMEM((BLOCK, BLOCK), BF16),
        ],
    )
    pieces = swap(late.reshape(tiles, rows, 128))
    total = call(partial(sum_kernel, scale), shape((rows, 128)), pieces)
    total = swap(jnp.broadcast_to(total[None], (tiles, rows, 128)))
    grads = call(
        unpack_kernel,
        [
            shape((9, own, 128), F32),
            shape((4, own, 128), F32),
            shape((9, own, 128), F32),
            shape((own, 128), F32),
        ],
        total.reshape(tiles * rows, 128),
    )
    return (output, *grads)


def solution(mesh):
    placed = (
        P("chan", "tile"),
        P(None, "chan", None),
        P(None, "chan", None),
        P(None, "chan", None),
        P("chan", None),
        P("chan", "tile"),
        P(),
    )
    return jax.shard_map(
        per_device,
        mesh=mesh,
        in_specs=placed,
        out_specs=(
            P("chan", "tile"),
            P(None, "chan", None),
            P(None, "chan", None),
            P(None, "chan", None),
            P("chan", None),
        ),
        check_vma=False,
    )
```
